128 devices in a mesh: win: 4 (over x), wide: 32 (over y, z, core).
Axes of the slice: x: 4, y: 4, z: 4, core: 2. Of those that a mesh axis runs over, the one named last changes fastest.
Arguments:
- block_input: bfloat16 [4, 128, 32, 768], P('win', None, 'wide'), may hold values from -6 to 6
- file_lengths: int32 [4, 8], P('win'), may hold values from 0 to 4096, as said below
- file_splits: int32 [4, 8, 2], P('win'), may hold values from 0 to 1024
- ln1_gain: bfloat16 [768], replicated, may hold values from 0.099609375 to 1.8984375
- ln1_bias: bfloat16 [768], replicated, may hold values from -1.25 to 1.25
- w_query: bfloat16 [768, 768], replicated, may hold values from -0.5 to 0.5
- b_query: bfloat16 [768], replicated, may hold values from -1.5 to 1.5
- w_kv: bfloat16 [768, 128], replicated, may hold values from -0.21875 to 0.21875
- b_value: bfloat16 [64], replicated, may hold values from -0.625 to 0.625
- w_out: bfloat16 [768, 768], replicated, may hold values from -0.4375 to 0.4375
- b_out: bfloat16 [768], replicated, may hold values from -0.625 to 0.625
- ln2_gain: bfloat16 [768], replicated, may hold values from 0.099609375 to 1.8984375
- ln2_bias: bfloat16 [768], replicated, may hold values from -1.25 to 1.25
- w_up: bfloat16 [768, 3072], replicated, may hold values from -0.21875 to 0.21875
- b_up: bfloat16 [3072], replicated, may hold values from -1.25 to 1.25
- w_down: bfloat16 [3072, 768], replicated, may hold values from -0.109375 to 0.109375
- b_down: bfloat16 [768], replicated, may hold values from -0.625 to 0.625
- out_cotangent: bfloat16 [4, 128, 32, 768], P('win', None, 'wide'), may hold values from -6 to 6
Outputs:
- block_output: bfloat16 [4, 128, 32, 768], P('win', None, 'wide')
- grad_in: float32 [4, 128, 32, 768], P('win', None, 'wide')
- grad_ln1_gain: float32 [768], replicated
- grad_ln1_bias: float32 [768], replicated
- grad_w_query: float32 [768, 768], replicated
- grad_b_query: float32 [768], replicated
- grad_w_kv: float32 [768, 128], replicated
- grad_b_value: float32 [64], replicated
- grad_w_out: float32 [768, 768], replicated
- grad_b_out: float32 [768], replicated
- grad_ln2_gain: float32 [768], replicated
- grad_ln2_bias: float32 [768], replicated
- grad_w_up: float32 [768, 3072], replicated
- grad_b_up: float32 [3072], replicated
- grad_w_down: float32 [3072, 768], replicated
- grad_b_down: float32 [768], replicated
The draws below stay inside these ranges and needn't reach their ends.
Inputs may be any that keep to these rules, and one draw needn't show every extreme that they name: `file_lengths`: in each window the lengths add up to 4096; the nonzero ones, two to 8 of them, come first.
All inputs are finite; a program needn't handle non-finite values.
Results may differ from the reference program's by a relative error of at most 0.018.
Values may be sent and summed in bfloat16 or wider, within the bound.
No kernel may reach another device: no remote copies, remote signals or barrier semaphores. Data moves between devices by JAX's collectives and lax.ppermute only.
A program may use at most 192 MiB of HBM per device.

```python
import jax
import jax.numpy as jnp
from jax import lax

D = 768
H = 12
HD = 64
FF = 3072
TOK_DEV = 128
FILES = 8
WINDOWS = 4
WINDOW = 4096
N_WIDE = 32


def draw_file_lengths(key, part):
    key = jax.random.fold_in(key, 11)
    key_count, key_before, key_short = jax.random.split(key, 3)
    counts = jax.random.randint(key_count, (WINDOWS,), 2, FILES + 1, dtype=jnp.int32)
    before = jax.random.randint(key_before, (WINDOWS,), 0, counts, dtype=jnp.int32)
    longest = (TOK_DEV - 1) // FILES
    short_len = jax.random.randint(key_short, (WINDOWS, FILES), 1, longest + 1, dtype=jnp.int32)
    slot_index = jnp.arange(FILES, dtype=jnp.int32)[None, :]
    live = slot_index < counts[:, None]
    others = (slot_index != before[:, None]) & live
    main_len = WINDOW - jnp.sum(jnp.where(others, short_len, 0), axis=1, dtype=jnp.int32)
    lengths = jnp.where(slot_index == before[:, None], main_len[:, None], jnp.where(live, short_len, 0))
    return lengths.astype(jnp.int32)


def touch_ends(values, stream_key, least, high):
    shape = values.shape
    spot = [jax.random.randint(jax.random.fold_in(stream_key, axis), (), 0, shape[axis]) for axis in range(len(shape))]
    values = values.at[tuple(spot)].set(least)
    longest = shape.index(max(shape))
    spot[longest] = (spot[longest] + 1) % shape[longest]
    return values.at[tuple(spot)].set(high)


def steps_of(rng, shape, shards, least, largest):
    gain = 1.0
    for position, parts in shards:
        heights = jax.random.uniform(jax.random.fold_in(jax.random.fold_in(rng, 6), position), (parts,), jnp.float32, least / len(shards), largest / len(shards))
        gain = gain * jnp.repeat(jnp.exp(heights), shape[position] // parts).reshape((-1,) + (1,) * (len(shape) - 1 - position))
    return gain


def gaussian(own_key, extent, scale, reach, cuts=(), kind=jnp.bfloat16):
    array = jax.random.normal(own_key, extent, jnp.float32) * scale
    if len(cuts) > 0:
        array = steps_of(own_key, extent, cuts, -0.22, 0.18) * array
    return jnp.clip(array, min=-reach, max=reach).astype(kind)


def setup_inputs(seed: int = 0) -> dict:
    key_of = jax.random.split(jax.random.key(seed), 19)
    block_input = gaussian(key_of[0], (WINDOWS, TOK_DEV, N_WIDE, D), 1.0, 6.0, ((0, 4), (2, 32)))
    file_lengths = draw_file_lengths(jax.random.fold_in(key_of[18], 71), 0)
    file_splits = touch_ends(jax.random.randint(key_of[2], (WINDOWS, FILES, 2), 0, 1025), jax.random.fold_in(key_of[2], 1), 0, 1024).astype(jnp.int32)
    ln1_gain = jnp.clip(1.0 + 0.18 * jax.random.normal(key_of[3], (D,), jnp.float32), 0.099609375, 1.8984375).astype(jnp.bfloat16)
    ln1_bias = gaussian(key_of[4], (D,), 0.2, 1.25)
    w_query = gaussian(key_of[5], (D, D), (max(1, D // 6)) ** -0.5, 0.5)
    b_query = gaussian(key_of[6], (D,), 0.25, 1.5)
    w_kv = gaussian(key_of[7], (D, 2 * HD), D ** -0.5, 0.21875)
    b_value = gaussian(key_of[8], (HD,), 0.1, 0.625)
    w_out = gaussian(key_of[9], (D, D), (max(1, D // 4)) ** -0.5, 0.4375)
    b_out = gaussian(key_of[10], (D,), 0.1, 0.625)
    ln2_gain = jnp.clip(1.0 + 0.18 * jax.random.normal(key_of[11], (D,), jnp.float32), 0.099609375, 1.8984375).astype(jnp.bfloat16)
    ln2_bias = gaussian(key_of[12], (D,), 0.2, 1.25)
    w_up = gaussian(key_of[13], (D, FF), D ** -0.5, 0.21875)
    b_up = gaussian(key_of[14], (FF,), 0.2, 1.25)
    w_down = gaussian(key_of[15], (FF, D), FF ** -0.5, 0.109375)
    b_down = gaussian(key_of[16], (D,), 0.1, 0.625)
    out_cotangent = gaussian(key_of[17], (WINDOWS, TOK_DEV, N_WIDE, D), 1.0, 6.0, ((0, 4), (2, 32)))
    return {"block_input": block_input, "file_lengths": file_lengths, "file_splits": file_splits, "ln1_gain": ln1_gain, "ln1_bias": ln1_bias, "w_query": w_query, "b_query": b_query, "w_kv": w_kv, "b_value": b_value, "w_out": w_out, "b_out": b_out, "ln2_gain": ln2_gain, "ln2_bias": ln2_bias, "w_up": w_up, "b_up": b_up, "w_down": w_down, "b_down": b_down, "out_cotangent": out_cotangent}


@jax.custom_vjp
def low(v):
    return lax.optimization_barrier(v.astype(jnp.bfloat16)).astype(jnp.float32)

@jax.custom_vjp
def low_back(v):
    return v

def low_keep(v):
    return (low(v), None)

def low_pass(kept, grad):
    return (grad,)

def back_keep(v):
    return (v, None)

def back_low(kept, grad):
    return (low(grad),)
low.defvjp(low_keep, low_pass)
low_back.defvjp(back_keep, back_low)
epsilon = 1e-05
masked_score = -1e+30

def norm_rows(values, gain_vec, shift_vec):
    row_mean = lax.optimization_barrier(jnp.mean(values, axis=-1, keepdims=True))
    centered = values - row_mean
    variance = lax.optimization_barrier(jnp.mean(centered * centered, axis=-1, keepdims=True))
    return centered * lax.rsqrt(variance + epsilon) * gain_vec + shift_vec

def gelu_tanh(values):
    return 0.5 * values * (1.0 + jnp.tanh(0.7978845608028654 * (values + 0.044715 * values * values * values)))

def file_positions(lengths, splits, total):
    files = lengths.shape[0]
    slot_index = jnp.arange(files, dtype=jnp.int32)
    is_live = lengths > 0
    live_len = jnp.where(is_live, lengths, 0).astype(jnp.int32)
    file_ends = jnp.cumsum(live_len, dtype=jnp.int32)
    file_starts = file_ends - live_len
    cut_first = lengths * jnp.minimum(splits[:, 0], splits[:, 1]) // 1024
    cut_second = lengths * jnp.maximum(splits[:, 0], splits[:, 1]) // 1024
    row_index = jnp.arange(total, dtype=jnp.int32)[:, None]
    inside = is_live[None, :] & (row_index >= file_starts[None, :]) & (row_index < file_ends[None, :])
    offset = row_index - file_starts[None, :]
    moved = jnp.where(offset < cut_first[None, :], offset, jnp.where(offset >= cut_second[None, :], cut_first[None, :] + offset - cut_second[None, :], cut_first[None, :] + lengths[None, :] - cut_second[None, :] + offset - cut_first[None, :]))
    hits_count = lax.optimization_barrier(jnp.sum(inside.astype(jnp.int32), axis=1, dtype=jnp.int32))
    sequence_pos = lax.optimization_barrier(jnp.sum(jnp.where(inside, file_starts[None, :] + moved, 0), axis=1, dtype=jnp.int32))
    owner_id = lax.optimization_barrier(jnp.sum(jnp.where(inside, slot_index[None, :], 0), axis=1, dtype=jnp.int32))
    seqpos = jnp.where(hits_count > 0, sequence_pos, row_index[:, 0]).astype(jnp.int32)
    fileid = jnp.where(hits_count > 0, owner_id, files).astype(jnp.int32)
    return (fileid, seqpos)

def window_positions(lengths, splits):
    return file_positions(lengths, splits, WINDOW)

def attend_window(operands):
    queries, keyvals, fileid, seqpos = operands
    query_rows = min(512, WINDOW)
    exact = lax.Precision.HIGHEST
    keys = keyvals[:, :HD]
    values = keyvals[:, HD:]
    score_scale = HD ** (-0.5)

    def one_block(pieces):
        query_block, file_rows, order_rows = pieces
        heads_view = query_block.reshape(query_rows, H, HD)
        scores = jnp.einsum('qhd,kd->qhk', heads_view, keys, precision=exact) * score_scale
        scores = low_back(scores)
        allowed = (file_rows[:, None] == fileid[None, :]) & (seqpos[None, :] <= order_rows[:, None])
        masked = jnp.where(allowed[:, None, :], scores, masked_score)
        row_max = lax.optimization_barrier(jnp.max(masked, axis=-1, keepdims=True))
        lse = row_max + jnp.log(lax.optimization_barrier(jnp.sum(jnp.exp(masked - row_max), axis=-1, keepdims=True)))
        probs = low(jnp.exp(masked - lse))
        mixed = jnp.einsum('qhk,kd->qhd', probs, values, precision=exact)
        return mixed.reshape(query_rows, H * HD)
    pieces = lax.map(jax.checkpoint(one_block), (queries.reshape(-1, query_rows, H * HD), fileid.reshape(-1, query_rows), seqpos.reshape(-1, query_rows)))
    return pieces.reshape(WINDOW, H * HD)

def layer(hidden_in, params, fileid, seqpos):
    gain_one, shift_one, w_query, b_query, w_kv, b_value, w_out, b_out, gain_two, shift_two, w_up, b_up, w_down, b_down = params
    exact = lax.Precision.HIGHEST
    normed_one = low(norm_rows(hidden_in, gain_one, shift_one))
    queries = low_back(low(jnp.einsum('wtd,de->wte', normed_one, w_query, precision=exact) + b_query))
    kv_shift = jnp.concatenate([jnp.zeros_like(b_value), b_value])
    keyvals = low_back(low(jnp.einsum('wtd,de->wte', normed_one, w_kv, precision=exact) + kv_shift))
    attended = low_back(low(lax.map(attend_window, (queries, keyvals, fileid, seqpos))))
    branch = low_back(jnp.einsum('wtd,de->wte', attended, w_out, precision=exact) + b_out)
    resid = hidden_in + branch
    normed_two = low(norm_rows(resid, gain_two, shift_two))
    pre_act = low_back(jnp.einsum('wtd,de->wte', normed_two, w_up, precision=exact) + b_up)
    activ = low(gelu_tanh(pre_act))
    mlp_out = low_back(jnp.einsum('wtf,fd->wtd', activ, w_down, precision=exact) + b_down)
    return resid + mlp_out

def reference(block_input, file_lengths, file_splits, ln1_gain, ln1_bias, w_query, b_query, w_kv, b_value, w_out, b_out, ln2_gain, ln2_bias, w_up, b_up, w_down, b_down, out_cotangent):
    hidden_in = block_input.astype(jnp.float32).reshape(WINDOWS, WINDOW, D)
    params = tuple((item.astype(jnp.float32) for item in (ln1_gain, ln1_bias, w_query, b_query, w_kv, b_value, w_out, b_out, ln2_gain, ln2_bias, w_up, b_up, w_down, b_down)))
    fileid, seqpos = jax.vmap(window_positions)(file_lengths, file_splits)

    def forward(inputs, weights):
        return layer(inputs, weights, fileid, seqpos)
    result, backward = jax.vjp(forward, hidden_in, params)
    grad_x, grads = backward(out_cotangent.astype(jnp.float32).reshape(WINDOWS, WINDOW, D))
    shape = block_input.shape
    return (result.astype(jnp.bfloat16).reshape(shape), grad_x.reshape(shape), grads[0], grads[1], grads[2], grads[3], grads[4], grads[5], grads[6], grads[7], grads[8], grads[9], grads[10], grads[11], grads[12], grads[13])
```

```python
import functools

import jax
import jax.numpy as jnp
from jax import lax
from jax.experimental import pallas as pl
from jax.experimental.pallas import tpu as pltpu
from jax.sharding import Mesh, PartitionSpec as P

EPS = 1e-05
MASKED = -1e30
ROWS = 128
WIDE = 32
D = 768
H = 12
HD = 64
FF = 3072
WINDOW = ROWS * WIDE
RB = 4
RBR = ROWS // RB
QB = RBR * H
KB = 8
KBR = ROWS // KB
KEYS = WINDOW // KB
FC = 512
VMEM = pl.BlockSpec(memory_space=pltpu.VMEM)
SMEM = pl.BlockSpec(memory_space=pltpu.SMEM)
f32 = jnp.float32
bf16 = jnp.bfloat16


def params(limit=56):
    return pltpu.CompilerParams(vmem_limit_bytes=limit * 1024 * 1024)


def cost(flops, nbytes):
    return pl.CostEstimate(flops=int(flops), bytes_accessed=int(nbytes), transcendentals=0)


def dot(a, b):
    return jnp.dot(a, b, preferred_element_type=f32)


def dot_nt(a, b):
    return lax.dot_general(a, b, (((1,), (1,)), ((), ())), preferred_element_type=f32)


def dot_tn(a, b):
    return lax.dot_general(a, b, (((0,), (0,)), ((), ())), preferred_element_type=f32)


def norm_parts(x):
    mean = jnp.mean(x, axis=-1, keepdims=True)
    centered = x - mean
    var = jnp.mean(centered * centered, axis=-1, keepdims=True)
    rstd = lax.rsqrt(var + EPS)
    return centered * rstd, rstd


def norm_back(e, n, rstd, gain):
    m = e * gain
    return rstd * (
        m - jnp.mean(m, axis=-1, keepdims=True) - n * jnp.mean(m * n, axis=-1, keepdims=True)
    )


def lanes_low(shape):
    return lax.broadcasted_iota(jnp.int32, shape, len(shape) - 1) < HD


def enter_kernel(x_ref, gain_ref, bias_ref, wkv_ref, bv_ref, n1_ref, kv_ref):
    n, _ = norm_parts(x_ref[...].astype(f32))
    n1 = (n * gain_ref[...].astype(f32) + bias_ref[...].astype(f32)).astype(bf16)
    n1_ref[...] = n1
    kv_ref[...] = (dot(n1, wkv_ref[...]) + bv_ref[...].astype(f32)).astype(bf16)


def query_kernel(n1_ref, wq_ref, bq_ref, q_ref):
    q_ref[...] = (dot(n1_ref[...], wq_ref[...]) + bq_ref[...].astype(f32)).astype(bf16)


def forward_kernel(cls_ref, q_ref, kv_ref, kp_ref, sp_ref, st_ref, att_ref, x_ref, o_ref, lse_ref, m_ref, l_ref, acc_ref):
    low = lanes_low((ROWS, 2 * HD))
    for h in range(H):
        pair = q_ref[:, (h // 2) * 128 : (h // 2) * 128 + 128].astype(f32) * 0.125
        if h % 2:
            pair = pltpu.roll(pair, HD, 1)
        head = jnp.where(low, pair, 0.0).astype(bf16)
        for rb in range(RB):
            x_ref[rb, h * RBR : (h + 1) * RBR, :] = head[rb * RBR : (rb + 1) * RBR, :]

    def row_block(rb, _):
        rows = pl.ds(pl.multiple_of(rb * RBR, RBR), RBR)
        m_ref[...] = jnp.full((QB, 128), MASKED, f32)
        l_ref[...] = jnp.zeros((QB, 128), f32)
        acc_ref[...] = jnp.zeros((QB, 128), f32)

        def step(kb, masked):
            kvb = kv_ref[:, pl.ds(pl.multiple_of(kb * KBR, KBR), KBR), :].reshape(KEYS, 2 * HD)
            s = dot_nt(x_ref[rb], kvb)
            if masked:
                kp = kp_ref[kb]
                allowed = (kp <= sp_ref[rows, :1]) & (kp >= st_ref[rows, :1])
                bias = jnp.where(allowed, 0.0, MASKED)
                s = (s.reshape(H, RBR, KEYS) + bias[None]).reshape(QB, KEYS)
            m_old = m_ref[...]
            m_new = jnp.maximum(m_old, jnp.max(s, axis=1, keepdims=True))
            alpha = jnp.exp(m_old - m_new)
            p = jnp.exp(s - m_new[:, :1])
            l_ref[...] = l_ref[...] * alpha + jnp.sum(p, axis=1, keepdims=True)
            acc_ref[...] = acc_ref[...] * alpha + dot(p.astype(bf16), kvb)
            m_ref[...] = m_new

        def key_block(kb, _):
            kind = cls_ref[rb * KB + kb]

            @pl.when(kind == 2)
            def _():
                step(kb, False)

            @pl.when(kind == 1)
            def _():
                step(kb, True)

            return 0

        lax.fori_loop(0, KB, key_block, 0)
        l = l_ref[...]
        out = acc_ref[...] / l
        lse_ref[rb] = m_ref[...] + jnp.log(l)
        o_ref[rb] = out
        keep = lanes_low((RBR, 2 * HD))
        for h in range(0, H, 2):
            even = out[h * RBR : (h + 1) * RBR, :]
            odd = out[(h + 1) * RBR : (h + 2) * RBR, :]
            att_ref[rows, h * HD : (h + 2) * HD] = jnp.where(keep, pltpu.roll(even, HD, 1), odd).astype(bf16)
        return 0

    lax.fori_loop(0, RB, row_block, 0)


def backward_kernel(cls_ref, x_ref, do_ref, o_ref, lse_ref, kv_ref, kpb_ref, spl_ref, stl_ref, dq_ref, dkv_ref, y_ref, lrow_ref, drow_ref, dqt_ref, acc_ref, kt_ref):
    low = lanes_low((ROWS, 2 * HD))
    for h in range(H):
        pair = do_ref[:, (h // 2) * 128 : (h // 2) * 128 + 128].astype(f32)
        if h % 2 == 0:
            pair = pltpu.roll(pair, HD, 1)
        head = jnp.where(low, 0.0, pair).astype(bf16)
        for rb in range(RB):
            y_ref[rb, h * RBR : (h + 1) * RBR, :] = head[rb * RBR : (rb + 1) * RBR, :]
    for rb in range(RB):
        delta = jnp.sum(y_ref[rb].astype(f32) * o_ref[rb], axis=1, keepdims=True)
        drow_ref[rb] = jnp.transpose(jnp.broadcast_to(delta, (QB, 128)))[:8]
        lrow_ref[rb] = jnp.transpose(lse_ref[rb])[:8]
    dqt_ref[...] = jnp.zeros((RB, 128, QB), f32)

    def key_block(kb, _):
        cols = pl.ds(pl.multiple_of(kb * KBR, KBR), KBR)
        kvb = kv_ref[:, cols, :].reshape(KEYS, 2 * HD)
        kt_ref[...] = jnp.transpose(kvb.astype(f32)).astype(bf16)
        acc_ref[...] = jnp.zeros((KEYS, 2 * HD), f32)

        def step(rb, masked):
            kvb = kv_ref[:, cols, :].reshape(KEYS, 2 * HD)
            xb, yb = x_ref[rb], y_ref[rb]
            s = dot_nt(kvb, xb)
            if masked:
                kp = kpb_ref[kb]
                allowed = (kp <= spl_ref[rb]) & (kp >= stl_ref[rb])
                bias = jnp.where(allowed, 0.0, MASKED)
                s = s + jnp.concatenate([bias] * (QB // 128), axis=1)
            p = jnp.exp(s - lrow_ref[rb, :1])
            ds = (p * (dot_nt(kvb, yb) - drow_ref[rb, :1])).astype(bf16)
            acc_ref[...] += dot(ds, xb) + dot(p.astype(bf16), yb)
            dqt_ref[rb] += dot(kt_ref[...], ds)

        def row_block(rb, _):
            kind = cls_ref[rb * KB + kb]

            @pl.when(kind == 2)
            def _():
                step(rb, False)

            @pl.when(kind == 1)
            def _():
                step(rb, True)

            return 0

        lax.fori_loop(0, RB, row_block, 0)
        dkv_ref[:, cols, :] = acc_ref[...].reshape(WIDE, KBR, 2 * HD).astype(bf16)
        return 0

    lax.fori_loop(0, KB, key_block, 0)
    keep = lanes_low((RBR, 2 * HD))
    for rb in range(RB):
        dq = jnp.transpose(dqt_ref[rb]) * 0.125
        for h in range(0, H, 2):
            even = dq[h * RBR : (h + 1) * RBR, :]
            odd = dq[(h + 1) * RBR : (h + 2) * RBR, :]
            dq_ref[rb * RBR : (rb + 1) * RBR, h * HD : (h + 2) * HD] = jnp.where(
                keep, even, pltpu.roll(odd, HD, 1)
            ).astype(bf16)


def middle_kernel(att_ref, x_ref, g_ref, wout_ref, bout_ref, gain_ref, bias_ref, wup_ref, bup_ref, wdown_ref, bdown_ref,
                  y_ref, n2_ref, act_ref, gp_ref, gr_ref, gb_ref, ga_ref, vec_ref, gbup_ref,
                  resid_ref, out_ref, gn2_ref):
    step = pl.program_id(0)

    @pl.when(step == 0)
    def _():
        resid = x_ref[...].astype(f32) + (dot(att_ref[...], wout_ref[...]) + bout_ref[...].astype(f32))
        resid_ref[...] = resid
        n, _ = norm_parts(resid)
        n2_ref[...] = (n * gain_ref[...].astype(f32) + bias_ref[...].astype(f32)).astype(bf16)
        out_ref[...] = jnp.zeros_like(out_ref)
        gn2_ref[...] = jnp.zeros_like(gn2_ref)

    g = g_ref[...]
    pre = dot(n2_ref[...], wup_ref[...]) + bup_ref[...].astype(f32)
    sq = pre * pre
    t = jnp.tanh(0.7978845608028654 * (pre + 0.044715 * sq * pre))
    half = 0.5 + 0.5 * t
    act = (pre * half).astype(bf16)
    act_ref[...] = act
    slope = half + (0.5 * 0.7978845608028654) * pre * (1.0 - t * t) * (1.0 + (3 * 0.044715) * sq)
    gp = (slope * dot_nt(g, wdown_ref[...])).astype(bf16)
    gp_ref[...] = gp
    gbup_ref[...] = jnp.sum(gp.astype(f32), axis=0, keepdims=True)
    out_ref[...] += dot(act, wdown_ref[...])
    gn2_ref[...] += dot_nt(gp, wup_ref[...])

    @pl.when(step == pl.num_programs(0) - 1)
    def _():
        resid = resid_ref[...]
        gf = g.astype(f32)
        y_ref[...] = (resid + (out_ref[...] + bdown_ref[...].astype(f32))).astype(bf16)
        n, rstd = norm_parts(resid)
        e = gn2_ref[...]
        gr = gf + norm_back(e, n, rstd, gain_ref[...].astype(f32))
        gr_ref[...] = gr
        gb = gr.astype(bf16)
        gb_ref[...] = gb
        ga_ref[...] = dot_nt(gb, wout_ref[...]).astype(bf16)
        vec_ref[0:1, :] = jnp.sum(gf, axis=0, keepdims=True)
        vec_ref[1:2, :] = jnp.sum(e * n, axis=0, keepdims=True)
        vec_ref[2:3, :] = jnp.sum(e, axis=0, keepdims=True)
        vec_ref[3:4, :] = jnp.sum(gb.astype(f32), axis=0, keepdims=True)
        vec_ref[4:8, :] = jnp.zeros((4, D), f32)


def leave_kernel(x_ref, gain_ref, wq_ref, wkv_ref, gq_ref, parts_ref, gr_ref, gin_ref, gkv_ref, vec_ref):
    gkv = jnp.sum(parts_ref[...].astype(f32), axis=0).astype(bf16)
    gkv_ref[...] = gkv
    gq = gq_ref[...]
    e = dot_nt(gq, wq_ref[...]) + dot_nt(gkv, wkv_ref[...])
    n, rstd = norm_parts(x_ref[...].astype(f32))
    gin_ref[...] = gr_ref[...] + norm_back(e, n, rstd, gain_ref[...].astype(f32))
    vec_ref[0:1, :] = jnp.sum(e * n, axis=0, keepdims=True)
    vec_ref[1:2, :] = jnp.sum(e, axis=0, keepdims=True)
    vec_ref[2:3, :] = jnp.sum(gq.astype(f32), axis=0, keepdims=True)
    vec_ref[3:4, 0:128] = jnp.sum(gkv.astype(f32), axis=0, keepdims=True)
    vec_ref[3:4, 128:] = jnp.zeros((1, D - 128), f32)
    vec_ref[4:8, :] = jnp.zeros((4, D), f32)


def shapes(*pairs):
    return tuple(jax.ShapeDtypeStruct(s, t) for s, t in pairs)


def positions(lengths, splits, wide_index):
    ends = jnp.cumsum(lengths, dtype=jnp.int32)
    starts = ends - lengths
    first = lengths * jnp.minimum(splits[:, 0], splits[:, 1]) // 1024
    second = lengths * jnp.maximum(splits[:, 0], splits[:, 1]) // 1024

    def place(row):
        shape = (1,) * row.ndim + (-1,)
        s, e, a, b, n = (v.reshape(shape) for v in (starts, ends, first, second, lengths))
        row = row[..., None]
        inside = (row >= s) & (row < e)
        u = row - s
        moved = jnp.where(u < a, u, jnp.where(u >= b, a + u - b, a + n - b + u - a))
        return (
            jnp.sum(jnp.where(inside, s + moved, 0), axis=-1, dtype=jnp.int32),
            jnp.sum(jnp.where(inside, s, 0), axis=-1, dtype=jnp.int32),
        )

    k = jnp.arange(KB, dtype=jnp.int32)[:, None, None]
    j = jnp.arange(WIDE, dtype=jnp.int32)[None, :, None]
    r = jnp.arange(KBR, dtype=jnp.int32)[None, None, :]
    keys, _ = place(((k * KBR + r) * WIDE + j).reshape(KB, KEYS))
    own, own_start = place(jnp.arange(ROWS, dtype=jnp.int32) * WIDE + wide_index)
    low, high = jnp.min(keys, axis=1), jnp.max(keys, axis=1)
    blocks, block_starts = own.reshape(RB, RBR), own_start.reshape(RB, RBR)
    top, start_low = jnp.max(blocks, axis=1), jnp.min(block_starts, axis=1)
    bottom, start_high = jnp.min(blocks, axis=1), jnp.max(block_starts, axis=1)
    some = (low[None] <= top[:, None]) & (high[None] >= start_low[:, None])
    every = (high[None] <= bottom[:, None]) & (low[None] >= start_high[:, None])
    kinds = jnp.where(every, 2, jnp.where(some, 1, 0)).astype(jnp.int32).reshape(-1)
    return keys, own, own_start, kinds


def body(block_input, file_lengths, file_splits, ln1_gain, ln1_bias, w_query, b_query, w_kv, b_value, w_out, b_out,
         ln2_gain, ln2_bias, w_up, b_up, w_down, b_down, out_cotangent):
    row = lambda v: v.reshape(1, -1)
    x = block_input.reshape(ROWS, D)
    g = out_cotangent.reshape(ROWS, D)
    wide_index = lax.axis_index("wide")
    kv_shift = jnp.concatenate([jnp.zeros_like(b_value), b_value])

    n1, kv = pl.pallas_call(
        enter_kernel,
        out_shape=shapes(((ROWS, D), bf16), ((ROWS, 2 * HD), bf16)),
        in_specs=[VMEM] * 5,
        out_specs=(VMEM, VMEM),
        compiler_params=params(),
        cost_estimate=cost(2 * ROWS * D * 128, 6e5),
        name="enter",
    )(x, row(ln1_gain), row(ln1_bias), w_kv, row(kv_shift))
    copies = jnp.broadcast_to(kv, (WIDE, ROWS, 2 * HD))
    kv_all = lax.all_to_all(copies, "wide", 0, 0, tiled=True)

    q = pl.pallas_call(
        query_kernel,
        out_shape=jax.ShapeDtypeStruct((ROWS, D), bf16),
        in_specs=[VMEM] * 3,
        out_specs=VMEM,
        compiler_params=params(),
        cost_estimate=cost(2 * ROWS * D * D, 2e6),
        name="query",
    )(n1, w_query, row(b_query))
    keys, own, own_start, kinds = positions(file_lengths[0], file_splits[0], wide_index)
    own_cols = jnp.broadcast_to(own[:, None], (ROWS, 128))
    start_cols = jnp.broadcast_to(own_start[:, None], (ROWS, 128))
    key_cols = jnp.broadcast_to(keys[:, :, None], (KB, KEYS, 128))
    own_lanes = jnp.tile(own.reshape(RB, 1, RBR), (1, 1, 4))
    start_lanes = jnp.tile(own_start.reshape(RB, 1, RBR), (1, 1, 4))

    att, xq, o, lse = pl.pallas_call(
        forward_kernel,
        out_shape=shapes(((ROWS, D), bf16), ((RB, QB, 128), bf16), ((RB, QB, 128), f32), ((RB, QB, 128), f32)),
        in_specs=[SMEM] + [VMEM] * 5,
        out_specs=(VMEM,) * 4,
        scratch_shapes=[pltpu.VMEM((QB, 128), f32)] * 3,
        compiler_params=params(),
        cost_estimate=cost(4 * ROWS * H * WINDOW * 64, 4e6),
        name="attend",
    )(kinds, q, kv_all, keys.reshape(KB, 1, KEYS), own_cols, start_cols)

    steps = FF // FC
    whole = lambda *s: pl.BlockSpec(s, lambda i: (0,) * len(s))
    y, n2, act, gp, gr, gb, ga, vec_mid, gb_up = pl.pallas_call(
        middle_kernel,
        grid=(steps,),
        out_shape=shapes(
            ((ROWS, D), bf16), ((ROWS, D), bf16), ((ROWS, FF), bf16), ((ROWS, FF), bf16), ((ROWS, D), f32),
            ((ROWS, D), bf16), ((ROWS, D), bf16), ((8, D), f32), ((1, FF), f32),
        ),
        in_specs=[
            whole(ROWS, D), whole(ROWS, D), whole(ROWS, D), whole(D, D), whole(1, D), whole(1, D), whole(1, D),
            pl.BlockSpec((D, FC), lambda i: (0, i)), pl.BlockSpec((1, FC), lambda i: (0, i)),
            pl.BlockSpec((FC, D), lambda i: (i, 0)), whole(1, D),
        ],
        out_specs=(
            whole(ROWS, D), whole(ROWS, D), pl.BlockSpec((ROWS, FC), lambda i: (0, i)),
            pl.BlockSpec((ROWS, FC), lambda i: (0, i)), whole(ROWS, D), whole(ROWS, D), whole(ROWS, D),
            whole(8, D), pl.BlockSpec((1, FC), lambda i: (0, i)),
        ),
        scratch_shapes=[pltpu.VMEM((ROWS, D), f32)] * 3,
        compiler_params=params(),
        cost_estimate=cost(8 * ROWS * D * FF, 2e7),
        name="middle",
    )(att, x, g, w_out, row(b_out), row(ln2_gain), row(ln2_bias), w_up, row(b_up), w_down, row(b_down))

    gq, dkv = pl.pallas_call(
        backward_kernel,
        out_shape=shapes(((ROWS, D), bf16), ((WIDE, ROWS, 2 * HD), bf16)),
        in_specs=[SMEM] + [VMEM] * 8,
        out_specs=(VMEM, VMEM),
        scratch_shapes=[
            pltpu.VMEM((RB, QB, 128), bf16), pltpu.VMEM((RB, 8, QB), f32), pltpu.VMEM((RB, 8, QB), f32),
            pltpu.VMEM((RB, 128, QB), f32), pltpu.VMEM((KEYS, 2 * HD), f32), pltpu.VMEM((2 * HD, KEYS), bf16),
        ],
        compiler_params=params(),
        cost_estimate=cost(10 * ROWS * H * WINDOW * 64, 8e6),
        name="attend_back",
    )(kinds, xq, ga, o, lse, kv_all, key_cols, own_lanes, start_lanes)
    parts = lax.all_to_all(dkv, "wide", 0, 0, tiled=True)

    gin, gkv, vec_end = pl.pallas_call(
        leave_kernel,
        out_shape=shapes(((ROWS, D), f32), ((ROWS, 2 * HD), bf16), ((8, D), f32)),
        in_specs=[VMEM] * 7,
        out_specs=(VMEM,) * 3,
        compiler_params=params(),
        cost_estimate=cost(2 * ROWS * D * 900, 4e6),
        name="leave",
    )(x, row(ln1_gain), w_query, w_kv, gq, parts, gr)

    grads = [dot_tn(act, g), dot_tn(n2, gp), dot_tn(att, gb), dot_tn(n1, gq), dot_tn(n1, gkv)]
    sums = lax.psum(tuple(v.astype(bf16) for v in grads), ("win", "wide"))
    g_down, g_up, g_out, g_query, g_kv = (v.astype(f32) for v in sums)
    vec_mid, gb_up, vec_end = lax.psum((vec_mid, gb_up, vec_end), ("win", "wide"))
    shape = block_input.shape
    return (
        y.reshape(shape), gin.reshape(shape), vec_end[0], vec_end[1], g_query, vec_end[2], g_kv, vec_end[3, HD : 2 * HD],
        g_out, vec_mid[3], vec_mid[1], vec_mid[2], g_up, gb_up[0], g_down, vec_mid[0],
    )


def solution(mesh):
    split = P("win", None, "wide", None)
    return jax.shard_map(
        body,
        mesh=mesh,
        in_specs=(split, P("win", None), P("win", None, None)) + (P(),) * 14 + (split,),
        out_specs=(split, split) + (P(),) * 14,
        check_vma=False,
    )
```

```python
import itertools

import jax
import jax.numpy as jnp
from jax import lax
from jax.experimental import pallas as pl
from jax.experimental.pallas import tpu as pltpu
from jax.sharding import Mesh, PartitionSpec as P

EPS = 1e-05
MASKED = -1e30
ROWS = 128
WIDE = 32
CHIPS = 16
D = 768
H = 12
HD = 64
FF = 3072
WINDOW = ROWS * WIDE
RB = 2
RBR = ROWS // RB
QB = RBR * H
KB = 4
KBR = ROWS // KB
KEYS = WINDOW // KB
FC = 512
VMEM = pl.BlockSpec(memory_space=pltpu.VMEM)
SMEM = pl.BlockSpec(memory_space=pltpu.SMEM)
ANY = pl.BlockSpec(memory_space=pl.ANY)
f32 = jnp.float32
bf16 = jnp.bfloat16


def params(limit=56):
    return pltpu.CompilerParams(vmem_limit_bytes=limit * 1024 * 1024)


def cost(flops, nbytes):
    return pl.CostEstimate(flops=1, bytes_accessed=1, transcendentals=0)


def dot(a, b):
    return jnp.dot(a, b, preferred_element_type=f32)


def dot_nt(a, b):
    return lax.dot_general(a, b, (((1,), (1,)), ((), ())), preferred_element_type=f32)


def dot_tn(a, b):
    return lax.dot_general(a, b, (((0,), (0,)), ((), ())), preferred_element_type=f32)


def norm_parts(x):
    mean = jnp.mean(x, axis=-1, keepdims=True)
    centered = x - mean
    var = jnp.mean(centered * centered, axis=-1, keepdims=True)
    rstd = lax.rsqrt(var + EPS)
    return centered * rstd, rstd


def norm_back(e, n, rstd, gain):
    m = e * gain
    return rstd * (
        m - jnp.mean(m, axis=-1, keepdims=True) - n * jnp.mean(m * n, axis=-1, keepdims=True)
    )


AXES = ("x", "y", "z", "c")
ORDER = ((2, 1, 0), (1, 0, 2))
FROM = (0, 3, 1, 2)


def ring(place, shift):
    pairs = []
    for at in itertools.product(range(4), range(4), range(4), range(2)):
        to = list(at)
        axis = ORDER[at[3]][place]
        to[axis] = (to[axis] + shift) % 4
        index = lambda v: ((v[0] * 4 + v[1]) * 4 + v[2]) * 2 + v[3]
        pairs.append((index(at), index(to)))
    return pairs


def ring_groups(place):
    groups = {}
    for at in itertools.product(range(4), range(4), range(4), range(2)):
        key = list(at)
        key[ORDER[at[3]][place]] = -1
        groups.setdefault(tuple(key), []).append(((at[0] * 4 + at[1]) * 4 + at[2]) * 2 + at[3])
    return list(groups.values())


def send(v, place, shift):
    return lax.ppermute(v, AXES, ring(place, shift))


def swap(v):
    return lax.ppermute(v, "c", [(0, 1), (1, 0)])


def spread(place, plus, minus, far):
    return send(plus, place, 1), send(minus, place, 3), send(far, place, 2)


def gather4(v, place):
    return (v,) + spread(place, v, v, v)


def lanes_low(shape):
    return lax.broadcasted_iota(jnp.int32, shape, len(shape) - 1) < HD


def vec(ref):
    return ref[...].astype(f32).reshape(1, -1)


def enter_kernel(x_ref, gain_ref, bias_ref, wkv_ref, bv_ref, n1_ref, kv_ref):
    n, _ = norm_parts(x_ref[...].astype(f32))
    n1 = (n * vec(gain_ref) + vec(bias_ref)).astype(bf16)
    n1_ref[...] = n1
    shift = jnp.concatenate([jnp.zeros((1, HD), f32), vec(bv_ref)], axis=1)
    kv = (dot(n1, wkv_ref[...]) + shift).astype(bf16)
    for i in range(CHIPS):
        kv_ref[i] = kv


def query_kernel(n1_ref, wq_ref, bq_ref, q_ref):
    q_ref[...] = (dot(n1_ref[...], wq_ref[...]) + vec(bq_ref)).astype(bf16)


def block_bias(kp, sp, st):
    bias = jnp.where((kp <= sp) & (kp >= st), 0.0, MASKED)
    return jnp.concatenate([bias] * (QB // 128), axis=1)


def visit(cls_ref, kb, step):
    def row_block(rb, _):
        kind = cls_ref[rb * KB + kb]

        @pl.when(kind == 2)
        def _():
            step(rb, False)

        @pl.when(kind == 1)
        def _():
            step(rb, True)

        return 0

    lax.fori_loop(0, RB, row_block, 0)


def forward_kernel(at_ref, cls_ref, q_ref, same_ref, other_ref, kpb_ref, spl_ref, stl_ref, n1_ref,
                   att_ref, keep_ref, send_ref, x_ref, o_ref, lse_ref, kv_ref, m_ref, l_ref, acc_ref, kt_ref):
    kv_ref[:CHIPS] = same_ref[...]
    kv_ref[CHIPS:] = other_ref[...]
    low = lanes_low((ROWS, 2 * HD))
    for h in range(H):
        pair = q_ref[:, (h // 2) * 128 : (h // 2) * 128 + 128].astype(f32) * 0.125
        if h % 2:
            pair = pltpu.roll(pair, HD, 1)
        head = jnp.where(low, pair, 0.0).astype(bf16)
        for rb in range(RB):
            x_ref[rb, h * RBR : (h + 1) * RBR, :] = head[rb * RBR : (rb + 1) * RBR, :]
    m_ref[...] = jnp.full((RB, 1, QB), MASKED, f32)
    l_ref[...] = jnp.zeros((RB, 1, QB), f32)
    acc_ref[...] = jnp.zeros((RB, 2 * HD, QB), f32)

    def key_block(kb, _):
        cols = pl.ds(pl.multiple_of(kb * KBR, KBR), KBR)
        kt_ref[...] = jnp.transpose(kv_ref[:, cols, :].reshape(KEYS, 2 * HD).astype(f32)).astype(bf16)

        def step(rb, masked):
            s = dot_nt(kv_ref[:, cols, :].reshape(KEYS, 2 * HD), x_ref[rb])
            if masked:
                s = s + block_bias(kpb_ref[kb], spl_ref[rb], stl_ref[rb])
            m_old = m_ref[rb]
            m_new = jnp.maximum(m_old, jnp.max(s, axis=0, keepdims=True))
            alpha = jnp.exp(m_old - m_new)
            p = jnp.exp(s - m_new)
            l_ref[rb] = l_ref[rb] * alpha + jnp.sum(p, axis=0, keepdims=True)
            acc_ref[rb] = acc_ref[rb] * alpha + dot(kt_ref[...], p.astype(bf16))
            m_ref[rb] = m_new

        visit(cls_ref, kb, step)
        return 0

    lax.fori_loop(0, KB, key_block, 0)
    keep = lanes_low((RBR, 2 * HD))
    first = at_ref[0] == 0
    for rb in range(RB):
        rows = slice(rb * RBR, (rb + 1) * RBR)
        l = l_ref[rb]
        lse_ref[rb] = m_ref[rb] + jnp.log(l)
        out = jnp.transpose(acc_ref[rb] / l)
        o_ref[rb] = out
        for h in range(0, H, 2):
            even = out[h * RBR : (h + 1) * RBR, :]
            odd = out[(h + 1) * RBR : (h + 2) * RBR, :]
            att_ref[rows, h * HD : (h + 2) * HD] = jnp.where(keep, pltpu.roll(even, HD, 1), odd).astype(bf16)
    n1, att = n1_ref[...], att_ref[...]
    keep_ref[...] = jnp.where(first, n1, att)
    send_ref[...] = jnp.where(first, att, n1)


def backward_kernel(at_ref, cls_ref, x_ref, do_ref, o_ref, lse_ref, kv_ref, kpb_ref, spl_ref, stl_ref, gb_ref,
                    dq_ref, keep_ref, send_ref, dkv_ref, y_ref, drow_ref, dqt_ref, acc_ref, kt_ref):
    low = lanes_low((ROWS, 2 * HD))
    for h in range(H):
        pair = do_ref[:, (h // 2) * 128 : (h // 2) * 128 + 128].astype(f32)
        if h % 2 == 0:
            pair = pltpu.roll(pair, HD, 1)
        head = jnp.where(low, 0.0, pair).astype(bf16)
        for rb in range(RB):
            y_ref[rb, h * RBR : (h + 1) * RBR, :] = head[rb * RBR : (rb + 1) * RBR, :]
    for rb in range(RB):
        delta = jnp.sum(y_ref[rb].astype(f32) * o_ref[rb], axis=1, keepdims=True)
        drow_ref[rb] = jnp.transpose(jnp.broadcast_to(delta, (QB, 128)))[:8]
    dqt_ref[...] = jnp.zeros((RB, 128, QB), f32)

    def key_block(kb, _):
        cols = pl.ds(pl.multiple_of(kb * KBR, KBR), KBR)
        kvb = kv_ref[:, cols, :].reshape(KEYS, 2 * HD)
        kt_ref[...] = jnp.transpose(kvb.astype(f32)).astype(bf16)
        acc_ref[...] = jnp.zeros((KEYS, 2 * HD), f32)

        def step(rb, masked):
            kvb = kv_ref[:, cols, :].reshape(KEYS, 2 * HD)
            xb, yb = x_ref[rb], y_ref[rb]
            s = dot_nt(kvb, xb)
            if masked:
                s = s + block_bias(kpb_ref[kb], spl_ref[rb], stl_ref[rb])
            p = jnp.exp(s - lse_ref[rb])
            ds = (p * (dot_nt(kvb, yb) - drow_ref[rb, :1])).astype(bf16)
            acc_ref[...] += dot(ds, xb) + dot(p.astype(bf16), yb)
            dqt_ref[rb] += dot(kt_ref[...], ds)

        visit(cls_ref, kb, step)
        sums = acc_ref[...].reshape(WIDE, KBR, 2 * HD).astype(bf16)
        for i in range(CHIPS):
            dkv_ref[2 * i + at_ref[0], cols, :] = sums[i]
            dkv_ref[2 * i + 1 - at_ref[0], cols, :] = sums[CHIPS + i]
        return 0

    lax.fori_loop(0, KB, key_block, 0)
    keep = lanes_low((RBR, 2 * HD))
    for rb in range(RB):
        dq = jnp.transpose(dqt_ref[rb]) * 0.125
        for h in range(0, H, 2):
            even = dq[h * RBR : (h + 1) * RBR, :]
            odd = dq[(h + 1) * RBR : (h + 2) * RBR, :]
            dq_ref[rb * RBR : (rb + 1) * RBR, h * HD : (h + 2) * HD] = jnp.where(
                keep, even, pltpu.roll(odd, HD, 1)
            ).astype(bf16)
    first = at_ref[0] == 0
    dq, gb = dq_ref[...], gb_ref[...]
    keep_ref[...] = jnp.where(first, dq, gb)
    send_ref[...] = jnp.where(first, gb, dq)


def put_rows(ref, at, row):
    for i in range(row.shape[1] // 128):
        ref[pl.ds(at + i, 1), :] = row[:, i * 128 : (i + 1) * 128]


def middle_kernel(at_ref, att_ref, x_ref, g_ref, wout_ref, bout_ref, gain_ref, bias_ref, wup_ref, bup_ref, wdown_ref, bdown_ref,
                  y_ref, bk_ref, bs_ref, sk_ref, ss_ref, gr_ref, gb_ref, ga_ref, vec_ref,
                  resid_ref, out_ref, gn2_ref, n2_ref):
    step = pl.program_id(0)
    first = at_ref[0] == 0

    @pl.when(step == 0)
    def _():
        resid = x_ref[...].astype(f32) + (dot(att_ref[...], wout_ref[...]) + vec(bout_ref))
        resid_ref[...] = resid
        n, _ = norm_parts(resid)
        n2 = (n * vec(gain_ref) + vec(bias_ref)).astype(bf16)
        n2_ref[...] = n2
        sk_ref[...] = jnp.where(first, g_ref[...], n2)
        ss_ref[...] = jnp.where(first, n2, g_ref[...])
        out_ref[...] = jnp.zeros_like(out_ref)
        gn2_ref[...] = jnp.zeros_like(gn2_ref)

    g = g_ref[...]
    pre = dot(n2_ref[...], wup_ref[...]) + vec(bup_ref)
    sq = pre * pre
    t = jnp.tanh(0.7978845608028654 * (pre + 0.044715 * sq * pre))
    half = 0.5 + 0.5 * t
    act = (pre * half).astype(bf16)
    slope = half + (0.5 * 0.7978845608028654) * pre * (1.0 - t * t) * (1.0 + (3 * 0.044715) * sq)
    gp = (slope * dot_nt(g, wdown_ref[...])).astype(bf16)
    bk_ref[...] = jnp.where(first, act, gp)
    bs_ref[...] = jnp.where(first, gp, act)
    put_rows(vec_ref, 24 + step * (FC // 128), jnp.sum(gp.astype(f32), axis=0, keepdims=True))
    out_ref[...] += dot(act, wdown_ref[...])
    gn2_ref[...] += dot_nt(gp, wup_ref[...])

    @pl.when(step == pl.num_programs(0) - 1)
    def _():
        resid = resid_ref[...]
        gf = g.astype(f32)
        y_ref[...] = (resid + (out_ref[...] + vec(bdown_ref))).astype(bf16)
        n, rstd = norm_parts(resid)
        e = gn2_ref[...]
        gr = gf + norm_back(e, n, rstd, vec(gain_ref))
        gr_ref[...] = gr
        gb = gr.astype(bf16)
        gb_ref[...] = gb
        ga_ref[...] = dot_nt(gb, wout_ref[...]).astype(bf16)
        put_rows(vec_ref, 0, jnp.sum(gf, axis=0, keepdims=True))
        put_rows(vec_ref, 6, jnp.sum(e * n, axis=0, keepdims=True))
        put_rows(vec_ref, 12, jnp.sum(e, axis=0, keepdims=True))
        put_rows(vec_ref, 18, jnp.sum(gb.astype(f32), axis=0, keepdims=True))


def leave_kernel(at_ref, x_ref, gain_ref, wq_ref, wkv_ref, gq_ref, parts_ref, gr_ref, mid_ref, gin_ref, keep_ref, send_ref, vec_ref):
    gkv = jnp.sum(parts_ref[...].astype(f32), axis=0).astype(bf16)
    gq = gq_ref[...]
    e = dot_nt(gq, wq_ref[...]) + dot_nt(gkv, wkv_ref[...])
    n, rstd = norm_parts(x_ref[...].astype(f32))
    gin_ref[...] = gr_ref[...] + norm_back(e, n, rstd, vec(gain_ref))
    gkv = gkv.astype(f32)
    vec_ref[0:48, :] = mid_ref[...]
    vec_ref[48:128, :] = jnp.zeros((80, 128), f32)
    put_rows(vec_ref, 48, jnp.sum(e * n, axis=0, keepdims=True))
    put_rows(vec_ref, 54, jnp.sum(e, axis=0, keepdims=True))
    put_rows(vec_ref, 60, jnp.sum(gq.astype(f32), axis=0, keepdims=True))
    put_rows(vec_ref, 66, jnp.sum(gkv, axis=0, keepdims=True))
    first = at_ref[0] == 0
    vecs = vec_ref[...]
    keep_ref[...] = jnp.where(first, gkv, vecs)
    send_ref[...] = jnp.where(first, vecs, gkv)


def pack_kernel(bk_ref, sk_ref, bp_ref, sp_ref, out_ref):
    for i in range(4):
        cols = slice(i * D, (i + 1) * D)
        out_ref[i, 0:ROWS, 0:D] = bk_ref[:, cols]
        out_ref[i, ROWS:, 0:D] = bp_ref[:, cols]
        out_ref[i, 0:ROWS, D:] = sk_ref[...]
        out_ref[i, ROWS:, D:] = sp_ref[...]

def quarters(at, which, total_ref, outs):
    rows = total_ref.shape[0]//4
    for rel, out in zip((0,1,3,2), outs):
        out[...] = total_ref[pl.ds(pl.multiple_of(((at[which]+rel)&3)*rows, rows), rows), :].astype(out.dtype)

def weight_kernel(at_ref, slab_ref, own_ref, plus_ref, minus_ref, far_ref, total_ref):
    @pl.when(at_ref[0] == 0)
    def _():
        total_ref[...] = sum(dot_tn(slab_ref[i, :, :D], slab_ref[i, :, D:]) for i in range(4))

    @pl.when(at_ref[0] == 1)
    def _():
        total_ref[...] = sum(dot_tn(slab_ref[i, :, D:], slab_ref[i, :, :D]) for i in range(4))

    quarters(at_ref, 2, total_ref, (own_ref, plus_ref, minus_ref, far_ref))


def join_kernel(at_ref,a_ref,b_ref,c_ref,d_ref,out_ref):
    rows=a_ref.shape[0]
    for rel, v in zip(FROM,(a_ref,b_ref,c_ref,d_ref)):
        out_ref[pl.ds(pl.multiple_of(((at_ref[2]+rel)&3)*rows,rows),rows),:] = v[...]

def place_kernel(at_ref, own_ref, other_ref, *rest):
    down_ref, up_ref = rest[-2:]
    first = at_ref[0]==0
    own, other = own_ref[...], other_ref[...]
    down_ref[...] = jnp.where(first, own, other).astype(f32)
    up_ref[...] = jnp.where(first, other, own).astype(f32)

def place(at, rel, own, other, kept):
    tile=256
    n=D//tile
    piece=pl.BlockSpec((tile,D), lambda i,at: (i,0))
    outs=(pl.BlockSpec((tile,D), lambda i,at: (((at[4]+rel)&3)*n+i,0)), pl.BlockSpec((tile,D), lambda i,at: (i,(at[5]+rel)&3)))
    anyspec=pl.BlockSpec(memory_space=pl.ANY)
    return pl.pallas_call(place_kernel,
        grid_spec=pltpu.PrefetchScalarGridSpec(num_scalar_prefetch=1, grid=(n,), in_specs=[piece,piece]+[anyspec]*len(kept), out_specs=outs),
        out_shape=shapes(((FF,D),f32),((D,FF),f32)),
        input_output_aliases={3:0,4:1} if kept else {},
        compiler_params=params(), cost_estimate=cost(0,8e6), name="place")(at, own, other, *kept)


def late_kernel(at_ref, lk_ref, lo_ref, rk_ref, ro_ref, tk_ref, to_ref, out_ref, total_ref):
    first = at_ref[0] == 0
    lk, lo = lk_ref[...], lo_ref[...]
    total_ref[:, 0:D] = dot_tn(lk, rk_ref[...]) + dot_tn(lo, ro_ref[...])

    @pl.when(first)
    def _():
        total_ref[:, D : D + 128] = dot_tn(lk, tk_ref[...].astype(bf16)) + dot_tn(lo, to_ref[...].astype(bf16))

    @pl.when(jnp.logical_not(first))
    def _():
        total_ref[0:128, D : D + 128] = tk_ref[...] + to_ref[...]
        total_ref[128:, D : D + 128] = jnp.zeros((D - 128, 128), f32)

    total_ref[:, D + 128 :] = jnp.zeros((D, 128), f32)
    for a in range(8):
        for b in range(8):
            out_ref[a * 8 + b] = total_ref[a * 96 : a * 96 + 96, b * 128 : b * 128 + 128].astype(bf16)


def late_sum_kernel(parts_ref, out_ref):
    total = jnp.sum(parts_ref[...].astype(f32), axis=0).astype(bf16)
    for i in range(64):
        out_ref[i] = total


VECTORS = ((0, 6), (6, 6), (12, 6), (18, 6), (24, 24), (48, 6), (54, 6), (60, 6))


def late_place_kernel(at_ref, own_ref, other_ref, query_ref, out_ref, kv_ref, value_ref, *vec_refs):
    first = at_ref[0] == 0
    for a in range(8):
        rows = slice(a * 96, a * 96 + 96)
        for b in range(7):
            own, other = own_ref[a * 8 + b].astype(f32), other_ref[a * 8 + b].astype(f32)
            zero, one = jnp.where(first, own, other), jnp.where(first, other, own)
            if b < 6:
                cols = slice(b * 128, b * 128 + 128)
                query_ref[rows, cols] = zero
                out_ref[rows, cols] = one
            else:
                kv_ref[rows, :] = zero
            if b == 6 and a == 0:
                value_ref[...] = one[66, HD:]
                for ref, (at, count) in zip(vec_refs, VECTORS):
                    for i in range(count):
                        ref[i * 128 : (i + 1) * 128] = one[at + i]


def call(kernel, args, outs, scratch=(), name=None, flops=0, nbytes=2e6, after=()):
    given, extra = len(args), len(after)
    run = lambda *refs: kernel(*refs[:given], *refs[given + extra :])
    return pl.pallas_call(
        run,
        out_shape=outs,
        in_specs=[SMEM if v.dtype == jnp.int32 and v.ndim == 1 else VMEM for v in args] + [ANY] * extra,
        out_specs=jax.tree.map(lambda _: VMEM, outs),
        scratch_shapes=list(scratch),
        compiler_params=params(),
        cost_estimate=cost(flops, nbytes),
        name=name,
    )(*args, *after)


def shapes(*pairs):
    return tuple(jax.ShapeDtypeStruct(s, t) for s, t in pairs)


def positions(lengths, splits, wide_index, core):
    ends = jnp.cumsum(lengths, dtype=jnp.int32)
    starts = ends - lengths
    first = lengths * jnp.minimum(splits[:, 0], splits[:, 1]) // 1024
    second = lengths * jnp.maximum(splits[:, 0], splits[:, 1]) // 1024

    def place(row):
        shape = (1,) * row.ndim + (-1,)
        s, e, a, b, n = (v.reshape(shape) for v in (starts, ends, first, second, lengths))
        row = row[..., None]
        inside = (row >= s) & (row < e)
        u = row - s
        moved = jnp.where(u < a, u, jnp.where(u >= b, a + u - b, a + n - b + u - a))
        return (
            jnp.sum(jnp.where(inside, s + moved, 0), axis=-1, dtype=jnp.int32),
            jnp.sum(jnp.where(inside, s, 0), axis=-1, dtype=jnp.int32),
        )

    k = jnp.arange(KB, dtype=jnp.int32)[:, None, None]
    j = jnp.arange(CHIPS, dtype=jnp.int32) * 2
    j = jnp.concatenate([j + core, j + 1 - core])[None, :, None]
    r = jnp.arange(KBR, dtype=jnp.int32)[None, None, :]
    keys, _ = place(((k * KBR + r) * WIDE + j).reshape(KB, KEYS))
    own, own_start = place(jnp.arange(ROWS, dtype=jnp.int32) * WIDE + wide_index)
    low, high = jnp.min(keys, axis=1), jnp.max(keys, axis=1)
    blocks, block_starts = own.reshape(RB, RBR), own_start.reshape(RB, RBR)
    top, start_low = jnp.max(blocks, axis=1), jnp.min(block_starts, axis=1)
    bottom, start_high = jnp.min(blocks, axis=1), jnp.max(block_starts, axis=1)
    some = (low[None] <= top[:, None]) & (high[None] >= start_low[:, None])
    every = (high[None] <= bottom[:, None]) & (low[None] >= start_high[:, None])
    kinds = jnp.where(every, 2, jnp.where(some, 1, 0)).astype(jnp.int32).reshape(-1)
    return keys, own, own_start, kinds


NARROW = ((ROWS, D), bf16)


def attend(*args):
    stat = pltpu.VMEM((RB, 1, QB), f32)
    return call(
        forward_kernel, args,
        shapes(NARROW, NARROW, NARROW, ((RB, QB, 128), bf16), ((RB, QB, 128), f32), ((RB, 1, QB), f32), ((WIDE, ROWS, 2 * HD), bf16)),
        [stat, stat, pltpu.VMEM((RB, 2 * HD, QB), f32), pltpu.VMEM((2 * HD, KEYS), bf16)],
        name="attend", flops=4 * ROWS * H * WINDOW * 64, nbytes=4e6,
    )


def attend_back(*args, after=()):
    return call(
        backward_kernel, args,
        shapes(NARROW, NARROW, NARROW, ((WIDE, ROWS, 2 * HD), bf16)),
        [
            pltpu.VMEM((RB, QB, 128), bf16), pltpu.VMEM((RB, 8, QB), f32),
            pltpu.VMEM((RB, 128, QB), f32), pltpu.VMEM((KEYS, 2 * HD), f32), pltpu.VMEM((2 * HD, KEYS), bf16),
        ],
        name="attend_back", flops=10 * ROWS * H * WINDOW * 64, nbytes=8e6, after=after,
    )


def coords():
    x, y, z, c = (lax.axis_index(a) for a in AXES)
    first = c == 0
    at = (c, jnp.where(first, z, y), jnp.where(first, y, x), jnp.where(first, x, z), z, y)
    return jnp.stack(at).astype(jnp.int32)


def halves_kernel(before_ref, after_ref, low_ref, high_ref):
    low_ref[...] = before_ref[D // 2 :, :]
    high_ref[...] = after_ref[: D // 2, :]


def stack_kernel(high_ref, low_ref, out_ref):
    out_ref[: D // 2, :] = high_ref[...]
    out_ref[D // 2 :, :] = low_ref[...]


QUARTER = ((D // 4, D), bf16)
HALF = ((D // 2, D), bf16)


def pair_sums(a, b, c, d):
    a, b, c, d = (v.astype(f32) for v in (a, b, c, d))
    return ((a + d) + (b + c)).astype(bf16)


def tie_kernel(v_ref, *refs):
    pass


def tie(v, *after):
    return pl.pallas_call(
        tie_kernel,
        out_shape=jax.ShapeDtypeStruct(v.shape, v.dtype),
        in_specs=[ANY] * (1 + len(after)),
        out_specs=ANY,
        input_output_aliases={0: 0},
        cost_estimate=cost(0, 0),
        name="tie",
    )(v, *after)


def feed_forward_spread(at, totals, before_join, before_far):
    u = call(join_kernel, (at,) + totals, shapes(((D, D), bf16))[0], name="join", after=before_join)
    before, after = send(u, 0, 1), send(u, 0, 3)
    kept = place(at, 0, u, swap(u), ())
    low, high = call(halves_kernel, (before, after), shapes(HALF, HALF), name="halves", after=kept[:1])
    low, high = send(low, 0, 1), send(high, 0, 3)
    kept = place(at, 3, before, swap(before), kept)
    kept = place(at, 1, after, swap(after), kept)
    far = call(stack_kernel, (high, low), shapes(((D, D), bf16))[0], name="stack", after=kept[:1] + tuple(before_far))
    return place(at, 2, far, swap(far), kept)


def body(block_input, file_lengths, file_splits, ln1_gain, ln1_bias, w_query, b_query, w_kv, b_value, w_out, b_out,
         ln2_gain, ln2_bias, w_up, b_up, w_down, b_down, out_cotangent):
    x = block_input.reshape(ROWS, D)
    g = out_cotangent.reshape(ROWS, D)
    wide = ("y", "z", "c")
    at = coords()
    narrow = NARROW

    n1, copies = call(enter_kernel, (x, ln1_gain, ln1_bias, w_kv, b_value), shapes(narrow, ((CHIPS, ROWS, 2 * HD), bf16)),
                      name="enter", flops=2 * ROWS * D * 128)
    kv_same = lax.all_to_all(copies, ("y", "z"), 0, 0, tiled=True)
    keys, own, own_start, kinds = positions(file_lengths[0], file_splits[0], lax.axis_index(wide), at[0])
    key_cols = jnp.broadcast_to(keys[:, :, None], (KB, KEYS, 128))
    own_lanes = jnp.tile(own.reshape(RB, 1, RBR), (1, 1, 128 // RBR))
    start_lanes = jnp.tile(own_start.reshape(RB, 1, RBR), (1, 1, 128 // RBR))
    q = call(query_kernel, (n1, w_query, b_query), shapes(narrow)[0], name="query", flops=2 * ROWS * D * D,
             after=(key_cols, own_lanes, start_lanes, kinds))
    kv_other = swap(tie(kv_same, q))

    att, left, left_send, xq, o, lse, kv_all = attend(at, kinds, q, kv_same, kv_other, key_cols, own_lanes, start_lanes, n1)
    left_other = swap(left_send)

    steps = FF // FC
    whole = lambda *s: pl.BlockSpec(s, lambda i: (0,) * len(s))
    wide_cols = pl.BlockSpec((ROWS, FC), lambda i: (0, i))
    y, big, big_send, small, small_send, gr, gb, ga, vec_mid = pl.pallas_call(
        middle_kernel,
        grid=(steps,),
        out_shape=shapes(narrow, ((ROWS, FF), bf16), ((ROWS, FF), bf16), narrow, narrow, ((ROWS, D), f32), narrow, narrow, ((48, 128), f32)),
        in_specs=[
            SMEM, whole(ROWS, D), whole(ROWS, D), whole(ROWS, D), whole(D, D), whole(D), whole(D), whole(D),
            pl.BlockSpec((D, FC), lambda i: (0, i)), pl.BlockSpec((FC,), lambda i: (i,)),
            pl.BlockSpec((FC, D), lambda i: (i, 0)), whole(D),
        ],
        out_specs=(
            whole(ROWS, D), wide_cols, wide_cols, whole(ROWS, D), whole(ROWS, D), whole(ROWS, D), whole(ROWS, D),
            whole(ROWS, D), whole(48, 128),
        ),
        scratch_shapes=[pltpu.VMEM((ROWS, D), f32)] * 3 + [pltpu.VMEM((ROWS, D), bf16)],
        compiler_params=params(),
        cost_estimate=cost(8 * ROWS * D * FF, 2e7),
        name="middle",
    )(at, att, x, g, w_out, b_out, ln2_gain, ln2_bias, w_up, b_up, w_down, b_down)

    packed = call(pack_kernel, (big, small, swap(big_send), swap(small_send)), shapes(((4, 2 * ROWS, 2 * D), bf16))[0], name="pack")
    slabs = lax.all_to_all(packed, AXES, 0, 0, axis_index_groups=ring_groups(0), tiled=True)

    gq, right, right_send, dkv = attend_back(at, kinds, xq, ga, o, lse, kv_all, key_cols, own_lanes, start_lanes, gb, after=(packed,))
    parts = lax.all_to_all(tie(dkv, slabs), wide, 0, 0, tiled=True)
    right_other = swap(right_send)

    pieces = call(weight_kernel, (at, slabs), shapes(*[QUARTER] * 4), [pltpu.VMEM((D, D), f32)], name="weights")
    ff_parts = (pieces[0],) + spread(1, *pieces[1:])
    gin, tail, tail_send, _ = call(
        leave_kernel, (at, x, ln1_gain, w_query, w_kv, gq, parts, gr, vec_mid),
        shapes(((ROWS, D), f32), ((128, 128), f32), ((128, 128), f32), ((128, 128), f32)),
        name="leave", flops=2 * ROWS * D * 900, nbytes=4e6, after=pieces[:1],
    )

    late_pieces = call(late_kernel, (at, left, left_other, right, right_other, tail, swap(tail_send)),
                  shapes(((64, 96, 128), bf16))[0], [pltpu.VMEM((D, 1024), f32)], name="late", after=ff_parts[1:])
    space = ("x", "y", "z")
    arrived = lax.all_to_all(late_pieces, space, 0, 0, tiled=True)
    ff_total = pair_sums(*gather4(pair_sums(*ff_parts), 2))
    ff_totals = gather4(ff_total, 1)
    copies = call(late_sum_kernel, (arrived,), shapes(((64, 96, 128), bf16))[0], name="late_sum", after=ff_totals[1:])
    late = lax.all_to_all(copies, space, 0, 0, tiled=True)
    one = lambda n: ((n,), f32)
    outs = call(
        late_place_kernel, (at, late, swap(late)),
        shapes(((D, D), f32), ((D, D), f32), ((D, 128), f32), one(HD), *[one(128 * n) for _, n in VECTORS]), name="late_place",
    )
    g_query, g_out, g_kv, g_value, g_bdown, g_gain2, g_bias2, g_bout, g_bup, g_gain1, g_bias1, g_bq = outs
    g_down, g_up = feed_forward_spread(at, ff_totals, (copies,), outs[:1])
    shape = block_input.shape
    return (
        y.reshape(shape), gin.reshape(shape), g_gain1, g_bias1, g_query, g_bq, g_kv, g_value,
        g_out, g_bout, g_gain2, g_bias2, g_up, g_bup, g_down, g_bdown,
    )


def solution(mesh):
    split = P("x", None, ("y", "z", "c"), None)
    return jax.shard_map(
        body,
        mesh=Mesh(mesh.devices.reshape(4, 4, 4, 2), AXES),
        in_specs=(split, P("x", None), P("x", None, None)) + (P(),) * 14 + (split,),
        out_specs=(split, split) + (P(),) * 14,
        check_vma=False,
    )
```

```python
import itertools

import jax
import jax.numpy as jnp
from jax import lax
from jax.experimental import pallas as pl
from jax.experimental.pallas import tpu as pltpu
from jax.sharding import Mesh, PartitionSpec as P

EPS = 1e-05
MASKED = -1e30
ROWS = 128
WIDE = 32
CHIPS = 16
D = 768
H = 12
HD = 64
FF = 3072
WINDOW = ROWS * WIDE
RB = 2
RBR = ROWS // RB
QB = RBR * H
KB = 4
KBR = ROWS // KB
KEYS = WINDOW // KB
STRIP = D // CHIPS
FC = 1024
VMEM = pl.BlockSpec(memory_space=pltpu.VMEM)
SMEM = pl.BlockSpec(memory_space=pltpu.SMEM)
ANY = pl.BlockSpec(memory_space=pl.ANY)
f32 = jnp.float32
bf16 = jnp.bfloat16


def params(limit=56):
    return pltpu.CompilerParams(vmem_limit_bytes=limit * 1024 * 1024)


def cost(flops, nbytes):
    return pl.CostEstimate(flops=1, bytes_accessed=1, transcendentals=0)


def dot(a, b):
    return jnp.dot(a, b, preferred_element_type=f32)


def dot_nt(a, b):
    return lax.dot_general(a, b, (((1,), (1,)), ((), ())), preferred_element_type=f32)


def dot_tn(a, b):
    return lax.dot_general(a, b, (((0,), (0,)), ((), ())), preferred_element_type=f32)


def norm_parts(x):
    mean = jnp.mean(x, axis=-1, keepdims=True)
    centered = x - mean
    var = jnp.mean(centered * centered, axis=-1, keepdims=True)
    rstd = lax.rsqrt(var + EPS)
    return centered * rstd, rstd


def norm_back(e, n, rstd, gain):
    m = e * gain
    return rstd * (
        m - jnp.mean(m, axis=-1, keepdims=True) - n * jnp.mean(m * n, axis=-1, keepdims=True)
    )


AXES = ("x", "y", "z", "c")
ORDER = ((2, 1, 0, 0), (1, 0, 2, 0))
FROM = (0, 3, 1, 2)


def ring(place, shift):
    pairs = []
    for at in itertools.product(range(4), range(4), range(4), range(2)):
        to = list(at)
        axis = ORDER[at[3]][place]
        to[axis] = (to[axis] + shift) % 4
        index = lambda v: ((v[0] * 4 + v[1]) * 4 + v[2]) * 2 + v[3]
        pairs.append((index(at), index(to)))
    return pairs


def ring_groups(place):
    groups = {}
    for at in itertools.product(range(4), range(4), range(4), range(2)):
        key = list(at)
        key[ORDER[at[3]][place]] = -1
        groups.setdefault(tuple(key), []).append(((at[0] * 4 + at[1]) * 4 + at[2]) * 2 + at[3])
    return list(groups.values())


def send(v, place, shift):
    return lax.ppermute(v, AXES, ring(place, shift))


def swap(v):
    return lax.ppermute(v, "c", [(0, 1), (1, 0)])


def spread(place, plus, minus, far):
    return send(plus, place, 1), send(minus, place, 3), send(far, place, 2)


def gather4(v, place):
    return (v,) + spread(place, v, v, v)


def lanes_low(shape):
    return lax.broadcasted_iota(jnp.int32, shape, len(shape) - 1) < HD


def vec(ref):
    return ref[...].astype(f32).reshape(1, -1)


def enter_kernel(x_ref, gain_ref, bias_ref, wkv_ref, bv_ref, n1_ref, kv_ref):
    n, _ = norm_parts(x_ref[...].astype(f32))
    n1 = (n * vec(gain_ref) + vec(bias_ref)).astype(bf16)
    n1_ref[...] = n1
    shift = jnp.concatenate([jnp.zeros((1, HD), f32), vec(bv_ref)], axis=1)
    kv = (dot(n1, wkv_ref[...]) + shift).astype(bf16)
    for i in range(CHIPS):
        kv_ref[i] = kv


def query_kernel(n1_ref, wq_ref, bq_ref, q_ref):
    q_ref[...] = (dot(n1_ref[...], wq_ref[...]) + vec(bq_ref)).astype(bf16)


def block_bias(kp, sp, st):
    bias = jnp.where((kp <= sp) & (kp >= st), 0.0, MASKED)
    return jnp.concatenate([bias] * (QB // 128), axis=1)


def visit(cls_ref, kb, step):
    def row_block(rb, _):
        kind = cls_ref[rb * KB + kb]

        @pl.when(kind == 2)
        def _():
            step(rb, False)

        @pl.when(kind == 1)
        def _():
            step(rb, True)

        return 0

    lax.fori_loop(0, RB, row_block, 0)


def forward_kernel(at_ref, cls_ref, q_ref, same_ref, other_ref, kpb_ref, spl_ref, stl_ref, n1_ref,
                   att_ref, keep_ref, send_ref, x_ref, o_ref, lse_ref, kv_ref, m_ref, l_ref, acc_ref, kt_ref):
    kv_ref[:CHIPS] = same_ref[...]
    kv_ref[CHIPS:] = other_ref[...]
    low = lanes_low((ROWS, 2 * HD))
    for h in range(H):
        pair = q_ref[:, (h // 2) * 128 : (h // 2) * 128 + 128].astype(f32) * 0.125
        if h % 2:
            pair = pltpu.roll(pair, HD, 1)
        head = jnp.where(low, pair, 0.0).astype(bf16)
        for rb in range(RB):
            x_ref[rb, h * RBR : (h + 1) * RBR, :] = head[rb * RBR : (rb + 1) * RBR, :]
    m_ref[...] = jnp.full((RB, 1, QB), MASKED, f32)
    l_ref[...] = jnp.zeros((RB, 1, QB), f32)
    acc_ref[...] = jnp.zeros((RB, 2 * HD, QB), f32)

    def key_block(kb, _):
        cols = pl.ds(pl.multiple_of(kb * KBR, KBR), KBR)
        kt_ref[...] = jnp.transpose(kv_ref[:, cols, :].reshape(KEYS, 2 * HD).astype(f32)).astype(bf16)

        def step(rb, masked):
            s = dot_nt(kv_ref[:, cols, :].reshape(KEYS, 2 * HD), x_ref[rb])
            if masked:
                s = s + block_bias(kpb_ref[kb], spl_ref[rb], stl_ref[rb])
            m_old = m_ref[rb]
            m_new = jnp.maximum(m_old, jnp.max(s, axis=0, keepdims=True))
            alpha = jnp.exp(m_old - m_new)
            p = jnp.exp(s - m_new)
            l_ref[rb] = l_ref[rb] * alpha + jnp.sum(p, axis=0, keepdims=True)
            acc_ref[rb] = acc_ref[rb] * alpha + dot(kt_ref[...], p.astype(bf16))
            m_ref[rb] = m_new

        visit(cls_ref, kb, step)
        return 0

    lax.fori_loop(0, KB, key_block, 0)
    keep = lanes_low((RBR, 2 * HD))
    first = at_ref[0] == 0
    for rb in range(RB):
        rows = slice(rb * RBR, (rb + 1) * RBR)
        l = l_ref[rb]
        lse_ref[rb] = m_ref[rb] + jnp.log(l)
        out = jnp.transpose(acc_ref[rb] / l)
        o_ref[rb] = out
        for h in range(0, H, 2):
            even = out[h * RBR : (h + 1) * RBR, :]
            odd = out[(h + 1) * RBR : (h + 2) * RBR, :]
            att_ref[rows, h * HD : (h + 2) * HD] = jnp.where(keep, pltpu.roll(even, HD, 1), odd).astype(bf16)
    n1, att = n1_ref[...], att_ref[...]
    keep_ref[...] = jnp.where(first, n1, att)
    send_ref[...] = jnp.where(first, att, n1)


def backward_kernel(at_ref, cls_ref, x_ref, do_ref, o_ref, lse_ref, kv_ref, kpb_ref, spl_ref, stl_ref, gb_ref,
                    dq_ref, keep_ref, send_ref, same_ref, other_ref, y_ref, drow_ref, dqt_ref, acc_ref, kt_ref):
    low = lanes_low((ROWS, 2 * HD))
    for h in range(H):
        pair = do_ref[:, (h // 2) * 128 : (h // 2) * 128 + 128].astype(f32)
        if h % 2 == 0:
            pair = pltpu.roll(pair, HD, 1)
        head = jnp.where(low, 0.0, pair).astype(bf16)
        for rb in range(RB):
            y_ref[rb, h * RBR : (h + 1) * RBR, :] = head[rb * RBR : (rb + 1) * RBR, :]
    for rb in range(RB):
        delta = jnp.sum(y_ref[rb].astype(f32) * o_ref[rb], axis=1, keepdims=True)
        drow_ref[rb] = jnp.transpose(jnp.broadcast_to(delta, (QB, 128)))[:8]
    dqt_ref[...] = jnp.zeros((RB, 128, QB), f32)

    def key_block(kb, _):
        cols = pl.ds(pl.multiple_of(kb * KBR, KBR), KBR)
        kvb = kv_ref[:, cols, :].reshape(KEYS, 2 * HD)
        kt_ref[...] = jnp.transpose(kvb.astype(f32)).astype(bf16)
        acc_ref[...] = jnp.zeros((KEYS, 2 * HD), f32)

        def step(rb, masked):
            kvb = kv_ref[:, cols, :].reshape(KEYS, 2 * HD)
            xb, yb = x_ref[rb], y_ref[rb]
            s = dot_nt(kvb, xb)
            if masked:
                s = s + block_bias(kpb_ref[kb], spl_ref[rb], stl_ref[rb])
            p = jnp.exp(s - lse_ref[rb])
            ds = (p * (dot_nt(kvb, yb) - drow_ref[rb, :1])).astype(bf16)
            acc_ref[...] += dot(ds, xb) + dot(p.astype(bf16), yb)
            dqt_ref[rb] += dot(kt_ref[...], ds)

        visit(cls_ref, kb, step)
        sums = acc_ref[...].reshape(WIDE, KBR, 2 * HD).astype(bf16)
        same_ref[:, cols, :] = sums[:CHIPS]
        other_ref[:, cols, :] = sums[CHIPS:]
        return 0

    lax.fori_loop(0, KB, key_block, 0)
    keep = lanes_low((RBR, 2 * HD))
    for rb in range(RB):
        dq = jnp.transpose(dqt_ref[rb]) * 0.125
        for h in range(0, H, 2):
            even = dq[h * RBR : (h + 1) * RBR, :]
            odd = dq[(h + 1) * RBR : (h + 2) * RBR, :]
            dq_ref[rb * RBR : (rb + 1) * RBR, h * HD : (h + 2) * HD] = jnp.where(
                keep, even, pltpu.roll(odd, HD, 1)
            ).astype(bf16)
    first = at_ref[0] == 0
    dq, gb = dq_ref[...], gb_ref[...]
    keep_ref[...] = jnp.where(first, dq, gb)
    send_ref[...] = jnp.where(first, gb, dq)


def put_rows(ref, at, row):
    for i in range(row.shape[1] // 128):
        ref[pl.ds(at + i, 1), :] = row[:, i * 128 : (i + 1) * 128]


def middle_kernel(at_ref, att_ref, x_ref, g_ref, wout_ref, bout_ref, gain_ref, bias_ref, wup_ref, bup_ref, wdown_ref, bdown_ref,
                  y_ref, bk_ref, bs_ref, sk_ref, ss_ref, gr_ref, gb_ref, ga_ref, vec_ref,
                  resid_ref, out_ref, gn2_ref, n2_ref):
    step = pl.program_id(0)
    first = at_ref[0] == 0

    @pl.when(step == 0)
    def _():
        resid = x_ref[...].astype(f32) + (dot(att_ref[...], wout_ref[...]) + vec(bout_ref))
        resid_ref[...] = resid
        n, _ = norm_parts(resid)
        n2 = (n * vec(gain_ref) + vec(bias_ref)).astype(bf16)
        n2_ref[...] = n2
        sk_ref[...] = jnp.where(first, g_ref[...], n2)
        ss_ref[...] = jnp.where(first, n2, g_ref[...])
        out_ref[...] = jnp.zeros_like(out_ref)
        gn2_ref[...] = jnp.zeros_like(gn2_ref)

    g = g_ref[...]
    pre = dot(n2_ref[...], wup_ref[...]) + vec(bup_ref)
    sq = pre * pre
    t = jnp.tanh(0.7978845608028654 * (pre + 0.044715 * sq * pre))
    half = 0.5 + 0.5 * t
    act = (pre * half).astype(bf16)
    slope = half + (0.5 * 0.7978845608028654) * pre * (1.0 - t * t) * (1.0 + (3 * 0.044715) * sq)
    gp = (slope * dot_nt(g, wdown_ref[...])).astype(bf16)
    bk_ref[...] = jnp.where(first, act, gp)
    bs_ref[...] = jnp.where(first, gp, act)
    put_rows(vec_ref, 24 + step * (FC // 128), jnp.sum(gp.astype(f32), axis=0, keepdims=True))
    out_ref[...] += dot(act, wdown_ref[...])
    gn2_ref[...] += dot_nt(gp, wup_ref[...])

    @pl.when(step == pl.num_programs(0) - 1)
    def _():
        resid = resid_ref[...]
        gf = g.astype(f32)
        y_ref[...] = (resid + (out_ref[...] + vec(bdown_ref))).astype(bf16)
        n, rstd = norm_parts(resid)
        e = gn2_ref[...]
        gr = gf + norm_back(e, n, rstd, vec(gain_ref))
        gr_ref[...] = gr
        gb = gr.astype(bf16)
        gb_ref[...] = gb
        ga_ref[...] = dot_nt(gb, wout_ref[...]).astype(bf16)
        put_rows(vec_ref, 0, jnp.sum(gf, axis=0, keepdims=True))
        put_rows(vec_ref, 6, jnp.sum(e * n, axis=0, keepdims=True))
        put_rows(vec_ref, 12, jnp.sum(e, axis=0, keepdims=True))
        put_rows(vec_ref, 18, jnp.sum(gb.astype(f32), axis=0, keepdims=True))


def leave_kernel(at_ref, x_ref, gain_ref, wq_ref, wkv_ref, gq_ref, gr_ref, mid_ref, parts_ref, _, gin_ref, keep_ref, send_ref, vec_ref):
    gkv = jnp.sum(parts_ref[...].astype(f32), axis=0).astype(bf16)
    gq = gq_ref[...]
    e = dot_nt(gq, wq_ref[...]) + dot_nt(gkv, wkv_ref[...])
    n, rstd = norm_parts(x_ref[...].astype(f32))
    gin = gr_ref[...] + norm_back(e, n, rstd, vec(gain_ref))
    for i in range(D // 128):
        gin_ref[pl.ds(i, ROWS, stride=D // 128), :] = gin[:, i * 128 : (i + 1) * 128]
    gkv = gkv.astype(f32)
    vec_ref[0:48, :] = mid_ref[...]
    vec_ref[48:128, :] = jnp.zeros((80, 128), f32)
    put_rows(vec_ref, 48, jnp.sum(e * n, axis=0, keepdims=True))
    put_rows(vec_ref, 54, jnp.sum(e, axis=0, keepdims=True))
    put_rows(vec_ref, 60, jnp.sum(gq.astype(f32), axis=0, keepdims=True))
    put_rows(vec_ref, 66, jnp.sum(gkv, axis=0, keepdims=True))
    first = at_ref[0] == 0
    vecs = vec_ref[...]
    keep_ref[...] = jnp.where(first, gkv, vecs)
    send_ref[...] = jnp.where(first, vecs, gkv)


def pack_kernel(bk_ref, sk_ref, bp_ref, sp_ref, out_ref):
    for i in range(4):
        cols = slice(i * D, (i + 1) * D)
        out_ref[i, 0:ROWS, 0:D] = bk_ref[:, cols]
        out_ref[i, ROWS:, 0:D] = bp_ref[:, cols]
        out_ref[i, 0:ROWS, D:] = sk_ref[...]
        out_ref[i, ROWS:, D:] = sp_ref[...]

def quarters(at, which, total_ref, outs):
    rows = total_ref.shape[0]//4
    for rel, out in zip((0,1,3,2), outs):
        out[...] = total_ref[pl.ds(pl.multiple_of(((at[which]+rel)&3)*rows, rows), rows), :].astype(out.dtype)

def weight_kernel(at_ref, slab_ref, own_ref, plus_ref, minus_ref, far_ref, total_ref):
    @pl.when(at_ref[0] == 0)
    def _():
        total_ref[...] = sum(dot_tn(slab_ref[i, :, :D], slab_ref[i, :, D:]) for i in range(4))

    @pl.when(at_ref[0] == 1)
    def _():
        total_ref[...] = sum(dot_tn(slab_ref[i, :, D:], slab_ref[i, :, :D]) for i in range(4))

    quarters(at_ref, 2, total_ref, (own_ref, plus_ref, minus_ref, far_ref))


def join_kernel(at_ref,a_ref,b_ref,c_ref,d_ref,out_ref):
    rows=a_ref.shape[0]
    for rel, v in zip(FROM,(a_ref,b_ref,c_ref,d_ref)):
        out_ref[pl.ds(pl.multiple_of(((at_ref[2]+rel)&3)*rows,rows),rows),:] = v[...]

def place_kernel(at_ref, own_ref, other_ref, *rest):
    down_ref, up_ref = rest[-2:]
    first = at_ref[0]==0
    own, other = own_ref[...], other_ref[...]
    down_ref[...] = jnp.where(first, own, other).astype(f32)
    up_ref[...] = jnp.where(first, other, own).astype(f32)

def place(at, rel, own, other, kept, part=0):
    tile = D // 2
    n = own.shape[0] // tile
    piece = pl.BlockSpec((tile, D), lambda i, at: (i, 0))
    outs = (
        pl.BlockSpec((tile, D), lambda i, at: (((at[4] + rel) & 3) * 2 + part + i, 0)),
        pl.BlockSpec((tile, D), lambda i, at: (part + i, (at[5] + rel) & 3)),
    )
    return pl.pallas_call(
        place_kernel,
        grid_spec=pltpu.PrefetchScalarGridSpec(
            num_scalar_prefetch=1, grid=(n,), in_specs=[piece, piece] + [ANY] * len(kept), out_specs=outs
        ),
        out_shape=shapes(((FF, D), f32), ((D, FF), f32)),
        input_output_aliases={3: 0, 4: 1} if kept else {},
        compiler_params=params(),
        cost_estimate=cost(0, 8e6),
        name="place",
    )(at, own, other, *kept)


def share_kernel(same_ref, other_ref, lk_ref, lo_ref, rk_ref, ro_ref, out_ref, total_ref):
    out_ref[:, 0:ROWS, :] = (same_ref[...].astype(f32) + other_ref[...].astype(f32)).astype(bf16)
    total_ref[...] = dot_tn(lk_ref[...], rk_ref[...]) + dot_tn(lo_ref[...], ro_ref[...])
    for i in range(CHIPS):
        for b in range(6):
            out_ref[i, ROWS + STRIP * b : ROWS + STRIP * (b + 1), :] = total_ref[
                STRIP * i : STRIP * (i + 1), 128 * b : 128 * (b + 1)
            ].astype(bf16)


def late_kernel(at_ref, lk_ref, lo_ref, tk_ref, to_ref, out_ref, total_ref):
    first = at_ref[0] == 0

    @pl.when(first)
    def _():
        total_ref[...] = dot_tn(lk_ref[...], tk_ref[...].astype(bf16)) + dot_tn(lo_ref[...], to_ref[...].astype(bf16))

    @pl.when(jnp.logical_not(first))
    def _():
        total_ref[0:128, :] = tk_ref[...] + to_ref[...]
        total_ref[128:, :] = jnp.zeros((D - 128, 128), f32)

    for i in range(CHIPS):
        out_ref[i] = total_ref[STRIP * i : STRIP * (i + 1), :].astype(bf16)


def strip_kernel(parts_ref, tail_ref, out_ref):
    for b in range(6):
        rows = slice(ROWS + STRIP * b, ROWS + STRIP * (b + 1))
        out_ref[:, 128 * b : 128 * (b + 1)] = jnp.sum(parts_ref[:, rows, :].astype(f32), axis=0).astype(bf16)
    out_ref[:, D:] = jnp.sum(tail_ref[...].astype(f32), axis=0).astype(bf16)


def copies_kernel(a_ref, b_ref, c_ref, d_ref, out_ref):
    total = pair_sums(a_ref[...], b_ref[...], c_ref[...], d_ref[...])
    for i in range(CHIPS):
        out_ref[i] = total


VECTORS = ((0, 6), (6, 6), (12, 6), (18, 6), (24, 24), (48, 6), (54, 6), (60, 6))


def late_place_kernel(at_ref, own_ref, other_ref, query_ref, out_ref, kv_ref, value_ref, *vec_refs):
    first = at_ref[0] == 0
    vecs = []
    for a in range(CHIPS):
        rows = slice(STRIP * a, STRIP * (a + 1))
        own, other = own_ref[a].astype(f32), other_ref[a].astype(f32)
        zero, one = jnp.where(first, own, other), jnp.where(first, other, own)
        query_ref[rows, :] = zero[:, :D]
        out_ref[rows, :] = one[:, :D]
        kv_ref[rows, :] = zero[:, D:]
        if a < 2:
            vecs.append(one[:, D:])
    row = lambda i: vecs[i // STRIP][i % STRIP]
    value_ref[...] = row(66)[HD:]
    for ref, (at, count) in zip(vec_refs, VECTORS):
        for i in range(count):
            ref[i * 128 : (i + 1) * 128] = row(at + i)


def call(kernel, args, outs, scratch=(), name=None, flops=0, nbytes=2e6, after=()):
    given, extra = len(args), len(after)
    run = lambda *refs: kernel(*refs[:given], *refs[given + extra :])
    return pl.pallas_call(
        run,
        out_shape=outs,
        in_specs=[SMEM if v.dtype == jnp.int32 and v.ndim == 1 else VMEM for v in args] + [ANY] * extra,
        out_specs=jax.tree.map(lambda _: VMEM, outs),
        scratch_shapes=list(scratch),
        compiler_params=params(),
        cost_estimate=cost(flops, nbytes),
        name=name,
    )(*args, *after)


def shapes(*pairs):
    return tuple(jax.ShapeDtypeStruct(s, t) for s, t in pairs)


def positions(lengths, splits, wide_index, core):
    ends = jnp.cumsum(lengths, dtype=jnp.int32)
    starts = ends - lengths
    first = lengths * jnp.minimum(splits[:, 0], splits[:, 1]) // 1024
    second = lengths * jnp.maximum(splits[:, 0], splits[:, 1]) // 1024

    def place(row):
        shape = (1,) * row.ndim + (-1,)
        s, e, a, b, n = (v.reshape(shape) for v in (starts, ends, first, second, lengths))
        row = row[..., None]
        inside = (row >= s) & (row < e)
        u = row - s
        moved = jnp.where(u < a, u, jnp.where(u >= b, a + u - b, a + n - b + u - a))
        return (
            jnp.sum(jnp.where(inside, s + moved, 0), axis=-1, dtype=jnp.int32),
            jnp.sum(jnp.where(inside, s, 0), axis=-1, dtype=jnp.int32),
        )

    k = jnp.arange(KB, dtype=jnp.int32)[:, None, None]
    j = jnp.arange(CHIPS, dtype=jnp.int32) * 2
    j = jnp.concatenate([j + core, j + 1 - core])[None, :, None]
    r = jnp.arange(KBR, dtype=jnp.int32)[None, None, :]
    keys, _ = place(((k * KBR + r) * WIDE + j).reshape(KB, KEYS))
    own, own_start = place(jnp.arange(ROWS, dtype=jnp.int32) * WIDE + wide_index)
    low, high = jnp.min(keys, axis=1), jnp.max(keys, axis=1)
    blocks, block_starts = own.reshape(RB, RBR), own_start.reshape(RB, RBR)
    top, start_low = jnp.max(blocks, axis=1), jnp.min(block_starts, axis=1)
    bottom, start_high = jnp.min(blocks, axis=1), jnp.max(block_starts, axis=1)
    some = (low[None] <= top[:, None]) & (high[None] >= start_low[:, None])
    every = (high[None] <= bottom[:, None]) & (low[None] >= start_high[:, None])
    kinds = jnp.where(every, 2, jnp.where(some, 1, 0)).astype(jnp.int32).reshape(-1)
    return keys, own, own_start, kinds


NARROW = ((ROWS, D), bf16)
KV_HALF = ((CHIPS, ROWS, 2 * HD), bf16)


def attend(*args):
    stat = pltpu.VMEM((RB, 1, QB), f32)
    return call(
        forward_kernel, args,
        shapes(NARROW, NARROW, NARROW, ((RB, QB, 128), bf16), ((RB, QB, 128), f32), ((RB, 1, QB), f32), ((WIDE, ROWS, 2 * HD), bf16)),
        [stat, stat, pltpu.VMEM((RB, 2 * HD, QB), f32), pltpu.VMEM((2 * HD, KEYS), bf16)],
        name="attend", flops=4 * ROWS * H * WINDOW * 64, nbytes=4e6,
    )


def attend_back(*args, after=()):
    return call(
        backward_kernel, args,
        shapes(NARROW, NARROW, NARROW, KV_HALF, KV_HALF),
        [
            pltpu.VMEM((RB, QB, 128), bf16), pltpu.VMEM((RB, 8, QB), f32),
            pltpu.VMEM((RB, 128, QB), f32), pltpu.VMEM((KEYS, 2 * HD), f32), pltpu.VMEM((2 * HD, KEYS), bf16),
        ],
        name="attend_back", flops=10 * ROWS * H * WINDOW * 64, nbytes=8e6, after=after,
    )


def coords():
    x, y, z, c = (lax.axis_index(a) for a in AXES)
    first = c == 0
    at = (c, jnp.where(first, z, y), jnp.where(first, y, x), jnp.where(first, x, z), z, y)
    return jnp.stack(at).astype(jnp.int32)


def halves_kernel(before_ref, after_ref, low_ref, high_ref):
    low_ref[...] = before_ref[D // 2 :, :]
    high_ref[...] = after_ref[: D // 2, :]


QUARTER = ((D // 4, D), bf16)
HALF = ((D // 2, D), bf16)


def pair_sums(a, b, c, d):
    a, b, c, d = (v.astype(f32) for v in (a, b, c, d))
    return ((a + d) + (b + c)).astype(bf16)


def tie_kernel(v_ref, *refs):
    pass


def tie(v, *after):
    return pl.pallas_call(
        tie_kernel,
        out_shape=jax.ShapeDtypeStruct(v.shape, v.dtype),
        in_specs=[ANY] * (1 + len(after)),
        out_specs=ANY,
        input_output_aliases={0: 0},
        cost_estimate=cost(0, 0),
        name="tie",
    )(v, *after)


def feed_forward_spread(at, totals, before_join, before_far):
    u = call(join_kernel, (at,) + totals, shapes(((D, D), bf16))[0], name="join", after=before_join)
    before, after = send(u, 0, 1), send(u, 0, 3)
    kept = place(at, 0, u, swap(u), ())
    low, high = call(halves_kernel, (before, after), shapes(HALF, HALF), name="halves", after=kept[:1])
    low, high = send(low, 0, 1), send(high, 0, 3)
    kept = place(at, 3, before, swap(before), kept)
    kept = place(at, 1, after, swap(after), kept)
    low, high = (tie(v, kept[0], *before_far) for v in (low, high))
    kept = place(at, 2, high, swap(high), kept)
    return place(at, 2, low, swap(low), kept, part=1)


def body(block_input, file_lengths, file_splits, ln1_gain, ln1_bias, w_query, b_query, w_kv, b_value, w_out, b_out,
         ln2_gain, ln2_bias, w_up, b_up, w_down, b_down, out_cotangent):
    x = block_input.reshape(ROWS, D)
    g = out_cotangent.reshape(ROWS, D)
    wide = ("y", "z", "c")
    at = coords()
    narrow = NARROW

    n1, copies = call(enter_kernel, (x, ln1_gain, ln1_bias, w_kv, b_value), shapes(narrow, ((CHIPS, ROWS, 2 * HD), bf16)),
                      name="enter", flops=2 * ROWS * D * 128)
    kv_same = lax.all_to_all(copies, ("y", "z"), 0, 0, tiled=True)
    keys, own, own_start, kinds = positions(file_lengths[0], file_splits[0], lax.axis_index(wide), at[0])
    key_cols = jnp.broadcast_to(keys[:, :, None], (KB, KEYS, 128))
    own_lanes = jnp.tile(own.reshape(RB, 1, RBR), (1, 1, 128 // RBR))
    start_lanes = jnp.tile(own_start.reshape(RB, 1, RBR), (1, 1, 128 // RBR))
    q = call(query_kernel, (n1, w_query, b_query), shapes(narrow)[0], name="query", flops=2 * ROWS * D * D,
             after=(key_cols, own_lanes, start_lanes, kinds))
    kv_other = swap(tie(kv_same, q))

    att, left, left_send, xq, o, lse, kv_all = attend(at, kinds, q, kv_same, kv_other, key_cols, own_lanes, start_lanes, n1)
    left_other = swap(left_send)

    steps = FF // FC
    whole = lambda *s: pl.BlockSpec(s, lambda i: (0,) * len(s))
    wide_cols = pl.BlockSpec((ROWS, FC), lambda i: (0, i))
    y, big, big_send, small, small_send, gr, gb, ga, vec_mid = pl.pallas_call(
        middle_kernel,
        grid=(steps,),
        out_shape=shapes(narrow, ((ROWS, FF), bf16), ((ROWS, FF), bf16), narrow, narrow, ((ROWS, D), f32), narrow, narrow, ((48, 128), f32)),
        in_specs=[
            SMEM, whole(ROWS, D), whole(ROWS, D), whole(ROWS, D), whole(D, D), whole(D), whole(D), whole(D),
            pl.BlockSpec((D, FC), lambda i: (0, i)), pl.BlockSpec((FC,), lambda i: (i,)),
            pl.BlockSpec((FC, D), lambda i: (i, 0)), whole(D),
        ],
        out_specs=(
            whole(ROWS, D), wide_cols, wide_cols, whole(ROWS, D), whole(ROWS, D), whole(ROWS, D), whole(ROWS, D),
            whole(ROWS, D), whole(48, 128),
        ),
        scratch_shapes=[pltpu.VMEM((ROWS, D), f32)] * 3 + [pltpu.VMEM((ROWS, D), bf16)],
        compiler_params=params(),
        cost_estimate=cost(8 * ROWS * D * FF, 2e7),
        name="middle",
    )(at, att, x, g, w_out, b_out, ln2_gain, ln2_bias, w_up, b_up, w_down, b_down)

    packed = call(pack_kernel, (big, small, swap(big_send), swap(small_send)), shapes(((4, 2 * ROWS, 2 * D), bf16))[0], name="pack")
    slabs = lax.all_to_all(packed, AXES, 0, 0, axis_index_groups=ring_groups(0), tiled=True)

    gq, right, right_send, kv_grads, kv_send = attend_back(at, kinds, xq, ga, o, lse, kv_all, key_cols, own_lanes, start_lanes, gb, after=(packed,))
    shares = call(share_kernel, (kv_grads, swap(kv_send), left, left_other, right, swap(right_send)),
                  shapes(((CHIPS, ROWS + 6 * STRIP, 128), bf16))[0], [pltpu.VMEM((D, D), f32)], name="share", after=(slabs,))
    parts = lax.all_to_all(shares, ("y", "z"), 0, 0, tiled=True)

    pieces = call(weight_kernel, (at, slabs), shapes(*[QUARTER] * 4), [pltpu.VMEM((D, D), f32)], name="weights")
    ff_parts = (pieces[0],) + spread(1, *pieces[1:])
    ff_crossed = gather4(pair_sums(*ff_parts), 2)
    gin, tail, tail_send, _ = pl.pallas_call(
        leave_kernel,
        grid=(1,),
        out_shape=shapes(((ROWS * D // 128, 128), f32), ((128, 128), f32), ((128, 128), f32), ((128, 128), f32)),
        in_specs=[SMEM] + [VMEM] * 7 + [pl.BlockSpec((CHIPS, ROWS, 128), lambda i: (0, 0, 0)), ANY],
        out_specs=(VMEM,) * 4,
        compiler_params=params(),
        cost_estimate=cost(2 * ROWS * D * 900, 4e6),
        name="leave",
    )(at, x, ln1_gain, w_query, w_kv, gq, gr, vec_mid, parts, pieces[0])

    late_parts = call(late_kernel, (at, left, left_other, tail, swap(tail_send)), shapes(((CHIPS, STRIP, 128), bf16))[0],
                      [pltpu.VMEM((D, 128), f32)], name="late", after=ff_parts[1:])
    late_parts = lax.all_to_all(late_parts, ("y", "z"), 0, 0, tiled=True)
    ff_totals = gather4(pair_sums(*ff_crossed), 1)
    strip = call(strip_kernel, (parts, late_parts), shapes(((STRIP, D + 128), bf16))[0], name="strip", after=ff_crossed[1:])
    strips = gather4(strip, 3)
    copies = call(copies_kernel, strips, shapes(((CHIPS, STRIP, D + 128), bf16))[0], name="copies", after=ff_totals[1:])
    late = lax.all_to_all(copies, ("y", "z"), 0, 0, tiled=True)
    one = lambda n: ((n,), f32)
    outs = call(
        late_place_kernel, (at, late, swap(late)),
        shapes(((D, D), f32), ((D, D), f32), ((D, 128), f32), one(HD), *[one(128 * n) for _, n in VECTORS]), name="late_place",
    )
    g_query, g_out, g_kv, g_value, g_bdown, g_gain2, g_bias2, g_bout, g_bup, g_gain1, g_bias1, g_bq = outs
    g_down, g_up = feed_forward_spread(at, ff_totals, (copies,), outs[:1])
    shape = block_input.shape
    return (
        y.reshape(shape), gin.reshape(shape), g_gain1, g_bias1, g_query, g_bq, g_kv, g_value,
        g_out, g_bout, g_gain2, g_bias2, g_up, g_bup, g_down, g_bdown,
    )


def solution(mesh):
    split = P("x", None, ("y", "z", "c"), None)
    return jax.shard_map(
        body,
        mesh=Mesh(mesh.devices.reshape(4, 4, 4, 2), AXES),
        in_specs=(split, P("x", None), P("x", None, None)) + (P(),) * 14 + (split,),
        out_specs=(split, split) + (P(),) * 14,
        check_vma=False,
    )
```

```python
import itertools

import jax
import jax.numpy as jnp
from jax import lax
from jax.experimental import pallas as pl
from jax.experimental.pallas import tpu as pltpu
from jax.sharding import Mesh, PartitionSpec as P

EPS = 1e-05
MASKED = -1e30
ROWS = 128
WIDE = 32
CHIPS = 16
D = 768
H = 12
HD = 64
FF = 3072
WINDOW = ROWS * WIDE
RB = 2
RBR = ROWS // RB
QB = RBR * H
KB = 4
KBR = ROWS // KB
KEYS = WINDOW // KB
STRIP = D // CHIPS
FC = 1024
VMEM = pl.BlockSpec(memory_space=pltpu.VMEM)
SMEM = pl.BlockSpec(memory_space=pltpu.SMEM)
ANY = pl.BlockSpec(memory_space=pl.ANY)
f32 = jnp.float32
bf16 = jnp.bfloat16


def params(limit=56):
    return pltpu.CompilerParams(vmem_limit_bytes=limit * 1024 * 1024)


def cost(flops, nbytes):
    return pl.CostEstimate(flops=1, bytes_accessed=1, transcendentals=0)


def dot(a, b):
    return jnp.dot(a, b, preferred_element_type=f32)


def dot_nt(a, b):
    return lax.dot_general(a, b, (((1,), (1,)), ((), ())), preferred_element_type=f32)


def dot_tn(a, b):
    return lax.dot_general(a, b, (((0,), (0,)), ((), ())), preferred_element_type=f32)


def norm_parts(x):
    mean = jnp.mean(x, axis=-1, keepdims=True)
    centered = x - mean
    var = jnp.mean(centered * centered, axis=-1, keepdims=True)
    rstd = lax.rsqrt(var + EPS)
    return centered * rstd, rstd


def norm_back(e, n, rstd, gain):
    m = e * gain
    return rstd * (
        m - jnp.mean(m, axis=-1, keepdims=True) - n * jnp.mean(m * n, axis=-1, keepdims=True)
    )


AXES = ("x", "y", "z", "c")
ORDER = ((2, 1, 0, 0), (1, 0, 2, 0))
FROM = (0, 3, 1, 2)


def ring(place, shift):
    pairs = []
    for at in itertools.product(range(4), range(4), range(4), range(2)):
        to = list(at)
        axis = ORDER[at[3]][place]
        to[axis] = (to[axis] + shift) % 4
        index = lambda v: ((v[0] * 4 + v[1]) * 4 + v[2]) * 2 + v[3]
        pairs.append((index(at), index(to)))
    return pairs


def ring_groups(place):
    groups = {}
    for at in itertools.product(range(4), range(4), range(4), range(2)):
        key = list(at)
        key[ORDER[at[3]][place]] = -1
        groups.setdefault(tuple(key), []).append(((at[0] * 4 + at[1]) * 4 + at[2]) * 2 + at[3])
    return list(groups.values())


def send(v, place, shift):
    return lax.ppermute(v, AXES, ring(place, shift))


def swap(v):
    return lax.ppermute(v, "c", [(0, 1), (1, 0)])


def spread(place, plus, minus, far):
    return send(plus, place, 1), send(minus, place, 3), send(far, place, 2)


def gather4(v, place):
    return (v,) + spread(place, v, v, v)


def lanes_low(shape):
    return lax.broadcasted_iota(jnp.int32, shape, len(shape) - 1) < HD


def vec(ref):
    return ref[...].astype(f32).reshape(1, -1)


def enter_kernel(x_ref, gain_ref, bias_ref, wkv_ref, bv_ref, n1_ref, kv_ref):
    n, _ = norm_parts(x_ref[...].astype(f32))
    n1 = (n * vec(gain_ref) + vec(bias_ref)).astype(bf16)
    n1_ref[...] = n1
    shift = jnp.concatenate([jnp.zeros((1, HD), f32), vec(bv_ref)], axis=1)
    kv = (dot(n1, wkv_ref[...]) + shift).astype(bf16)
    for i in range(CHIPS):
        kv_ref[i] = kv


def query_kernel(n1_ref, wq_ref, bq_ref, q_ref):
    q_ref[...] = (dot(n1_ref[...], wq_ref[...]) + vec(bq_ref)).astype(bf16)


def block_bias(kp, sp, st):
    bias = jnp.where((kp <= sp) & (kp >= st), 0.0, MASKED)
    return jnp.concatenate([bias] * (QB // 128), axis=1)


def visit(cls_ref, kb, step):
    def row_block(rb, _):
        kind = cls_ref[rb * KB + kb]

        @pl.when(kind == 2)
        def _():
            step(rb, False)

        @pl.when(kind == 1)
        def _():
            step(rb, True)

        return 0

    lax.fori_loop(0, RB, row_block, 0)


def forward_kernel(at_ref, cls_ref, q_ref, same_ref, other_ref, kpb_ref, spl_ref, stl_ref, n1_ref,
                   att_ref, keep_ref, send_ref, x_ref, o_ref, lse_ref, kv_ref, m_ref, l_ref, acc_ref, kt_ref):
    kv_ref[:CHIPS] = same_ref[...]
    kv_ref[CHIPS:] = other_ref[...]
    low = lanes_low((ROWS, 2 * HD))
    for h in range(H):
        pair = q_ref[:, (h // 2) * 128 : (h // 2) * 128 + 128].astype(f32) * 0.125
        if h % 2:
            pair = pltpu.roll(pair, HD, 1)
        head = jnp.where(low, pair, 0.0).astype(bf16)
        for rb in range(RB):
            x_ref[rb, h * RBR : (h + 1) * RBR, :] = head[rb * RBR : (rb + 1) * RBR, :]
    m_ref[...] = jnp.full((RB, 1, QB), MASKED, f32)
    l_ref[...] = jnp.zeros((RB, 1, QB), f32)
    acc_ref[...] = jnp.zeros((RB, 2 * HD, QB), f32)

    def key_block(kb, _):
        cols = pl.ds(pl.multiple_of(kb * KBR, KBR), KBR)
        kt_ref[...] = jnp.transpose(kv_ref[:, cols, :].reshape(KEYS, 2 * HD).astype(f32)).astype(bf16)

        def step(rb, masked):
            s = dot_nt(kv_ref[:, cols, :].reshape(KEYS, 2 * HD), x_ref[rb])
            if masked:
                s = s + block_bias(kpb_ref[kb], spl_ref[rb], stl_ref[rb])
            m_old = m_ref[rb]
            m_new = jnp.maximum(m_old, jnp.max(s, axis=0, keepdims=True))
            alpha = jnp.exp(m_old - m_new)
            p = jnp.exp(s - m_new)
            l_ref[rb] = l_ref[rb] * alpha + jnp.sum(p, axis=0, keepdims=True)
            acc_ref[rb] = acc_ref[rb] * alpha + dot(kt_ref[...], p.astype(bf16))
            m_ref[rb] = m_new

        visit(cls_ref, kb, step)
        return 0

    lax.fori_loop(0, KB, key_block, 0)
    keep = lanes_low((RBR, 2 * HD))
    first = at_ref[0] == 0
    for rb in range(RB):
        rows = slice(rb * RBR, (rb + 1) * RBR)
        l = l_ref[rb]
        lse_ref[rb] = m_ref[rb] + jnp.log(l)
        out = jnp.transpose(acc_ref[rb] / l)
        o_ref[rb] = out
        for h in range(0, H, 2):
            even = out[h * RBR : (h + 1) * RBR, :]
            odd = out[(h + 1) * RBR : (h + 2) * RBR, :]
            att_ref[rows, h * HD : (h + 2) * HD] = jnp.where(keep, pltpu.roll(even, HD, 1), odd).astype(bf16)
    n1, att = n1_ref[...], att_ref[...]
    keep_ref[...] = jnp.where(first, n1, att)
    send_ref[...] = jnp.where(first, att, n1)


def backward_kernel(at_ref, cls_ref, x_ref, do_ref, o_ref, lse_ref, kv_ref, kpb_ref, spl_ref, stl_ref, gb_ref,
                    dq_ref, keep_ref, send_ref, same_ref, other_ref, y_ref, drow_ref, dqt_ref, acc_ref, kt_ref):
    low = lanes_low((ROWS, 2 * HD))
    for h in range(H):
        pair = do_ref[:, (h // 2) * 128 : (h // 2) * 128 + 128].astype(f32)
        if h % 2 == 0:
            pair = pltpu.roll(pair, HD, 1)
        head = jnp.where(low, 0.0, pair).astype(bf16)
        for rb in range(RB):
            y_ref[rb, h * RBR : (h + 1) * RBR, :] = head[rb * RBR : (rb + 1) * RBR, :]
    for rb in range(RB):
        delta = jnp.sum(y_ref[rb].astype(f32) * o_ref[rb], axis=1, keepdims=True)
        drow_ref[rb] = jnp.transpose(jnp.broadcast_to(delta, (QB, 128)))[:8]
    dqt_ref[...] = jnp.zeros((RB, 128, QB), f32)

    def key_block(kb, _):
        cols = pl.ds(pl.multiple_of(kb * KBR, KBR), KBR)
        kvb = kv_ref[:, cols, :].reshape(KEYS, 2 * HD)
        kt_ref[...] = jnp.transpose(kvb.astype(f32)).astype(bf16)
        acc_ref[...] = jnp.zeros((KEYS, 2 * HD), f32)

        def step(rb, masked):
            kvb = kv_ref[:, cols, :].reshape(KEYS, 2 * HD)
            xb, yb = x_ref[rb], y_ref[rb]
            s = dot_nt(kvb, xb)
            if masked:
                s = s + block_bias(kpb_ref[kb], spl_ref[rb], stl_ref[rb])
            p = jnp.exp(s - lse_ref[rb])
            ds = (p * (dot_nt(kvb, yb) - drow_ref[rb, :1])).astype(bf16)
            acc_ref[...] += dot(ds, xb) + dot(p.astype(bf16), yb)
            dqt_ref[rb] += dot(kt_ref[...], ds)

        visit(cls_ref, kb, step)
        sums = acc_ref[...].reshape(WIDE, KBR, 2 * HD).astype(bf16)
        same_ref[:, cols, :] = sums[:CHIPS]
        other_ref[:, cols, :] = sums[CHIPS:]
        return 0

    lax.fori_loop(0, KB, key_block, 0)
    keep = lanes_low((RBR, 2 * HD))
    for rb in range(RB):
        dq = jnp.transpose(dqt_ref[rb]) * 0.125
        for h in range(0, H, 2):
            even = dq[h * RBR : (h + 1) * RBR, :]
            odd = dq[(h + 1) * RBR : (h + 2) * RBR, :]
            dq_ref[rb * RBR : (rb + 1) * RBR, h * HD : (h + 2) * HD] = jnp.where(
                keep, even, pltpu.roll(odd, HD, 1)
            ).astype(bf16)
    first = at_ref[0] == 0
    dq, gb = dq_ref[...], gb_ref[...]
    keep_ref[...] = jnp.where(first, dq, gb)
    send_ref[...] = jnp.where(first, gb, dq)


def put_rows(ref, at, row):
    for i in range(row.shape[1] // 128):
        ref[pl.ds(at + i, 1), :] = row[:, i * 128 : (i + 1) * 128]


def middle_kernel(at_ref, att_ref, x_ref, g_ref, wout_ref, bout_ref, gain_ref, bias_ref, wup_ref, bup_ref, wdown_ref, bdown_ref,
                  y_ref, bk_ref, bs_ref, sk_ref, ss_ref, gr_ref, gb_ref, ga_ref, vec_ref,
                  resid_ref, out_ref, gn2_ref, n2_ref):
    step = pl.program_id(0)
    first = at_ref[0] == 0

    @pl.when(step == 0)
    def _():
        resid = x_ref[...].astype(f32) + (dot(att_ref[...], wout_ref[...]) + vec(bout_ref))
        resid_ref[...] = resid
        n, _ = norm_parts(resid)
        n2 = (n * vec(gain_ref) + vec(bias_ref)).astype(bf16)
        n2_ref[...] = n2
        sk_ref[...] = jnp.where(first, g_ref[...], n2)
        ss_ref[...] = jnp.where(first, n2, g_ref[...])
        out_ref[...] = jnp.zeros_like(out_ref)
        gn2_ref[...] = jnp.zeros_like(gn2_ref)

    g = g_ref[...]
    pre = dot(n2_ref[...], wup_ref[...]) + vec(bup_ref)
    sq = pre * pre
    t = jnp.tanh(0.7978845608028654 * (pre + 0.044715 * sq * pre))
    half = 0.5 + 0.5 * t
    act = (pre * half).astype(bf16)
    slope = half + (0.5 * 0.7978845608028654) * pre * (1.0 - t * t) * (1.0 + (3 * 0.044715) * sq)
    gp = (slope * dot_nt(g, wdown_ref[...])).astype(bf16)
    bk_ref[...] = jnp.where(first, act, gp)
    bs_ref[...] = jnp.where(first, gp, act)
    put_rows(vec_ref, 24 + step * (FC // 128), jnp.sum(gp.astype(f32), axis=0, keepdims=True))
    out_ref[...] += dot(act, wdown_ref[...])
    gn2_ref[...] += dot_nt(gp, wup_ref[...])

    @pl.when(step == pl.num_programs(0) - 1)
    def _():
        resid = resid_ref[...]
        gf = g.astype(f32)
        y_ref[...] = (resid + (out_ref[...] + vec(bdown_ref))).astype(bf16)
        n, rstd = norm_parts(resid)
        e = gn2_ref[...]
        gr = gf + norm_back(e, n, rstd, vec(gain_ref))
        gr_ref[...] = gr
        gb = gr.astype(bf16)
        gb_ref[...] = gb
        ga_ref[...] = dot_nt(gb, wout_ref[...]).astype(bf16)
        put_rows(vec_ref, 0, jnp.sum(gf, axis=0, keepdims=True))
        put_rows(vec_ref, 6, jnp.sum(e * n, axis=0, keepdims=True))
        put_rows(vec_ref, 12, jnp.sum(e, axis=0, keepdims=True))
        put_rows(vec_ref, 18, jnp.sum(gb.astype(f32), axis=0, keepdims=True))


def leave_kernel(at_ref, x_ref, gain_ref, wq_ref, wkv_ref, gq_ref, gr_ref, mid_ref, parts_ref, _, gin_ref, keep_ref, send_ref, vec_ref):
    gkv = jnp.sum(parts_ref[...].astype(f32), axis=0).astype(bf16)
    gq = gq_ref[...]
    e = dot_nt(gq, wq_ref[...]) + dot_nt(gkv, wkv_ref[...])
    n, rstd = norm_parts(x_ref[...].astype(f32))
    gin = gr_ref[...] + norm_back(e, n, rstd, vec(gain_ref))
    for i in range(D // 128):
        gin_ref[pl.ds(i, ROWS, stride=D // 128), :] = gin[:, i * 128 : (i + 1) * 128]
    gkv = gkv.astype(f32)
    vec_ref[0:48, :] = mid_ref[...]
    vec_ref[48:128, :] = jnp.zeros((80, 128), f32)
    put_rows(vec_ref, 48, jnp.sum(e * n, axis=0, keepdims=True))
    put_rows(vec_ref, 54, jnp.sum(e, axis=0, keepdims=True))
    put_rows(vec_ref, 60, jnp.sum(gq.astype(f32), axis=0, keepdims=True))
    put_rows(vec_ref, 66, jnp.sum(gkv, axis=0, keepdims=True))
    first = at_ref[0] == 0
    vecs = vec_ref[...]
    keep_ref[...] = jnp.where(first, gkv, vecs)
    send_ref[...] = jnp.where(first, vecs, gkv)


def pack_kernel(bk_ref, sk_ref, bp_ref, sp_ref, out_ref):
    for i in range(4):
        cols = slice(i * D, (i + 1) * D)
        out_ref[i, 0:ROWS, 0:D] = bk_ref[:, cols]
        out_ref[i, ROWS:, 0:D] = bp_ref[:, cols]
        out_ref[i, 0:ROWS, D:] = sk_ref[...]
        out_ref[i, ROWS:, D:] = sp_ref[...]

def quarters(at, which, total_ref, outs):
    rows = total_ref.shape[0]//4
    for rel, out in zip((0,1,3,2), outs):
        out[...] = total_ref[pl.ds(pl.multiple_of(((at[which]+rel)&3)*rows, rows), rows), :].astype(out.dtype)

def weight_kernel(at_ref, slab_ref, own_ref, plus_ref, minus_ref, far_ref, total_ref):
    @pl.when(at_ref[0] == 0)
    def _():
        total_ref[...] = sum(dot_tn(slab_ref[i, :, :D], slab_ref[i, :, D:]) for i in range(4))

    @pl.when(at_ref[0] == 1)
    def _():
        total_ref[...] = sum(dot_tn(slab_ref[i, :, D:], slab_ref[i, :, :D]) for i in range(4))

    quarters(at_ref, 2, total_ref, (own_ref, plus_ref, minus_ref, far_ref))


def join_kernel(at_ref,a_ref,b_ref,c_ref,d_ref,out_ref):
    rows=a_ref.shape[0]
    for rel, v in zip(FROM,(a_ref,b_ref,c_ref,d_ref)):
        out_ref[pl.ds(pl.multiple_of(((at_ref[2]+rel)&3)*rows,rows),rows),:] = v[...]

def place_kernel(at_ref, own_ref, other_ref, *rest):
    down_ref, up_ref = rest[-2:]
    first = at_ref[0]==0
    own, other = own_ref[...], other_ref[...]
    down_ref[...] = jnp.where(first, own, other).astype(f32)
    up_ref[...] = jnp.where(first, other, own).astype(f32)

def place(at, rel, own, other, kept, part=0):
    tile = D // 2
    n = own.shape[0] // tile
    piece = pl.BlockSpec((tile, D), lambda i, at: (i, 0))
    outs = (
        pl.BlockSpec((tile, D), lambda i, at: (((at[4] + rel) & 3) * 2 + part + i, 0)),
        pl.BlockSpec((tile, D), lambda i, at: (part + i, (at[5] + rel) & 3)),
    )
    return pl.pallas_call(
        place_kernel,
        grid_spec=pltpu.PrefetchScalarGridSpec(
            num_scalar_prefetch=1, grid=(n,), in_specs=[piece, piece] + [ANY] * len(kept), out_specs=outs
        ),
        out_shape=shapes(((FF, D), f32), ((D, FF), f32)),
        input_output_aliases={3: 0, 4: 1} if kept else {},
        compiler_params=params(),
        cost_estimate=cost(0, 8e6),
        name="place",
    )(at, own, other, *kept)


def share_kernel(same_ref, other_ref, lk_ref, lo_ref, rk_ref, ro_ref, out_ref, total_ref):
    out_ref[:, 0:ROWS, :] = (same_ref[...].astype(f32) + other_ref[...].astype(f32)).astype(bf16)
    total_ref[...] = dot_tn(lk_ref[...], rk_ref[...]) + dot_tn(lo_ref[...], ro_ref[...])
    for i in range(CHIPS):
        for b in range(6):
            out_ref[i, ROWS + STRIP * b : ROWS + STRIP * (b + 1), :] = total_ref[
                STRIP * i : STRIP * (i + 1), 128 * b : 128 * (b + 1)
            ].astype(bf16)


def late_kernel(at_ref, lk_ref, lo_ref, tk_ref, to_ref, out_ref, total_ref):
    first = at_ref[0] == 0

    @pl.when(first)
    def _():
        total_ref[...] = dot_tn(lk_ref[...], tk_ref[...].astype(bf16)) + dot_tn(lo_ref[...], to_ref[...].astype(bf16))

    @pl.when(jnp.logical_not(first))
    def _():
        total_ref[0:128, :] = tk_ref[...] + to_ref[...]
        total_ref[128:, :] = jnp.zeros((D - 128, 128), f32)

    for i in range(CHIPS):
        out_ref[i] = total_ref[STRIP * i : STRIP * (i + 1), :].astype(bf16)


def strip_kernel(parts_ref, tail_ref, out_ref):
    for b in range(6):
        rows = slice(ROWS + STRIP * b, ROWS + STRIP * (b + 1))
        out_ref[:, 128 * b : 128 * (b + 1)] = jnp.sum(parts_ref[:, rows, :].astype(f32), axis=0).astype(bf16)
    out_ref[:, D:] = jnp.sum(tail_ref[...].astype(f32), axis=0).astype(bf16)


def part_kernel(a_ref, b_ref, c_ref, d_ref, out_ref):
    out_ref[...] = pair_sums(a_ref[...], b_ref[...], c_ref[...], d_ref[...])


def copies_kernel(a_ref, b_ref, c_ref, d_ref, out_ref):
    total = pair_sums(a_ref[...], b_ref[...], c_ref[...], d_ref[...])
    for i in range(CHIPS):
        out_ref[i] = total


VECTORS = ((0, 6), (6, 6), (12, 6), (18, 6), (24, 24), (48, 6), (54, 6), (60, 6))


def late_place_kernel(at_ref, own_ref, other_ref, query_ref, out_ref, kv_ref, value_ref, *vec_refs):
    first = at_ref[0] == 0
    vecs = []
    for a in range(CHIPS):
        rows = slice(STRIP * a, STRIP * (a + 1))
        own, other = own_ref[a].astype(f32), other_ref[a].astype(f32)
        zero, one = jnp.where(first, own, other), jnp.where(first, other, own)
        query_ref[rows, :] = zero[:, :D]
        out_ref[rows, :] = one[:, :D]
        kv_ref[rows, :] = zero[:, D:]
        if a < 2:
            vecs.append(one[:, D:])
    row = lambda i: vecs[i // STRIP][i % STRIP]
    value_ref[...] = row(66)[HD:]
    for ref, (at, count) in zip(vec_refs, VECTORS):
        for i in range(count):
            ref[i * 128 : (i + 1) * 128] = row(at + i)


def call(kernel, args, outs, scratch=(), name=None, flops=0, nbytes=2e6, after=()):
    given, extra = len(args), len(after)
    run = lambda *refs: kernel(*refs[:given], *refs[given + extra :])
    return pl.pallas_call(
        run,
        out_shape=outs,
        in_specs=[SMEM if v.dtype == jnp.int32 and v.ndim == 1 else VMEM for v in args] + [ANY] * extra,
        out_specs=jax.tree.map(lambda _: VMEM, outs),
        scratch_shapes=list(scratch),
        compiler_params=params(),
        cost_estimate=cost(flops, nbytes),
        name=name,
    )(*args, *after)


def shapes(*pairs):
    return tuple(jax.ShapeDtypeStruct(s, t) for s, t in pairs)


def positions(lengths, splits, wide_index, core):
    ends = jnp.cumsum(lengths, dtype=jnp.int32)
    starts = ends - lengths
    first = lengths * jnp.minimum(splits[:, 0], splits[:, 1]) // 1024
    second = lengths * jnp.maximum(splits[:, 0], splits[:, 1]) // 1024

    def place(row):
        shape = (1,) * row.ndim + (-1,)
        s, e, a, b, n = (v.reshape(shape) for v in (starts, ends, first, second, lengths))
        row = row[..., None]
        inside = (row >= s) & (row < e)
        u = row - s
        moved = jnp.where(u < a, u, jnp.where(u >= b, a + u - b, a + n - b + u - a))
        return (
            jnp.sum(jnp.where(inside, s + moved, 0), axis=-1, dtype=jnp.int32),
            jnp.sum(jnp.where(inside, s, 0), axis=-1, dtype=jnp.int32),
        )

    k = jnp.arange(KB, dtype=jnp.int32)[:, None, None]
    j = jnp.arange(CHIPS, dtype=jnp.int32) * 2
    j = jnp.concatenate([j + core, j + 1 - core])[None, :, None]
    r = jnp.arange(KBR, dtype=jnp.int32)[None, None, :]
    keys, _ = place(((k * KBR + r) * WIDE + j).reshape(KB, KEYS))
    own, own_start = place(jnp.arange(ROWS, dtype=jnp.int32) * WIDE + wide_index)
    low, high = jnp.min(keys, axis=1), jnp.max(keys, axis=1)
    blocks, block_starts = own.reshape(RB, RBR), own_start.reshape(RB, RBR)
    top, start_low = jnp.max(blocks, axis=1), jnp.min(block_starts, axis=1)
    bottom, start_high = jnp.min(blocks, axis=1), jnp.max(block_starts, axis=1)
    some = (low[None] <= top[:, None]) & (high[None] >= start_low[:, None])
    every = (high[None] <= bottom[:, None]) & (low[None] >= start_high[:, None])
    kinds = jnp.where(every, 2, jnp.where(some, 1, 0)).astype(jnp.int32).reshape(-1)
    return keys, own, own_start, kinds


NARROW = ((ROWS, D), bf16)
KV_HALF = ((CHIPS, ROWS, 2 * HD), bf16)


def attend(*args):
    stat = pltpu.VMEM((RB, 1, QB), f32)
    return call(
        forward_kernel, args,
        shapes(NARROW, NARROW, NARROW, ((RB, QB, 128), bf16), ((RB, QB, 128), f32), ((RB, 1, QB), f32), ((WIDE, ROWS, 2 * HD), bf16)),
        [stat, stat, pltpu.VMEM((RB, 2 * HD, QB), f32), pltpu.VMEM((2 * HD, KEYS), bf16)],
        name="attend", flops=4 * ROWS * H * WINDOW * 64, nbytes=4e6,
    )


def attend_back(*args, after=()):
    return call(
        backward_kernel, args,
        shapes(NARROW, NARROW, NARROW, KV_HALF, KV_HALF),
        [
            pltpu.VMEM((RB, QB, 128), bf16), pltpu.VMEM((RB, 8, QB), f32),
            pltpu.VMEM((RB, 128, QB), f32), pltpu.VMEM((KEYS, 2 * HD), f32), pltpu.VMEM((2 * HD, KEYS), bf16),
        ],
        name="attend_back", flops=10 * ROWS * H * WINDOW * 64, nbytes=8e6, after=after,
    )


def coords():
    x, y, z, c = (lax.axis_index(a) for a in AXES)
    first = c == 0
    at = (c, jnp.where(first, z, y), jnp.where(first, y, x), jnp.where(first, x, z), z, y)
    return jnp.stack(at).astype(jnp.int32)


def halves_kernel(before_ref, after_ref, low_ref, high_ref):
    low_ref[...] = before_ref[D // 2 :, :]
    high_ref[...] = after_ref[: D // 2, :]


QUARTER = ((D // 4, D), bf16)
HALF = ((D // 2, D), bf16)


def pair_sums(a, b, c, d):
    a, b, c, d = (v.astype(f32) for v in (a, b, c, d))
    return ((a + d) + (b + c)).astype(bf16)


def tie_kernel(v_ref, *refs):
    pass


def tie(v, *after):
    return pl.pallas_call(
        tie_kernel,
        out_shape=jax.ShapeDtypeStruct(v.shape, v.dtype),
        in_specs=[ANY] * (1 + len(after)),
        out_specs=ANY,
        input_output_aliases={0: 0},
        cost_estimate=cost(0, 0),
        name="tie",
    )(v, *after)


def feed_forward_spread(at, totals, before_join, beside):
    u = call(join_kernel, (at,) + totals, shapes(((D, D), bf16))[0], name="join", after=before_join)
    before, after = send(u, 0, 1), send(u, 0, 3)
    kept = place(at, 0, u, swap(u), ())
    marks = (swap(kept[0][:8, :128]),)
    low, high = call(halves_kernel, (before, after), shapes(HALF, HALF), name="halves", after=marks)
    before, after = tie(before, low), tie(after, low)
    low, high = send(low, 0, 1), send(high, 0, 3)
    kept = place(at, 3, before, swap(before), kept)
    kept = place(at, 1, after, swap(after), kept)
    low, high = (tie(v, kept[0], beside) for v in (low, high))
    kept = place(at, 2, high, swap(high), kept)
    return place(at, 2, low, swap(low), kept, part=1)


def body(block_input, file_lengths, file_splits, ln1_gain, ln1_bias, w_query, b_query, w_kv, b_value, w_out, b_out,
         ln2_gain, ln2_bias, w_up, b_up, w_down, b_down, out_cotangent):
    x = block_input.reshape(ROWS, D)
    g = out_cotangent.reshape(ROWS, D)
    wide = ("y", "z", "c")
    at = coords()
    narrow = NARROW

    n1, copies = call(enter_kernel, (x, ln1_gain, ln1_bias, w_kv, b_value), shapes(narrow, ((CHIPS, ROWS, 2 * HD), bf16)),
                      name="enter", flops=2 * ROWS * D * 128)
    kv_same = lax.all_to_all(copies, ("y", "z"), 0, 0, tiled=True)
    keys, own, own_start, kinds = positions(file_lengths[0], file_splits[0], lax.axis_index(wide), at[0])
    key_cols = jnp.broadcast_to(keys[:, :, None], (KB, KEYS, 128))
    own_lanes = jnp.tile(own.reshape(RB, 1, RBR), (1, 1, 128 // RBR))
    start_lanes = jnp.tile(own_start.reshape(RB, 1, RBR), (1, 1, 128 // RBR))
    q = call(query_kernel, (n1, w_query, b_query), shapes(narrow)[0], name="query", flops=2 * ROWS * D * D,
             after=(key_cols, own_lanes, start_lanes, kinds))
    kv_same = tie(kv_same, q)
    kv_other = swap(kv_same)

    att, left, left_send, xq, o, lse, kv_all = attend(at, kinds, q, kv_same, kv_other, key_cols, own_lanes, start_lanes, n1)
    left_other = swap(left_send)

    steps = FF // FC
    whole = lambda *s: pl.BlockSpec(s, lambda i: (0,) * len(s))
    wide_cols = pl.BlockSpec((ROWS, FC), lambda i: (0, i))
    y, big, big_send, small, small_send, gr, gb, ga, vec_mid = pl.pallas_call(
        middle_kernel,
        grid=(steps,),
        out_shape=shapes(narrow, ((ROWS, FF), bf16), ((ROWS, FF), bf16), narrow, narrow, ((ROWS, D), f32), narrow, narrow, ((48, 128), f32)),
        in_specs=[
            SMEM, whole(ROWS, D), whole(ROWS, D), whole(ROWS, D), whole(D, D), whole(D), whole(D), whole(D),
            pl.BlockSpec((D, FC), lambda i: (0, i)), pl.BlockSpec((FC,), lambda i: (i,)),
            pl.BlockSpec((FC, D), lambda i: (i, 0)), whole(D),
        ],
        out_specs=(
            whole(ROWS, D), wide_cols, wide_cols, whole(ROWS, D), whole(ROWS, D), whole(ROWS, D), whole(ROWS, D),
            whole(ROWS, D), whole(48, 128),
        ),
        scratch_shapes=[pltpu.VMEM((ROWS, D), f32)] * 3 + [pltpu.VMEM((ROWS, D), bf16)],
        compiler_params=params(),
        cost_estimate=cost(8 * ROWS * D * FF, 2e7),
        name="middle",
    )(at, att, x, g, w_out, b_out, ln2_gain, ln2_bias, w_up, b_up, w_down, b_down)

    packed = call(pack_kernel, (big, small, swap(big_send), swap(small_send)), shapes(((4, 2 * ROWS, 2 * D), bf16))[0], name="pack")
    slabs = lax.all_to_all(packed, AXES, 0, 0, axis_index_groups=ring_groups(0), tiled=True)

    gq, right, right_send, kv_grads, kv_send = attend_back(at, kinds, xq, ga, o, lse, kv_all, key_cols, own_lanes, start_lanes, gb, after=(packed,))
    shares = call(share_kernel, (kv_grads, swap(kv_send), left, left_other, right, swap(right_send)),
                  shapes(((CHIPS, ROWS + 6 * STRIP, 128), bf16))[0], [pltpu.VMEM((D, D), f32)], name="share", after=(slabs,))
    parts = lax.all_to_all(shares, ("y", "z"), 0, 0, tiled=True)

    pieces = call(weight_kernel, (at, slabs), shapes(*[QUARTER] * 4), [pltpu.VMEM((D, D), f32)], name="weights")
    ff_parts = (pieces[0],) + spread(1, *pieces[1:])
    gin, tail, tail_send, _ = pl.pallas_call(
        leave_kernel,
        grid=(1,),
        out_shape=shapes(((ROWS * D // 128, 128), f32), ((128, 128), f32), ((128, 128), f32), ((128, 128), f32)),
        in_specs=[SMEM] + [VMEM] * 7 + [pl.BlockSpec((CHIPS, ROWS, 128), lambda i: (0, 0, 0)), ANY],
        out_specs=(VMEM,) * 4,
        compiler_params=params(),
        cost_estimate=cost(2 * ROWS * D * 900, 4e6),
        name="leave",
    )(at, x, ln1_gain, w_query, w_kv, gq, gr, vec_mid, parts, pieces[0])

    late_parts = call(late_kernel, (at, left, left_other, tail, swap(tail_send)), shapes(((CHIPS, STRIP, 128), bf16))[0],
                      [pltpu.VMEM((D, 128), f32)], name="late", after=ff_parts[1:])
    ff_part = call(part_kernel, ff_parts, shapes(QUARTER)[0], name="part", after=(late_parts,))
    ff_crossed = gather4(ff_part, 2)
    late_parts = lax.all_to_all(late_parts, ("y", "z"), 0, 0, tiled=True)
    ff_totals = gather4(pair_sums(*ff_crossed), 1)
    strip = call(strip_kernel, (parts, late_parts), shapes(((STRIP, D + 128), bf16))[0], name="strip", after=ff_crossed[1:])
    strips = gather4(strip, 3)
    copies = call(copies_kernel, strips, shapes(((CHIPS, STRIP, D + 128), bf16))[0], name="copies", after=ff_totals[1:])
    late = lax.all_to_all(copies, ("y", "z"), 0, 0, tiled=True)
    one = lambda n: ((n,), f32)
    outs = call(
        late_place_kernel, (at, late, swap(late)),
        shapes(((D, D), f32), ((D, D), f32), ((D, 128), f32), one(HD), *[one(128 * n) for _, n in VECTORS]), name="late_place",
    )
    g_query, g_out, g_kv, g_value, g_bdown, g_gain2, g_bias2, g_bout, g_bup, g_gain1, g_bias1, g_bq = outs
    g_down, g_up = feed_forward_spread(at, ff_totals, (copies,), outs[2])
    shape = block_input.shape
    return (
        y.reshape(shape), gin.reshape(shape), g_gain1, g_bias1, g_query, g_bq, g_kv, g_value,
        g_out, g_bout, g_gain2, g_bias2, g_up, g_bup, g_down, g_bdown,
    )


def solution(mesh):
    split = P("x", None, ("y", "z", "c"), None)
    return jax.shard_map(
        body,
        mesh=Mesh(mesh.devices.reshape(4, 4, 4, 2), AXES),
        in_specs=(split, P("x", None), P("x", None, None)) + (P(),) * 14 + (split,),
        out_specs=(split, split) + (P(),) * 14,
        check_vma=False,
    )
```

```python
import itertools

import jax
import jax.numpy as jnp
from jax import lax
from jax.experimental import pallas as pl
from jax.experimental.pallas import tpu as pltpu
from jax.sharding import Mesh, PartitionSpec as P

EPS = 1e-05
MASKED = -1e30
ROWS = 128
WIDE = 32
CHIPS = 16
D = 768
H = 12
HD = 64
FF = 3072
WINDOW = ROWS * WIDE
RB = 2
RBR = ROWS // RB
QB = RBR * H
KB = 4
KBR = ROWS // KB
KEYS = WINDOW // KB
STRIP = D // CHIPS
FC = 1024
VMEM = pl.BlockSpec(memory_space=pltpu.VMEM)
SMEM = pl.BlockSpec(memory_space=pltpu.SMEM)
ANY = pl.BlockSpec(memory_space=pl.ANY)
f32 = jnp.float32
bf16 = jnp.bfloat16


def params(limit=56):
    return pltpu.CompilerParams(vmem_limit_bytes=limit * 1024 * 1024)


def cost(flops, nbytes):
    return pl.CostEstimate(flops=1, bytes_accessed=1, transcendentals=0)


def dot(a, b):
    return jnp.dot(a, b, preferred_element_type=f32)


def dot_nt(a, b):
    return lax.dot_general(a, b, (((1,), (1,)), ((), ())), preferred_element_type=f32)


def dot_tn(a, b):
    return lax.dot_general(a, b, (((0,), (0,)), ((), ())), preferred_element_type=f32)


def norm_parts(x):
    mean = jnp.mean(x, axis=-1, keepdims=True)
    centered = x - mean
    var = jnp.mean(centered * centered, axis=-1, keepdims=True)
    rstd = lax.rsqrt(var + EPS)
    return centered * rstd, rstd


def norm_back(e, n, rstd, gain):
    m = e * gain
    return rstd * (
        m - jnp.mean(m, axis=-1, keepdims=True) - n * jnp.mean(m * n, axis=-1, keepdims=True)
    )


AXES = ("x", "y", "z", "c")
ORDER = ((2, 1, 0, 0), (1, 0, 2, 0))
FROM = (0, 3, 1, 2)


def ring(place, shift):
    pairs = []
    for at in itertools.product(range(4), range(4), range(4), range(2)):
        to = list(at)
        axis = ORDER[at[3]][place]
        to[axis] = (to[axis] + shift) % 4
        index = lambda v: ((v[0] * 4 + v[1]) * 4 + v[2]) * 2 + v[3]
        pairs.append((index(at), index(to)))
    return pairs


def ring_groups(place):
    groups = {}
    for at in itertools.product(range(4), range(4), range(4), range(2)):
        key = list(at)
        key[ORDER[at[3]][place]] = -1
        groups.setdefault(tuple(key), []).append(((at[0] * 4 + at[1]) * 4 + at[2]) * 2 + at[3])
    return list(groups.values())


def send(v, place, shift):
    return lax.ppermute(v, AXES, ring(place, shift))


def swap(v):
    return lax.ppermute(v, "c", [(0, 1), (1, 0)])


def spread(place, plus, minus, far):
    return send(plus, place, 1), send(minus, place, 3), send(far, place, 2)


def gather4(v, place):
    return (v,) + spread(place, v, v, v)


def lanes_low(shape):
    return lax.broadcasted_iota(jnp.int32, shape, len(shape) - 1) < HD


def vec(ref):
    return ref[...].astype(f32).reshape(1, -1)


def enter_kernel(x_ref, gain_ref, bias_ref, wkv_ref, bv_ref, n1_ref, kv_ref):
    n, _ = norm_parts(x_ref[...].astype(f32))
    n1 = (n * vec(gain_ref) + vec(bias_ref)).astype(bf16)
    n1_ref[...] = n1
    shift = jnp.concatenate([jnp.zeros((1, HD), f32), vec(bv_ref)], axis=1)
    kv = (dot(n1, wkv_ref[...]) + shift).astype(bf16)
    for i in range(CHIPS):
        kv_ref[i] = kv


def query_kernel(n1_ref, wq_ref, bq_ref, q_ref):
    q_ref[...] = (dot(n1_ref[...], wq_ref[...]) + vec(bq_ref)).astype(bf16)


def block_bias(kp, sp, st):
    bias = jnp.where((kp <= sp) & (kp >= st), 0.0, MASKED)
    return jnp.concatenate([bias] * (QB // 128), axis=1)


def visit(cls_ref, kb, step):
    def row_block(rb, _):
        kind = cls_ref[rb * KB + kb]

        @pl.when(kind == 2)
        def _():
            step(rb, False)

        @pl.when(kind == 1)
        def _():
            step(rb, True)

        return 0

    lax.fori_loop(0, RB, row_block, 0)


def forward_kernel(at_ref, cls_ref, q_ref, same_ref, other_ref, kpb_ref, spl_ref, stl_ref, n1_ref,
                   att_ref, keep_ref, send_ref, x_ref, o_ref, lse_ref, kv_ref, m_ref, l_ref, acc_ref, kt_ref):
    kv_ref[:CHIPS] = same_ref[...]
    kv_ref[CHIPS:] = other_ref[...]
    low = lanes_low((ROWS, 2 * HD))
    for h in range(H):
        pair = q_ref[:, (h // 2) * 128 : (h // 2) * 128 + 128].astype(f32) * 0.125
        if h % 2:
            pair = pltpu.roll(pair, HD, 1)
        head = jnp.where(low, pair, 0.0).astype(bf16)
        for rb in range(RB):
            x_ref[rb, h * RBR : (h + 1) * RBR, :] = head[rb * RBR : (rb + 1) * RBR, :]
    m_ref[...] = jnp.full((RB, 1, QB), MASKED, f32)
    l_ref[...] = jnp.zeros((RB, 1, QB), f32)
    acc_ref[...] = jnp.zeros((RB, 2 * HD, QB), f32)

    def key_block(kb, _):
        cols = pl.ds(pl.multiple_of(kb * KBR, KBR), KBR)
        kt_ref[...] = jnp.transpose(kv_ref[:, cols, :].reshape(KEYS, 2 * HD).astype(f32)).astype(bf16)

        def step(rb, masked):
            s = dot_nt(kv_ref[:, cols, :].reshape(KEYS, 2 * HD), x_ref[rb])
            if masked:
                s = s + block_bias(kpb_ref[kb], spl_ref[rb], stl_ref[rb])
            m_old = m_ref[rb]
            m_new = jnp.maximum(m_old, jnp.max(s, axis=0, keepdims=True))
            alpha = jnp.exp(m_old - m_new)
            p = jnp.exp(s - m_new)
            l_ref[rb] = l_ref[rb] * alpha + jnp.sum(p, axis=0, keepdims=True)
            acc_ref[rb] = acc_ref[rb] * alpha + dot(kt_ref[...], p.astype(bf16))
            m_ref[rb] = m_new

        visit(cls_ref, kb, step)
        return 0

    lax.fori_loop(0, KB, key_block, 0)
    keep = lanes_low((RBR, 2 * HD))
    first = at_ref[0] == 0
    for rb in range(RB):
        rows = slice(rb * RBR, (rb + 1) * RBR)
        l = l_ref[rb]
        lse_ref[rb] = m_ref[rb] + jnp.log(l)
        out = jnp.transpose(acc_ref[rb] / l)
        o_ref[rb] = out
        for h in range(0, H, 2):
            even = out[h * RBR : (h + 1) * RBR, :]
            odd = out[(h + 1) * RBR : (h + 2) * RBR, :]
            att_ref[rows, h * HD : (h + 2) * HD] = jnp.where(keep, pltpu.roll(even, HD, 1), odd).astype(bf16)
    n1, att = n1_ref[...], att_ref[...]
    keep_ref[...] = jnp.where(first, n1, att)
    send_ref[...] = jnp.where(first, att, n1)


def backward_kernel(at_ref, cls_ref, x_ref, do_ref, o_ref, lse_ref, kv_ref, kpb_ref, spl_ref, stl_ref, gb_ref,
                    dq_ref, keep_ref, send_ref, same_ref, other_ref, y_ref, drow_ref, dqt_ref, acc_ref, kt_ref):
    low = lanes_low((ROWS, 2 * HD))
    for h in range(H):
        pair = do_ref[:, (h // 2) * 128 : (h // 2) * 128 + 128].astype(f32)
        if h % 2 == 0:
            pair = pltpu.roll(pair, HD, 1)
        head = jnp.where(low, 0.0, pair).astype(bf16)
        for rb in range(RB):
            y_ref[rb, h * RBR : (h + 1) * RBR, :] = head[rb * RBR : (rb + 1) * RBR, :]
    for rb in range(RB):
        delta = jnp.sum(y_ref[rb].astype(f32) * o_ref[rb], axis=1, keepdims=True)
        drow_ref[rb] = jnp.transpose(jnp.broadcast_to(delta, (QB, 128)))[:8]
    dqt_ref[...] = jnp.zeros((RB, 128, QB), f32)

    def key_block(kb, _):
        cols = pl.ds(pl.multiple_of(kb * KBR, KBR), KBR)
        kvb = kv_ref[:, cols, :].reshape(KEYS, 2 * HD)
        kt_ref[...] = jnp.transpose(kvb.astype(f32)).astype(bf16)
        acc_ref[...] = jnp.zeros((KEYS, 2 * HD), f32)

        def step(rb, masked):
            kvb = kv_ref[:, cols, :].reshape(KEYS, 2 * HD)
            xb, yb = x_ref[rb], y_ref[rb]
            s = dot_nt(kvb, xb)
            if masked:
                s = s + block_bias(kpb_ref[kb], spl_ref[rb], stl_ref[rb])
            p = jnp.exp(s - lse_ref[rb])
            ds = (p * (dot_nt(kvb, yb) - drow_ref[rb, :1])).astype(bf16)
            acc_ref[...] += dot(ds, xb) + dot(p.astype(bf16), yb)
            dqt_ref[rb] += dot(kt_ref[...], ds)

        visit(cls_ref, kb, step)
        sums = acc_ref[...].reshape(WIDE, KBR, 2 * HD).astype(bf16)
        same_ref[:, cols, :] = sums[:CHIPS]
        other_ref[:, cols, :] = sums[CHIPS:]
        return 0

    lax.fori_loop(0, KB, key_block, 0)
    keep = lanes_low((RBR, 2 * HD))
    for rb in range(RB):
        dq = jnp.transpose(dqt_ref[rb]) * 0.125
        for h in range(0, H, 2):
            even = dq[h * RBR : (h + 1) * RBR, :]
            odd = dq[(h + 1) * RBR : (h + 2) * RBR, :]
            dq_ref[rb * RBR : (rb + 1) * RBR, h * HD : (h + 2) * HD] = jnp.where(
                keep, even, pltpu.roll(odd, HD, 1)
            ).astype(bf16)
    first = at_ref[0] == 0
    dq, gb = dq_ref[...], gb_ref[...]
    keep_ref[...] = jnp.where(first, dq, gb)
    send_ref[...] = jnp.where(first, gb, dq)


def put_rows(ref, at, row):
    for i in range(row.shape[1] // 128):
        ref[pl.ds(at + i, 1), :] = row[:, i * 128 : (i + 1) * 128]


def middle_kernel(at_ref, att_ref, x_ref, g_ref, wout_ref, bout_ref, gain_ref, bias_ref, wup_ref, bup_ref, wdown_ref, bdown_ref,
                  y_ref, bk_ref, bs_ref, sk_ref, ss_ref, gr_ref, gb_ref, ga_ref, vec_ref,
                  resid_ref, out_ref, gn2_ref, n2_ref):
    step = pl.program_id(0)
    first = at_ref[0] == 0

    @pl.when(step == 0)
    def _():
        resid = x_ref[...].astype(f32) + (dot(att_ref[...], wout_ref[...]) + vec(bout_ref))
        resid_ref[...] = resid
        n, _ = norm_parts(resid)
        n2 = (n * vec(gain_ref) + vec(bias_ref)).astype(bf16)
        n2_ref[...] = n2
        sk_ref[...] = jnp.where(first, g_ref[...], n2)
        ss_ref[...] = jnp.where(first, n2, g_ref[...])
        out_ref[...] = jnp.zeros_like(out_ref)
        gn2_ref[...] = jnp.zeros_like(gn2_ref)

    g = g_ref[...]
    pre = dot(n2_ref[...], wup_ref[...]) + vec(bup_ref)
    sq = pre * pre
    t = jnp.tanh(0.7978845608028654 * (pre + 0.044715 * sq * pre))
    half = 0.5 + 0.5 * t
    act = (pre * half).astype(bf16)
    slope = half + (0.5 * 0.7978845608028654) * pre * (1.0 - t * t) * (1.0 + (3 * 0.044715) * sq)
    gp = (slope * dot_nt(g, wdown_ref[...])).astype(bf16)
    bk_ref[...] = jnp.where(first, act, gp)
    bs_ref[...] = jnp.where(first, gp, act)
    put_rows(vec_ref, 24 + step * (FC // 128), jnp.sum(gp.astype(f32), axis=0, keepdims=True))
    out_ref[...] += dot(act, wdown_ref[...])
    gn2_ref[...] += dot_nt(gp, wup_ref[...])

    @pl.when(step == pl.num_programs(0) - 1)
    def _():
        resid = resid_ref[...]
        gf = g.astype(f32)
        y_ref[...] = (resid + (out_ref[...] + vec(bdown_ref))).astype(bf16)
        n, rstd = norm_parts(resid)
        e = gn2_ref[...]
        gr = gf + norm_back(e, n, rstd, vec(gain_ref))
        gr_ref[...] = gr
        gb = gr.astype(bf16)
        gb_ref[...] = gb
        ga_ref[...] = dot_nt(gb, wout_ref[...]).astype(bf16)
        put_rows(vec_ref, 0, jnp.sum(gf, axis=0, keepdims=True))
        put_rows(vec_ref, 6, jnp.sum(e * n, axis=0, keepdims=True))
        put_rows(vec_ref, 12, jnp.sum(e, axis=0, keepdims=True))
        put_rows(vec_ref, 18, jnp.sum(gb.astype(f32), axis=0, keepdims=True))


def leave_kernel(at_ref, x_ref, gain_ref, wq_ref, wkv_ref, gq_ref, gr_ref, mid_ref, parts_ref, gin_ref, keep_ref, send_ref, vec_ref):
    gkv = jnp.sum(parts_ref[...].astype(f32), axis=0).astype(bf16)
    gq = gq_ref[...]
    e = dot_nt(gq, wq_ref[...]) + dot_nt(gkv, wkv_ref[...])
    n, rstd = norm_parts(x_ref[...].astype(f32))
    gin = gr_ref[...] + norm_back(e, n, rstd, vec(gain_ref))
    for i in range(D // 128):
        gin_ref[pl.ds(i, ROWS, stride=D // 128), :] = gin[:, i * 128 : (i + 1) * 128]
    gkv = gkv.astype(f32)
    vec_ref[0:48, :] = mid_ref[...]
    vec_ref[48:128, :] = jnp.zeros((80, 128), f32)
    put_rows(vec_ref, 48, jnp.sum(e * n, axis=0, keepdims=True))
    put_rows(vec_ref, 54, jnp.sum(e, axis=0, keepdims=True))
    put_rows(vec_ref, 60, jnp.sum(gq.astype(f32), axis=0, keepdims=True))
    put_rows(vec_ref, 66, jnp.sum(gkv, axis=0, keepdims=True))
    first = at_ref[0] == 0
    vecs = vec_ref[...]
    keep_ref[...] = jnp.where(first, gkv, vecs)
    send_ref[...] = jnp.where(first, vecs, gkv)


def pack_kernel(bk_ref, sk_ref, bp_ref, sp_ref, out_ref):
    for i in range(4):
        cols = slice(i * D, (i + 1) * D)
        out_ref[i, 0:ROWS, 0:D] = bk_ref[:, cols]
        out_ref[i, ROWS:, 0:D] = bp_ref[:, cols]
        out_ref[i, 0:ROWS, D:] = sk_ref[...]
        out_ref[i, ROWS:, D:] = sp_ref[...]

def quarters(at, which, total_ref, outs):
    rows = total_ref.shape[0]//4
    for rel, out in zip((0,1,3,2), outs):
        out[...] = total_ref[pl.ds(pl.multiple_of(((at[which]+rel)&3)*rows, rows), rows), :].astype(out.dtype)

def weight_kernel(at_ref, slab_ref, own_ref, plus_ref, minus_ref, far_ref, total_ref):
    @pl.when(at_ref[0] == 0)
    def _():
        total_ref[...] = sum(dot_tn(slab_ref[i, :, :D], slab_ref[i, :, D:]) for i in range(4))

    @pl.when(at_ref[0] == 1)
    def _():
        total_ref[...] = sum(dot_tn(slab_ref[i, :, D:], slab_ref[i, :, :D]) for i in range(4))

    quarters(at_ref, 2, total_ref, (own_ref, plus_ref, minus_ref, far_ref))


def join_kernel(at_ref,a_ref,b_ref,c_ref,d_ref,out_ref):
    rows=a_ref.shape[0]
    for rel, v in zip(FROM,(a_ref,b_ref,c_ref,d_ref)):
        out_ref[pl.ds(pl.multiple_of(((at_ref[2]+rel)&3)*rows,rows),rows),:] = v[...]

def place_kernel(at_ref, own_ref, other_ref, *rest):
    down_ref, up_ref = rest[-2:]
    first = at_ref[0]==0
    own, other = own_ref[...], other_ref[...]
    down_ref[...] = jnp.where(first, own, other).astype(f32)
    up_ref[...] = jnp.where(first, other, own).astype(f32)

def place(at, rel, own, other, kept, part=0):
    tile = D // 2
    n = own.shape[0] // tile
    piece = pl.BlockSpec((tile, D), lambda i, at: (i, 0))
    outs = (
        pl.BlockSpec((tile, D), lambda i, at: (((at[4] + rel) & 3) * 2 + part + i, 0)),
        pl.BlockSpec((tile, D), lambda i, at: (part + i, (at[5] + rel) & 3)),
    )
    return pl.pallas_call(
        place_kernel,
        grid_spec=pltpu.PrefetchScalarGridSpec(
            num_scalar_prefetch=1, grid=(n,), in_specs=[piece, piece] + [ANY] * len(kept), out_specs=outs
        ),
        out_shape=shapes(((FF, D), f32), ((D, FF), f32)),
        input_output_aliases={3: 0, 4: 1} if kept else {},
        compiler_params=params(),
        cost_estimate=cost(0, 8e6),
        name="place",
    )(at, own, other, *kept)


def share_kernel(same_ref, other_ref, out_ref):
    out_ref[...] = (same_ref[...].astype(f32) + other_ref[...].astype(f32)).astype(bf16)


def square_kernel(lk_ref, lo_ref, rk_ref, ro_ref, out_ref):
    out_ref[...] = (dot_tn(lk_ref[...], rk_ref[...]) + dot_tn(lo_ref[...], ro_ref[...])).astype(bf16)


def late_kernel(at_ref, lk_ref, lo_ref, tk_ref, to_ref, square_ref, out_ref, total_ref):
    first = at_ref[0] == 0

    @pl.when(first)
    def _():
        total_ref[...] = dot_tn(lk_ref[...], tk_ref[...].astype(bf16)) + dot_tn(lo_ref[...], to_ref[...].astype(bf16))

    @pl.when(jnp.logical_not(first))
    def _():
        total_ref[0:128, :] = tk_ref[...] + to_ref[...]
        total_ref[128:, :] = jnp.zeros((D - 128, 128), f32)

    for i in range(CHIPS):
        rows = slice(STRIP * i, STRIP * (i + 1))
        out_ref[i, :, :D] = square_ref[rows, :]
        out_ref[i, :, D:] = total_ref[rows, :].astype(bf16)


def strip_kernel(parts_ref, out_ref):
    out_ref[...] = jnp.sum(parts_ref[...].astype(f32), axis=0).astype(bf16)


def part_kernel(a_ref, b_ref, c_ref, d_ref, out_ref):
    out_ref[...] = pair_sums(a_ref[...], b_ref[...], c_ref[...], d_ref[...])


def copies_kernel(a_ref, b_ref, c_ref, d_ref, out_ref):
    total = pair_sums(a_ref[...], b_ref[...], c_ref[...], d_ref[...])
    for i in range(CHIPS):
        out_ref[i] = total


VECTORS = ((0, 6), (6, 6), (12, 6), (18, 6), (24, 24), (48, 6), (54, 6), (60, 6))


def late_place_kernel(at_ref, own_ref, other_ref, query_ref, out_ref, kv_ref, value_ref, *vec_refs):
    first = at_ref[0] == 0
    vecs = []
    for a in range(CHIPS):
        rows = slice(STRIP * a, STRIP * (a + 1))
        own, other = own_ref[a].astype(f32), other_ref[a].astype(f32)
        zero, one = jnp.where(first, own, other), jnp.where(first, other, own)
        query_ref[rows, :] = zero[:, :D]
        out_ref[rows, :] = one[:, :D]
        kv_ref[rows, :] = zero[:, D:]
        if a < 2:
            vecs.append(one[:, D:])
    row = lambda i: vecs[i // STRIP][i % STRIP]
    value_ref[...] = row(66)[HD:]
    for ref, (at, count) in zip(vec_refs, VECTORS):
        for i in range(count):
            ref[i * 128 : (i + 1) * 128] = row(at + i)


def call(kernel, args, outs, scratch=(), name=None, flops=0, nbytes=2e6, after=()):
    given, extra = len(args), len(after)
    run = lambda *refs: kernel(*refs[:given], *refs[given + extra :])
    return pl.pallas_call(
        run,
        out_shape=outs,
        in_specs=[SMEM if v.dtype == jnp.int32 and v.ndim == 1 else VMEM for v in args] + [ANY] * extra,
        out_specs=jax.tree.map(lambda _: VMEM, outs),
        scratch_shapes=list(scratch),
        compiler_params=params(),
        cost_estimate=cost(flops, nbytes),
        name=name,
    )(*args, *after)


def shapes(*pairs):
    return tuple(jax.ShapeDtypeStruct(s, t) for s, t in pairs)


def positions(lengths, splits, wide_index, core):
    ends = jnp.cumsum(lengths, dtype=jnp.int32)
    starts = ends - lengths
    first = lengths * jnp.minimum(splits[:, 0], splits[:, 1]) // 1024
    second = lengths * jnp.maximum(splits[:, 0], splits[:, 1]) // 1024

    def place(row):
        shape = (1,) * row.ndim + (-1,)
        s, e, a, b, n = (v.reshape(shape) for v in (starts, ends, first, second, lengths))
        row = row[..., None]
        inside = (row >= s) & (row < e)
        u = row - s
        moved = jnp.where(u < a, u, jnp.where(u >= b, a + u - b, a + n - b + u - a))
        return (
            jnp.sum(jnp.where(inside, s + moved, 0), axis=-1, dtype=jnp.int32),
            jnp.sum(jnp.where(inside, s, 0), axis=-1, dtype=jnp.int32),
        )

    k = jnp.arange(KB, dtype=jnp.int32)[:, None, None]
    j = jnp.arange(CHIPS, dtype=jnp.int32) * 2
    j = jnp.concatenate([j + core, j + 1 - core])[None, :, None]
    r = jnp.arange(KBR, dtype=jnp.int32)[None, None, :]
    keys, _ = place(((k * KBR + r) * WIDE + j).reshape(KB, KEYS))
    own, own_start = place(jnp.arange(ROWS, dtype=jnp.int32) * WIDE + wide_index)
    low, high = jnp.min(keys, axis=1), jnp.max(keys, axis=1)
    blocks, block_starts = own.reshape(RB, RBR), own_start.reshape(RB, RBR)
    top, start_low = jnp.max(blocks, axis=1), jnp.min(block_starts, axis=1)
    bottom, start_high = jnp.min(blocks, axis=1), jnp.max(block_starts, axis=1)
    some = (low[None] <= top[:, None]) & (high[None] >= start_low[:, None])
    every = (high[None] <= bottom[:, None]) & (low[None] >= start_high[:, None])
    kinds = jnp.where(every, 2, jnp.where(some, 1, 0)).astype(jnp.int32).reshape(-1)
    return keys, own, own_start, kinds


NARROW = ((ROWS, D), bf16)
KV_HALF = ((CHIPS, ROWS, 2 * HD), bf16)


def attend(*args):
    stat = pltpu.VMEM((RB, 1, QB), f32)
    return call(
        forward_kernel, args,
        shapes(NARROW, NARROW, NARROW, ((RB, QB, 128), bf16), ((RB, QB, 128), f32), ((RB, 1, QB), f32), ((WIDE, ROWS, 2 * HD), bf16)),
        [stat, stat, pltpu.VMEM((RB, 2 * HD, QB), f32), pltpu.VMEM((2 * HD, KEYS), bf16)],
        name="attend", flops=4 * ROWS * H * WINDOW * 64, nbytes=4e6,
    )


def attend_back(*args, after=()):
    return call(
        backward_kernel, args,
        shapes(NARROW, NARROW, NARROW, KV_HALF, KV_HALF),
        [
            pltpu.VMEM((RB, QB, 128), bf16), pltpu.VMEM((RB, 8, QB), f32),
            pltpu.VMEM((RB, 128, QB), f32), pltpu.VMEM((KEYS, 2 * HD), f32), pltpu.VMEM((2 * HD, KEYS), bf16),
        ],
        name="attend_back", flops=10 * ROWS * H * WINDOW * 64, nbytes=8e6, after=after,
    )


def coords():
    x, y, z, c = (lax.axis_index(a) for a in AXES)
    first = c == 0
    at = (c, jnp.where(first, z, y), jnp.where(first, y, x), jnp.where(first, x, z), z, y)
    return jnp.stack(at).astype(jnp.int32)


def halves_kernel(before_ref, after_ref, low_ref, high_ref):
    low_ref[...] = before_ref[D // 2 :, :]
    high_ref[...] = after_ref[: D // 2, :]


QUARTER = ((D // 4, D), bf16)
HALF = ((D // 2, D), bf16)


def pair_sums(a, b, c, d):
    a, b, c, d = (v.astype(f32) for v in (a, b, c, d))
    return ((a + d) + (b + c)).astype(bf16)


def tie_kernel(v_ref, *refs):
    pass


def tie(v, *after):
    return pl.pallas_call(
        tie_kernel,
        out_shape=jax.ShapeDtypeStruct(v.shape, v.dtype),
        in_specs=[ANY] * (1 + len(after)),
        out_specs=ANY,
        input_output_aliases={0: 0},
        cost_estimate=cost(0, 0),
        name="tie",
    )(v, *after)


def feed_forward_spread(at, u):
    before, after = send(u, 0, 1), send(u, 0, 3)
    kept = place(at, 0, u, swap(u), ())
    return before, after, kept, swap(kept[0][:8, :128])


def feed_forward_rest(at, before, after, kept, mark, beside):
    low, high = call(halves_kernel, (before, after), shapes(HALF, HALF), name="halves", after=(mark,))
    before, after = tie(before, low), tie(after, high)
    low, high = send(low, 0, 1), send(high, 0, 3)
    kept = place(at, 3, before, swap(before), kept)
    kept = place(at, 1, after, swap(after), kept)
    low, high = (tie(v, kept[0], beside) for v in (low, high))
    kept = place(at, 2, high, swap(high), kept)
    return place(at, 2, low, swap(low), kept, part=1)


def body(block_input, file_lengths, file_splits, ln1_gain, ln1_bias, w_query, b_query, w_kv, b_value, w_out, b_out,
         ln2_gain, ln2_bias, w_up, b_up, w_down, b_down, out_cotangent):
    x = block_input.reshape(ROWS, D)
    g = out_cotangent.reshape(ROWS, D)
    wide = ("y", "z", "c")
    at = coords()
    narrow = NARROW

    n1, copies = call(enter_kernel, (x, ln1_gain, ln1_bias, w_kv, b_value), shapes(narrow, ((CHIPS, ROWS, 2 * HD), bf16)),
                      name="enter", flops=2 * ROWS * D * 128)
    kv_same = lax.all_to_all(copies, ("y", "z"), 0, 0, tiled=True)
    keys, own, own_start, kinds = positions(file_lengths[0], file_splits[0], lax.axis_index(wide), at[0])
    key_cols = jnp.broadcast_to(keys[:, :, None], (KB, KEYS, 128))
    own_lanes = jnp.tile(own.reshape(RB, 1, RBR), (1, 1, 128 // RBR))
    start_lanes = jnp.tile(own_start.reshape(RB, 1, RBR), (1, 1, 128 // RBR))
    q = call(query_kernel, (n1, w_query, b_query), shapes(narrow)[0], name="query", flops=2 * ROWS * D * D,
             after=(key_cols, own_lanes, start_lanes, kinds))
    kv_same = tie(kv_same, q)
    kv_other = swap(kv_same)

    att, left, left_send, xq, o, lse, kv_all = attend(at, kinds, q, kv_same, kv_other, key_cols, own_lanes, start_lanes, n1)
    left_other = swap(left_send)

    steps = FF // FC
    whole = lambda *s: pl.BlockSpec(s, lambda i: (0,) * len(s))
    wide_cols = pl.BlockSpec((ROWS, FC), lambda i: (0, i))
    y, big, big_send, small, small_send, gr, gb, ga, vec_mid = pl.pallas_call(
        middle_kernel,
        grid=(steps,),
        out_shape=shapes(narrow, ((ROWS, FF), bf16), ((ROWS, FF), bf16), narrow, narrow, ((ROWS, D), f32), narrow, narrow, ((48, 128), f32)),
        in_specs=[
            SMEM, whole(ROWS, D), whole(ROWS, D), whole(ROWS, D), whole(D, D), whole(D), whole(D), whole(D),
            pl.BlockSpec((D, FC), lambda i: (0, i)), pl.BlockSpec((FC,), lambda i: (i,)),
            pl.BlockSpec((FC, D), lambda i: (i, 0)), whole(D),
        ],
        out_specs=(
            whole(ROWS, D), wide_cols, wide_cols, whole(ROWS, D), whole(ROWS, D), whole(ROWS, D), whole(ROWS, D),
            whole(ROWS, D), whole(48, 128),
        ),
        scratch_shapes=[pltpu.VMEM((ROWS, D), f32)] * 3 + [pltpu.VMEM((ROWS, D), bf16)],
        compiler_params=params(),
        cost_estimate=cost(8 * ROWS * D * FF, 2e7),
        name="middle",
    )(at, att, x, g, w_out, b_out, ln2_gain, ln2_bias, w_up, b_up, w_down, b_down)

    packed = call(pack_kernel, (big, small, swap(big_send), swap(small_send)), shapes(((4, 2 * ROWS, 2 * D), bf16))[0], name="pack")
    slabs = lax.all_to_all(packed, AXES, 0, 0, axis_index_groups=ring_groups(0), tiled=True)

    gq, right, right_send, kv_grads, kv_send = attend_back(at, kinds, xq, ga, o, lse, kv_all, key_cols, own_lanes, start_lanes, gb, after=(packed,))
    shares = call(share_kernel, (kv_grads, swap(kv_send)), shapes(KV_HALF)[0], name="share", after=(slabs,))
    parts = lax.all_to_all(shares, ("y", "z"), 0, 0, tiled=True)

    pieces = call(weight_kernel, (at, slabs), shapes(*[QUARTER] * 4), [pltpu.VMEM((D, D), f32)], name="weights")
    ff_parts = (pieces[0],) + spread(1, *pieces[1:])
    square = call(square_kernel, (left, left_other, right, swap(right_send)), shapes(((D, D), bf16))[0], name="square")
    gin, tail, tail_send, _ = call(
        leave_kernel, (at, x, ln1_gain, w_query, w_kv, gq, gr, vec_mid, parts),
        shapes(((ROWS * D // 128, 128), f32), ((128, 128), f32), ((128, 128), f32), ((128, 128), f32)),
        name="leave", after=(pieces[0], square),
    )

    shares = call(late_kernel, (at, left, left_other, tail, swap(tail_send), square), shapes(((CHIPS, STRIP, D + 128), bf16))[0],
                  [pltpu.VMEM((D, 128), f32)], name="late", after=ff_parts[1:])
    ff_part = call(part_kernel, ff_parts, shapes(QUARTER)[0], name="part", after=(shares,))
    ff_crossed = gather4(ff_part, 2)
    late_parts = lax.all_to_all(shares, ("y", "z"), 0, 0, tiled=True)
    ff_totals = gather4(pair_sums(*ff_crossed), 1)
    strip = call(strip_kernel, (late_parts,), shapes(((STRIP, D + 128), bf16))[0], name="strip", after=ff_crossed[1:])
    u = call(join_kernel, (at,) + ff_totals, shapes(((D, D), bf16))[0], name="join")
    copies = call(copies_kernel, gather4(strip, 3), shapes(((CHIPS, STRIP, D + 128), bf16))[0], name="copies", after=(u,))
    spreading = feed_forward_spread(at, u)
    late = tie(lax.all_to_all(copies, ("y", "z"), 0, 0, tiled=True), spreading[-1])
    one = lambda n: ((n,), f32)
    outs = call(
        late_place_kernel, (at, late, swap(late)),
        shapes(((D, D), f32), ((D, D), f32), ((D, 128), f32), one(HD), *[one(128 * n) for _, n in VECTORS]), name="late_place",
    )
    g_query, g_out, g_kv, g_value, g_bdown, g_gain2, g_bias2, g_bout, g_bup, g_gain1, g_bias1, g_bq = outs
    g_down, g_up = feed_forward_rest(at, *spreading, outs[2])
    shape = block_input.shape
    return (
        y.reshape(shape), gin.reshape(shape), g_gain1, g_bias1, g_query, g_bq, g_kv, g_value,
        g_out, g_bout, g_gain2, g_bias2, g_up, g_bup, g_down, g_bdown,
    )


def solution(mesh):
    split = P("x", None, ("y", "z", "c"), None)
    return jax.shard_map(
        body,
        mesh=Mesh(mesh.devices.reshape(4, 4, 4, 2), AXES),
        in_specs=(split, P("x", None), P("x", None, None)) + (P(),) * 14 + (split,),
        out_specs=(split, split) + (P(),) * 14,
        check_vma=False,
    )
```

```python
import itertools

import jax
import jax.numpy as jnp
from jax import lax
from jax.experimental import pallas as pl
from jax.experimental.pallas import tpu as pltpu
from jax.sharding import Mesh, PartitionSpec as P

EPS = 1e-05
MASKED = -1e30
ROWS = 128
WIDE = 32
CHIPS = 16
D = 768
H = 12
HD = 64
FF = 3072
WINDOW = ROWS * WIDE
RB = 2
RBR = ROWS // RB
QB = RBR * H
KB = 4
KBR = ROWS // KB
KEYS = WINDOW // KB
STRIP = D // CHIPS
FC = 1024
VMEM = pl.BlockSpec(memory_space=pltpu.VMEM)
SMEM = pl.BlockSpec(memory_space=pltpu.SMEM)
ANY = pl.BlockSpec(memory_space=pl.ANY)
f32 = jnp.float32
bf16 = jnp.bfloat16


def params(limit=56):
    return pltpu.CompilerParams(vmem_limit_bytes=limit * 1024 * 1024)


def cost(flops, nbytes):
    return pl.CostEstimate(flops=1, bytes_accessed=1, transcendentals=0)


def dot(a, b):
    return jnp.dot(a, b, preferred_element_type=f32)


def dot_nt(a, b):
    return lax.dot_general(a, b, (((1,), (1,)), ((), ())), preferred_element_type=f32)


def dot_tn(a, b):
    return lax.dot_general(a, b, (((0,), (0,)), ((), ())), preferred_element_type=f32)


def norm_parts(x):
    mean = jnp.mean(x, axis=-1, keepdims=True)
    centered = x - mean
    var = jnp.mean(centered * centered, axis=-1, keepdims=True)
    rstd = lax.rsqrt(var + EPS)
    return centered * rstd, rstd


def norm_back(e, n, rstd, gain):
    m = e * gain
    return rstd * (
        m - jnp.mean(m, axis=-1, keepdims=True) - n * jnp.mean(m * n, axis=-1, keepdims=True)
    )


AXES = ("x", "y", "z", "c")
ORDER = ((2, 1, 0, 0), (1, 0, 2, 0))
FROM = (0, 3, 1, 2)


def ring(place, shift):
    pairs = []
    for at in itertools.product(range(4), range(4), range(4), range(2)):
        to = list(at)
        axis = ORDER[at[3]][place]
        to[axis] = (to[axis] + shift) % 4
        index = lambda v: ((v[0] * 4 + v[1]) * 4 + v[2]) * 2 + v[3]
        pairs.append((index(at), index(to)))
    return pairs


def ring_groups(place):
    groups = {}
    for at in itertools.product(range(4), range(4), range(4), range(2)):
        key = list(at)
        key[ORDER[at[3]][place]] = -1
        groups.setdefault(tuple(key), []).append(((at[0] * 4 + at[1]) * 4 + at[2]) * 2 + at[3])
    return list(groups.values())


def send(v, place, shift):
    return lax.ppermute(v, AXES, ring(place, shift))


def swap(v):
    return lax.ppermute(v, "c", [(0, 1), (1, 0)])


def spread(place, plus, minus, far):
    return send(plus, place, 1), send(minus, place, 3), send(far, place, 2)


def gather4(v, place):
    return (v,) + spread(place, v, v, v)


def lanes_low(shape):
    return lax.broadcasted_iota(jnp.int32, shape, len(shape) - 1) < HD


def vec(ref):
    return ref[...].astype(f32).reshape(1, -1)


def enter_kernel(x_ref, gain_ref, bias_ref, wkv_ref, bv_ref, n1_ref, kv_ref):
    n, _ = norm_parts(x_ref[...].astype(f32))
    n1 = (n * vec(gain_ref) + vec(bias_ref)).astype(bf16)
    n1_ref[...] = n1
    shift = jnp.concatenate([jnp.zeros((1, HD), f32), vec(bv_ref)], axis=1)
    kv = (dot(n1, wkv_ref[...]) + shift).astype(bf16)
    for i in range(CHIPS):
        kv_ref[i] = kv


def query_kernel(n1_ref, wq_ref, bq_ref, q_ref):
    q_ref[...] = (dot(n1_ref[...], wq_ref[...]) + vec(bq_ref)).astype(bf16)


def block_bias(kp, sp, st):
    bias = jnp.where((kp <= sp) & (kp >= st), 0.0, MASKED)
    return jnp.concatenate([bias] * (QB // 128), axis=1)


def visit(cls_ref, kb, step):
    def row_block(rb, _):
        kind = cls_ref[rb * KB + kb]

        @pl.when(kind == 2)
        def _():
            step(rb, False)

        @pl.when(kind == 1)
        def _():
            step(rb, True)

        return 0

    lax.fori_loop(0, RB, row_block, 0)


def forward_kernel(at_ref, cls_ref, q_ref, same_ref, other_ref, kpb_ref, spl_ref, stl_ref, n1_ref,
                   att_ref, keep_ref, send_ref, x_ref, o_ref, lse_ref, kv_ref, m_ref, l_ref, acc_ref, kt_ref):
    kv_ref[:CHIPS] = same_ref[...]
    kv_ref[CHIPS:] = other_ref[...]
    low = lanes_low((ROWS, 2 * HD))
    for h in range(H):
        pair = q_ref[:, (h // 2) * 128 : (h // 2) * 128 + 128].astype(f32) * 0.125
        if h % 2:
            pair = pltpu.roll(pair, HD, 1)
        head = jnp.where(low, pair, 0.0).astype(bf16)
        for rb in range(RB):
            x_ref[rb, h * RBR : (h + 1) * RBR, :] = head[rb * RBR : (rb + 1) * RBR, :]
    m_ref[...] = jnp.full((RB, 1, QB), MASKED, f32)
    l_ref[...] = jnp.zeros((RB, 1, QB), f32)
    acc_ref[...] = jnp.zeros((RB, 2 * HD, QB), f32)

    def key_block(kb, _):
        cols = pl.ds(pl.multiple_of(kb * KBR, KBR), KBR)
        kt_ref[...] = jnp.transpose(kv_ref[:, cols, :].reshape(KEYS, 2 * HD).astype(f32)).astype(bf16)

        def step(rb, masked):
            s = dot_nt(kv_ref[:, cols, :].reshape(KEYS, 2 * HD), x_ref[rb])
            if masked:
                s = s + block_bias(kpb_ref[kb], spl_ref[rb], stl_ref[rb])
            m_old = m_ref[rb]
            m_new = jnp.maximum(m_old, jnp.max(s, axis=0, keepdims=True))
            alpha = jnp.exp(m_old - m_new)
            p = jnp.exp(s - m_new)
            l_ref[rb] = l_ref[rb] * alpha + jnp.sum(p, axis=0, keepdims=True)
            acc_ref[rb] = acc_ref[rb] * alpha + dot(kt_ref[...], p.astype(bf16))
            m_ref[rb] = m_new

        visit(cls_ref, kb, step)
        return 0

    lax.fori_loop(0, KB, key_block, 0)
    keep = lanes_low((RBR, 2 * HD))
    first = at_ref[0] == 0
    for rb in range(RB):
        rows = slice(rb * RBR, (rb + 1) * RBR)
        l = l_ref[rb]
        lse_ref[rb] = m_ref[rb] + jnp.log(l)
        out = jnp.transpose(acc_ref[rb] / l)
        o_ref[rb] = out
        for h in range(0, H, 2):
            even = out[h * RBR : (h + 1) * RBR, :]
            odd = out[(h + 1) * RBR : (h + 2) * RBR, :]
            att_ref[rows, h * HD : (h + 2) * HD] = jnp.where(keep, pltpu.roll(even, HD, 1), odd).astype(bf16)
    n1, att = n1_ref[...], att_ref[...]
    keep_ref[...] = jnp.where(first, n1, att)
    send_ref[...] = jnp.where(first, att, n1)


def backward_kernel(at_ref, cls_ref, x_ref, do_ref, o_ref, lse_ref, kv_ref, kpb_ref, spl_ref, stl_ref, gb_ref,
                    dq_ref, keep_ref, send_ref, same_ref, other_ref, y_ref, drow_ref, dqt_ref, acc_ref, kt_ref):
    low = lanes_low((ROWS, 2 * HD))
    for h in range(H):
        pair = do_ref[:, (h // 2) * 128 : (h // 2) * 128 + 128].astype(f32)
        if h % 2 == 0:
            pair = pltpu.roll(pair, HD, 1)
        head = jnp.where(low, 0.0, pair).astype(bf16)
        for rb in range(RB):
            y_ref[rb, h * RBR : (h + 1) * RBR, :] = head[rb * RBR : (rb + 1) * RBR, :]
    for rb in range(RB):
        delta = jnp.sum(y_ref[rb].astype(f32) * o_ref[rb], axis=1, keepdims=True)
        drow_ref[rb] = jnp.transpose(jnp.broadcast_to(delta, (QB, 128)))[:8]
    dqt_ref[...] = jnp.zeros((RB, 128, QB), f32)

    def key_block(kb, _):
        cols = pl.ds(pl.multiple_of(kb * KBR, KBR), KBR)
        kvb = kv_ref[:, cols, :].reshape(KEYS, 2 * HD)
        kt_ref[...] = jnp.transpose(kvb.astype(f32)).astype(bf16)
        acc_ref[...] = jnp.zeros((KEYS, 2 * HD), f32)

        def step(rb, masked):
            kvb = kv_ref[:, cols, :].reshape(KEYS, 2 * HD)
            xb, yb = x_ref[rb], y_ref[rb]
            s = dot_nt(kvb, xb)
            if masked:
                s = s + block_bias(kpb_ref[kb], spl_ref[rb], stl_ref[rb])
            p = jnp.exp(s - lse_ref[rb])
            ds = (p * (dot_nt(kvb, yb) - drow_ref[rb, :1])).astype(bf16)
            acc_ref[...] += dot(ds, xb) + dot(p.astype(bf16), yb)
            dqt_ref[rb] += dot(kt_ref[...], ds)

        visit(cls_ref, kb, step)
        sums = acc_ref[...].reshape(WIDE, KBR, 2 * HD).astype(bf16)
        same_ref[:, cols, :] = sums[:CHIPS]
        other_ref[:, cols, :] = sums[CHIPS:]
        return 0

    lax.fori_loop(0, KB, key_block, 0)
    keep = lanes_low((RBR, 2 * HD))
    for rb in range(RB):
        dq = jnp.transpose(dqt_ref[rb]) * 0.125
        for h in range(0, H, 2):
            even = dq[h * RBR : (h + 1) * RBR, :]
            odd = dq[(h + 1) * RBR : (h + 2) * RBR, :]
            dq_ref[rb * RBR : (rb + 1) * RBR, h * HD : (h + 2) * HD] = jnp.where(
                keep, even, pltpu.roll(odd, HD, 1)
            ).astype(bf16)
    first = at_ref[0] == 0
    dq, gb = dq_ref[...], gb_ref[...]
    keep_ref[...] = jnp.where(first, dq, gb)
    send_ref[...] = jnp.where(first, gb, dq)


def put_rows(ref, at, row):
    for i in range(row.shape[1] // 128):
        ref[pl.ds(at + i, 1), :] = row[:, i * 128 : (i + 1) * 128]


def middle_kernel(at_ref, att_ref, x_ref, g_ref, wout_ref, bout_ref, gain_ref, bias_ref, wup_ref, bup_ref, wdown_ref, bdown_ref,
                  y_ref, bk_ref, bs_ref, sk_ref, ss_ref, gr_ref, gb_ref, ga_ref, vec_ref,
                  resid_ref, out_ref, gn2_ref, n2_ref):
    step = pl.program_id(0)
    first = at_ref[0] == 0

    @pl.when(step == 0)
    def _():
        resid = x_ref[...].astype(f32) + (dot(att_ref[...], wout_ref[...]) + vec(bout_ref))
        resid_ref[...] = resid
        n, _ = norm_parts(resid)
        n2 = (n * vec(gain_ref) + vec(bias_ref)).astype(bf16)
        n2_ref[...] = n2
        sk_ref[...] = jnp.where(first, g_ref[...], n2)
        ss_ref[...] = jnp.where(first, n2, g_ref[...])
        out_ref[...] = jnp.zeros_like(out_ref)
        gn2_ref[...] = jnp.zeros_like(gn2_ref)

    g = g_ref[...]
    pre = dot(n2_ref[...], wup_ref[...]) + vec(bup_ref)
    sq = pre * pre
    t = jnp.tanh(0.7978845608028654 * (pre + 0.044715 * sq * pre))
    half = 0.5 + 0.5 * t
    act = (pre * half).astype(bf16)
    slope = half + (0.5 * 0.7978845608028654) * pre * (1.0 - t * t) * (1.0 + (3 * 0.044715) * sq)
    gp = (slope * dot_nt(g, wdown_ref[...])).astype(bf16)
    bk_ref[...] = jnp.where(first, act, gp)
    bs_ref[...] = jnp.where(first, gp, act)
    put_rows(vec_ref, 24 + step * (FC // 128), jnp.sum(gp.astype(f32), axis=0, keepdims=True))
    out_ref[...] += dot(act, wdown_ref[...])
    gn2_ref[...] += dot_nt(gp, wup_ref[...])

    @pl.when(step == pl.num_programs(0) - 1)
    def _():
        resid = resid_ref[...]
        gf = g.astype(f32)
        y_ref[...] = (resid + (out_ref[...] + vec(bdown_ref))).astype(bf16)
        n, rstd = norm_parts(resid)
        e = gn2_ref[...]
        gr = gf + norm_back(e, n, rstd, vec(gain_ref))
        gr_ref[...] = gr
        gb = gr.astype(bf16)
        gb_ref[...] = gb
        ga_ref[...] = dot_nt(gb, wout_ref[...]).astype(bf16)
        put_rows(vec_ref, 0, jnp.sum(gf, axis=0, keepdims=True))
        put_rows(vec_ref, 6, jnp.sum(e * n, axis=0, keepdims=True))
        put_rows(vec_ref, 12, jnp.sum(e, axis=0, keepdims=True))
        put_rows(vec_ref, 18, jnp.sum(gb.astype(f32), axis=0, keepdims=True))


def leave_kernel(at_ref, x_ref, gain_ref, wq_ref, wkv_ref, gq_ref, gr_ref, mid_ref, parts_ref, gin_ref, keep_ref, send_ref, vec_ref):
    gkv = jnp.sum(parts_ref[...].astype(f32), axis=0).astype(bf16)
    gq = gq_ref[...]
    e = dot_nt(gq, wq_ref[...]) + dot_nt(gkv, wkv_ref[...])
    n, rstd = norm_parts(x_ref[...].astype(f32))
    gin = gr_ref[...] + norm_back(e, n, rstd, vec(gain_ref))
    for i in range(D // 128):
        gin_ref[pl.ds(i, ROWS, stride=D // 128), :] = gin[:, i * 128 : (i + 1) * 128]
    gkv = gkv.astype(f32)
    vec_ref[0:48, :] = mid_ref[...]
    vec_ref[48:128, :] = jnp.zeros((80, 128), f32)
    put_rows(vec_ref, 48, jnp.sum(e * n, axis=0, keepdims=True))
    put_rows(vec_ref, 54, jnp.sum(e, axis=0, keepdims=True))
    put_rows(vec_ref, 60, jnp.sum(gq.astype(f32), axis=0, keepdims=True))
    put_rows(vec_ref, 66, jnp.sum(gkv, axis=0, keepdims=True))
    first = at_ref[0] == 0
    vecs = vec_ref[...]
    keep_ref[...] = jnp.where(first, gkv, vecs)
    send_ref[...] = jnp.where(first, vecs, gkv)


def pack_kernel(bk_ref, sk_ref, bp_ref, sp_ref, out_ref):
    for i in range(4):
        cols = slice(i * D, (i + 1) * D)
        out_ref[i, 0:ROWS, 0:D] = bk_ref[:, cols]
        out_ref[i, ROWS:, 0:D] = bp_ref[:, cols]
        out_ref[i, 0:ROWS, D:] = sk_ref[...]
        out_ref[i, ROWS:, D:] = sp_ref[...]

def quarters(at, which, total_ref, outs):
    rows = total_ref.shape[0]//4
    for rel, out in zip((0,1,3,2), outs):
        out[...] = total_ref[pl.ds(pl.multiple_of(((at[which]+rel)&3)*rows, rows), rows), :].astype(out.dtype)

def weight_kernel(at_ref, slab_ref, own_ref, plus_ref, minus_ref, far_ref, total_ref):
    step = pl.program_id(0)

    @pl.when(step == 0)
    def _():
        total_ref[...] = jnp.zeros_like(total_ref)

    @pl.when(at_ref[0] == 0)
    def _():
        total_ref[...] += dot_tn(slab_ref[0, :, :D], slab_ref[0, :, D:])

    @pl.when(at_ref[0] == 1)
    def _():
        total_ref[...] += dot_tn(slab_ref[0, :, D:], slab_ref[0, :, :D])

    @pl.when(step == pl.num_programs(0) - 1)
    def _():
        quarters(at_ref, 2, total_ref, (own_ref, plus_ref, minus_ref, far_ref))


def join_kernel(at_ref,a_ref,b_ref,c_ref,d_ref,out_ref):
    rows=a_ref.shape[0]
    for rel, v in zip(FROM,(a_ref,b_ref,c_ref,d_ref)):
        out_ref[pl.ds(pl.multiple_of(((at_ref[2]+rel)&3)*rows,rows),rows),:] = v[...]

def place_kernel(at_ref, own_ref, other_ref, *rest):
    down_ref, up_ref = rest[-2:]
    first = at_ref[0]==0
    own, other = own_ref[...], other_ref[...]
    down_ref[...] = jnp.where(first, own, other).astype(f32)
    up_ref[...] = jnp.where(first, other, own).astype(f32)

def place(at, rel, own, other, kept, part=0):
    tile = D // 2
    piece = pl.BlockSpec((tile, D), lambda i, at: (i, 0))
    outs = (
        pl.BlockSpec((tile, D), lambda i, at: (((at[4] + rel) & 3) * 2 + part + i, 0)),
        pl.BlockSpec((tile, D), lambda i, at: (part + i, (at[5] + rel) & 3)),
    )
    return pl.pallas_call(
        place_kernel,
        grid_spec=pltpu.PrefetchScalarGridSpec(
            num_scalar_prefetch=1, grid=(own.shape[0] // tile,), in_specs=[piece, piece] + [ANY] * len(kept), out_specs=outs
        ),
        out_shape=shapes(((FF, D), f32), ((D, FF), f32)),
        input_output_aliases={3: 0, 4: 1} if kept else {},
        compiler_params=params(62),
        cost_estimate=cost(0, 0),
        name="place",
    )(at, own, other, *kept)


def share_kernel(same_ref, other_ref, out_ref):
    out_ref[...] = (same_ref[...].astype(f32) + other_ref[...].astype(f32)).astype(bf16)


def square_kernel(lk_ref, lo_ref, rk_ref, ro_ref, out_ref):
    out_ref[...] = (dot_tn(lk_ref[...], rk_ref[...]) + dot_tn(lo_ref[...], ro_ref[...])).astype(bf16)


def late_kernel(at_ref, lk_ref, lo_ref, tk_ref, to_ref, square_ref, out_ref, total_ref):
    first = at_ref[0] == 0

    @pl.when(first)
    def _():
        total_ref[...] = dot_tn(lk_ref[...], tk_ref[...].astype(bf16)) + dot_tn(lo_ref[...], to_ref[...].astype(bf16))

    @pl.when(jnp.logical_not(first))
    def _():
        total_ref[0:128, :] = tk_ref[...] + to_ref[...]
        total_ref[128:, :] = jnp.zeros((D - 128, 128), f32)

    for i in range(CHIPS):
        rows = slice(STRIP * i, STRIP * (i + 1))
        out_ref[i, :, :D] = square_ref[rows, :]
        out_ref[i, :, D:] = total_ref[rows, :].astype(bf16)


def strip_kernel(parts_ref, out_ref):
    out_ref[...] = jnp.sum(parts_ref[...].astype(f32), axis=0).astype(bf16)


def part_kernel(a_ref, b_ref, c_ref, d_ref, out_ref):
    out_ref[...] = pair_sums(a_ref[...], b_ref[...], c_ref[...], d_ref[...])


def copies_kernel(a_ref, b_ref, c_ref, d_ref, out_ref):
    total = pair_sums(a_ref[...], b_ref[...], c_ref[...], d_ref[...])
    for i in range(CHIPS):
        out_ref[i] = total


VECTORS = ((0, 6), (6, 6), (12, 6), (18, 6), (24, 24), (48, 6), (54, 6), (60, 6))


def late_place_kernel(at_ref, own_ref, other_ref, query_ref, out_ref, kv_ref, value_ref, *vec_refs):
    first = at_ref[0] == 0
    vecs = []
    for a in range(CHIPS):
        rows = slice(STRIP * a, STRIP * (a + 1))
        own, other = own_ref[a].astype(f32), other_ref[a].astype(f32)
        zero, one = jnp.where(first, own, other), jnp.where(first, other, own)
        query_ref[rows, :] = zero[:, :D]
        out_ref[rows, :] = one[:, :D]
        kv_ref[rows, :] = zero[:, D:]
        if a < 2:
            vecs.append(one[:, D:])
    row = lambda i: vecs[i // STRIP][i % STRIP]
    value_ref[...] = row(66)[HD:]
    for ref, (at, count) in zip(vec_refs, VECTORS):
        for i in range(count):
            ref[i * 128 : (i + 1) * 128] = row(at + i)


def call(kernel, args, outs, scratch=(), name=None, flops=0, nbytes=2e6, after=()):
    given, extra = len(args), len(after)
    run = lambda *refs: kernel(*refs[:given], *refs[given + extra :])
    return pl.pallas_call(
        run,
        out_shape=outs,
        in_specs=[SMEM if v.dtype == jnp.int32 and v.ndim == 1 else VMEM for v in args] + [ANY] * extra,
        out_specs=jax.tree.map(lambda _: VMEM, outs),
        scratch_shapes=list(scratch),
        compiler_params=params(),
        cost_estimate=cost(flops, nbytes),
        name=name,
    )(*args, *after)


def shapes(*pairs):
    return tuple(jax.ShapeDtypeStruct(s, t) for s, t in pairs)


def positions(lengths, splits, wide_index, core):
    ends = jnp.cumsum(lengths, dtype=jnp.int32)
    starts = ends - lengths
    first = lengths * jnp.minimum(splits[:, 0], splits[:, 1]) // 1024
    second = lengths * jnp.maximum(splits[:, 0], splits[:, 1]) // 1024

    def place(row):
        shape = (1,) * row.ndim + (-1,)
        s, e, a, b, n = (v.reshape(shape) for v in (starts, ends, first, second, lengths))
        row = row[..., None]
        inside = (row >= s) & (row < e)
        u = row - s
        moved = jnp.where(u < a, u, jnp.where(u >= b, a + u - b, a + n - b + u - a))
        return (
            jnp.sum(jnp.where(inside, s + moved, 0), axis=-1, dtype=jnp.int32),
            jnp.sum(jnp.where(inside, s, 0), axis=-1, dtype=jnp.int32),
        )

    k = jnp.arange(KB, dtype=jnp.int32)[:, None, None]
    j = jnp.arange(CHIPS, dtype=jnp.int32) * 2
    j = jnp.concatenate([j + core, j + 1 - core])[None, :, None]
    r = jnp.arange(KBR, dtype=jnp.int32)[None, None, :]
    keys, _ = place(((k * KBR + r) * WIDE + j).reshape(KB, KEYS))
    own, own_start = place(jnp.arange(ROWS, dtype=jnp.int32) * WIDE + wide_index)
    low, high = jnp.min(keys, axis=1), jnp.max(keys, axis=1)
    blocks, block_starts = own.reshape(RB, RBR), own_start.reshape(RB, RBR)
    top, start_low = jnp.max(blocks, axis=1), jnp.min(block_starts, axis=1)
    bottom, start_high = jnp.min(blocks, axis=1), jnp.max(block_starts, axis=1)
    some = (low[None] <= top[:, None]) & (high[None] >= start_low[:, None])
    every = (high[None] <= bottom[:, None]) & (low[None] >= start_high[:, None])
    kinds = jnp.where(every, 2, jnp.where(some, 1, 0)).astype(jnp.int32).reshape(-1)
    return keys, own, own_start, kinds


NARROW = ((ROWS, D), bf16)
KV_HALF = ((CHIPS, ROWS, 2 * HD), bf16)


def attend(*args):
    stat = pltpu.VMEM((RB, 1, QB), f32)
    return call(
        forward_kernel, args,
        shapes(NARROW, NARROW, NARROW, ((RB, QB, 128), bf16), ((RB, QB, 128), f32), ((RB, 1, QB), f32), ((WIDE, ROWS, 2 * HD), bf16)),
        [stat, stat, pltpu.VMEM((RB, 2 * HD, QB), f32), pltpu.VMEM((2 * HD, KEYS), bf16)],
        name="attend", flops=4 * ROWS * H * WINDOW * 64, nbytes=4e6,
    )


def attend_back(*args, after=()):
    return call(
        backward_kernel, args,
        shapes(NARROW, NARROW, NARROW, KV_HALF, KV_HALF),
        [
            pltpu.VMEM((RB, QB, 128), bf16), pltpu.VMEM((RB, 8, QB), f32),
            pltpu.VMEM((RB, 128, QB), f32), pltpu.VMEM((KEYS, 2 * HD), f32), pltpu.VMEM((2 * HD, KEYS), bf16),
        ],
        name="attend_back", flops=10 * ROWS * H * WINDOW * 64, nbytes=8e6, after=after,
    )


def coords():
    x, y, z, c = (lax.axis_index(a) for a in AXES)
    first = c == 0
    at = (c, jnp.where(first, z, y), jnp.where(first, y, x), jnp.where(first, x, z), z, y)
    return jnp.stack(at).astype(jnp.int32)


QUARTER = ((D // 4, D), bf16)
HALF = ((D // 2, D), bf16)


def pair_sums(a, b, c, d):
    a, b, c, d = (v.astype(f32) for v in (a, b, c, d))
    return ((a + d) + (b + c)).astype(bf16)


def tie_kernel(v_ref, *refs):
    pass


def tie(v, *after):
    return pl.pallas_call(
        tie_kernel,
        out_shape=jax.ShapeDtypeStruct(v.shape, v.dtype),
        in_specs=[ANY] * (1 + len(after)),
        out_specs=ANY,
        input_output_aliases={0: 0},
        cost_estimate=cost(0, 0),
        name="tie",
    )(v, *after)


def corner(v):
    return swap(v[:8, :128])


def halves_kernel(before_ref, after_ref, low_ref, high_ref):
    low_ref[...] = before_ref[D // 2 :, :]
    high_ref[...] = after_ref[: D // 2, :]


def feed_forward_rest(at, before, after, kept, mark):
    low, high = call(halves_kernel, (before, after), shapes(HALF, HALF), name="halves", after=(mark,))
    before, after = tie(before, low), tie(after, high)
    low, high = send(low, 0, 1), send(high, 0, 3)
    kept = place(at, 3, before, swap(before), kept)
    kept = place(at, 1, after, swap(after), kept)
    low, high = (tie(v, kept[0]) for v in (low, high))
    kept = place(at, 2, high, swap(high), kept)
    return *place(at, 2, low, swap(low), kept, part=1), low, high


def body(block_input, file_lengths, file_splits, ln1_gain, ln1_bias, w_query, b_query, w_kv, b_value, w_out, b_out,
         ln2_gain, ln2_bias, w_up, b_up, w_down, b_down, out_cotangent):
    x = block_input.reshape(ROWS, D)
    g = out_cotangent.reshape(ROWS, D)
    wide = ("y", "z", "c")
    at = coords()
    narrow = NARROW

    n1, copies = call(enter_kernel, (x, ln1_gain, ln1_bias, w_kv, b_value), shapes(narrow, ((CHIPS, ROWS, 2 * HD), bf16)),
                      name="enter", flops=2 * ROWS * D * 128)
    kv_same = lax.all_to_all(copies, ("y", "z"), 0, 0, tiled=True)
    keys, own, own_start, kinds = positions(file_lengths[0], file_splits[0], lax.axis_index(wide), at[0])
    key_cols = jnp.broadcast_to(keys[:, :, None], (KB, KEYS, 128))
    own_lanes = jnp.tile(own.reshape(RB, 1, RBR), (1, 1, 128 // RBR))
    start_lanes = jnp.tile(own_start.reshape(RB, 1, RBR), (1, 1, 128 // RBR))
    q = call(query_kernel, (n1, w_query, b_query), shapes(narrow)[0], name="query", flops=2 * ROWS * D * D,
             after=(key_cols, own_lanes, start_lanes, kinds))
    kv_same = tie(kv_same, q)
    kv_other = swap(kv_same)

    att, left, left_send, xq, o, lse, kv_all = attend(at, kinds, q, kv_same, kv_other, key_cols, own_lanes, start_lanes, n1)
    left_other = swap(left_send)

    steps = FF // FC
    whole = lambda *s: pl.BlockSpec(s, lambda i: (0,) * len(s))
    wide_cols = pl.BlockSpec((ROWS, FC), lambda i: (0, i))
    y, big, big_send, small, small_send, gr, gb, ga, vec_mid = pl.pallas_call(
        middle_kernel,
        grid=(steps,),
        out_shape=shapes(narrow, ((ROWS, FF), bf16), ((ROWS, FF), bf16), narrow, narrow, ((ROWS, D), f32), narrow, narrow, ((48, 128), f32)),
        in_specs=[
            SMEM, whole(ROWS, D), whole(ROWS, D), whole(ROWS, D), whole(D, D), whole(D), whole(D), whole(D),
            pl.BlockSpec((D, FC), lambda i: (0, i)), pl.BlockSpec((FC,), lambda i: (i,)),
            pl.BlockSpec((FC, D), lambda i: (i, 0)), whole(D),
        ],
        out_specs=(
            whole(ROWS, D), wide_cols, wide_cols, whole(ROWS, D), whole(ROWS, D), whole(ROWS, D), whole(ROWS, D),
            whole(ROWS, D), whole(48, 128),
        ),
        scratch_shapes=[pltpu.VMEM((ROWS, D), f32)] * 3 + [pltpu.VMEM((ROWS, D), bf16)],
        compiler_params=params(),
        cost_estimate=cost(8 * ROWS * D * FF, 2e7),
        name="middle",
    )(at, att, x, g, w_out, b_out, ln2_gain, ln2_bias, w_up, b_up, w_down, b_down)

    packed = call(pack_kernel, (big, small, swap(big_send), swap(small_send)), shapes(((4, 2 * ROWS, 2 * D), bf16))[0], name="pack")
    slabs = lax.all_to_all(packed, AXES, 0, 0, axis_index_groups=ring_groups(0), tiled=True)

    gq, right, right_send, kv_grads, kv_send = attend_back(at, kinds, xq, ga, o, lse, kv_all, key_cols, own_lanes, start_lanes, gb, after=(packed,))
    shares = call(share_kernel, (kv_grads, swap(kv_send)), shapes(KV_HALF)[0], name="share", after=(slabs,))
    parts = lax.all_to_all(shares, ("y", "z"), 0, 0, tiled=True)

    pieces = pl.pallas_call(
        weight_kernel,
        grid=(4,),
        out_shape=shapes(*[QUARTER] * 4),
        in_specs=[SMEM, pl.BlockSpec((1, 2 * ROWS, 2 * D), lambda i: (i, 0, 0))],
        out_specs=(VMEM,) * 4,
        scratch_shapes=[pltpu.VMEM((D, D), f32)],
        compiler_params=params(62),
        cost_estimate=cost(0, 0),
        name="weights",
    )(at, slabs)
    ff_parts = (pieces[0],) + spread(1, *pieces[1:])
    square = call(square_kernel, (left, left_other, right, swap(right_send)), shapes(((D, D), bf16))[0], name="square")
    gin, tail, tail_send, _ = call(
        leave_kernel, (at, x, ln1_gain, w_query, w_kv, gq, gr, vec_mid, parts),
        shapes(((ROWS * D // 128, 128), f32), ((128, 128), f32), ((128, 128), f32), ((128, 128), f32)),
        name="leave", after=(pieces[0], square),
    )

    shares = call(late_kernel, (at, left, left_other, tail, swap(tail_send), square), shapes(((CHIPS, STRIP, D + 128), bf16))[0],
                  [pltpu.VMEM((D, 128), f32)], name="late", after=ff_parts[1:])
    ff_part = call(part_kernel, ff_parts, shapes(QUARTER)[0], name="part", after=(shares,))
    ff_crossed = gather4(ff_part, 2)
    late_parts = lax.all_to_all(shares, ("y", "z"), 0, 0, tiled=True)
    ff_totals = gather4(pair_sums(*ff_crossed), 1)
    strip = call(strip_kernel, (late_parts,), shapes(((STRIP, D + 128), bf16))[0], name="strip", after=ff_crossed[1:])
    u = call(join_kernel, (at,) + ff_totals, shapes(((D, D), bf16))[0], name="join", after=(strip,))
    before, after = send(u, 0, 1), send(u, 0, 3)
    kept = place(at, 0, u, swap(u), ())
    mark = corner(kept[0])
    copies = call(copies_kernel, gather4(strip, 3), shapes(((CHIPS, STRIP, D + 128), bf16))[0], name="copies",
                  after=(before, after, mark))
    late = lax.all_to_all(copies, ("y", "z"), 0, 0, tiled=True)
    g_down, g_up, *rest = feed_forward_rest(at, before, after, kept, mark)
    late = tie(late, *rest)
    one = lambda n: ((n,), f32)
    outs = call(
        late_place_kernel, (at, late, swap(late)),
        shapes(((D, D), f32), ((D, D), f32), ((D, 128), f32), one(HD), *[one(128 * n) for _, n in VECTORS]), name="late_place",
    )
    g_query, g_out, g_kv, g_value, g_bdown, g_gain2, g_bias2, g_bout, g_bup, g_gain1, g_bias1, g_bq = outs
    shape = block_input.shape
    return (
        y.reshape(shape), gin.reshape(shape), g_gain1, g_bias1, g_query, g_bq, g_kv, g_value,
        g_out, g_bout, g_gain2, g_bias2, g_up, g_bup, g_down, g_bdown,
    )


def solution(mesh):
    split = P("x", None, ("y", "z", "c"), None)
    return jax.shard_map(
        body,
        mesh=Mesh(mesh.devices.reshape(4, 4, 4, 2), AXES),
        in_specs=(split, P("x", None), P("x", None, None)) + (P(),) * 14 + (split,),
        out_specs=(split, split) + (P(),) * 14,
        check_vma=False,
    )
```

```python
import itertools

import jax
import jax.numpy as jnp
from jax import lax
from jax.experimental import pallas as pl
from jax.experimental.pallas import tpu as pltpu
from jax.sharding import Mesh, PartitionSpec as P

EPS = 1e-05
MASKED = -1e30
ROWS = 128
WIDE = 32
CHIPS = 16
D = 768
H = 12
HD = 64
FF = 3072
WINDOW = ROWS * WIDE
RB = 2
RBR = ROWS // RB
QB = RBR * H
KB = 4
KBR = ROWS // KB
KEYS = WINDOW // KB
STRIP = D // CHIPS
FC = 1024
VMEM = pl.BlockSpec(memory_space=pltpu.VMEM)
SMEM = pl.BlockSpec(memory_space=pltpu.SMEM)
ANY = pl.BlockSpec(memory_space=pl.ANY)
f32 = jnp.float32
bf16 = jnp.bfloat16


def params(limit=56):
    return pltpu.CompilerParams(vmem_limit_bytes=limit * 1024 * 1024)


def cost(flops, nbytes):
    return pl.CostEstimate(flops=1, bytes_accessed=1, transcendentals=0)


def dot(a, b):
    return jnp.dot(a, b, preferred_element_type=f32)


def dot_nt(a, b):
    return lax.dot_general(a, b, (((1,), (1,)), ((), ())), preferred_element_type=f32)


def dot_tn(a, b):
    return lax.dot_general(a, b, (((0,), (0,)), ((), ())), preferred_element_type=f32)


def norm_parts(x):
    mean = jnp.mean(x, axis=-1, keepdims=True)
    centered = x - mean
    var = jnp.mean(centered * centered, axis=-1, keepdims=True)
    rstd = lax.rsqrt(var + EPS)
    return centered * rstd, rstd


def norm_back(e, n, rstd, gain):
    m = e * gain
    return rstd * (
        m - jnp.mean(m, axis=-1, keepdims=True) - n * jnp.mean(m * n, axis=-1, keepdims=True)
    )


AXES = ("x", "y", "z", "c")
ORDER = ((2, 1, 0, 0), (1, 0, 2, 2))
FROM = (0, 3, 1, 2)


def ring(place, shift):
    pairs = []
    for at in itertools.product(range(4), range(4), range(4), range(2)):
        to = list(at)
        axis = ORDER[at[3]][place]
        to[axis] = (to[axis] + shift) % 4
        index = lambda v: ((v[0] * 4 + v[1]) * 4 + v[2]) * 2 + v[3]
        pairs.append((index(at), index(to)))
    return pairs


def groups_by(key):
    groups = {}
    for at in itertools.product(range(4), range(4), range(4), range(2)):
        groups.setdefault(key(at), []).append(((at[0] * 4 + at[1]) * 4 + at[2]) * 2 + at[3])
    return list(groups.values())


def ring_groups(place):
    return groups_by(lambda at: tuple(-1 if i == ORDER[at[3]][place] else v for i, v in enumerate(at)))


def in_plane(v):
    planes = groups_by(lambda at: (at[ORDER[at[3]][3]], at[3]))
    return lax.all_to_all(v, AXES, 0, 0, axis_index_groups=planes, tiled=True)


def send(v, place, shift):
    return lax.ppermute(v, AXES, ring(place, shift))


def swap(v):
    return lax.ppermute(v, "c", [(0, 1), (1, 0)])


def spread(place, plus, minus, far):
    return send(plus, place, 1), send(minus, place, 3), send(far, place, 2)


def gather4(v, place):
    return (v,) + spread(place, v, v, v)


def lanes_low(shape):
    return lax.broadcasted_iota(jnp.int32, shape, len(shape) - 1) < HD


def vec(ref):
    return ref[...].astype(f32).reshape(1, -1)


def enter_kernel(x_ref, gain_ref, bias_ref, wkv_ref, bv_ref, n1_ref, kv_ref):
    n, _ = norm_parts(x_ref[...].astype(f32))
    n1 = (n * vec(gain_ref) + vec(bias_ref)).astype(bf16)
    n1_ref[...] = n1
    shift = jnp.concatenate([jnp.zeros((1, HD), f32), vec(bv_ref)], axis=1)
    kv = (dot(n1, wkv_ref[...]) + shift).astype(bf16)
    for i in range(CHIPS):
        kv_ref[i] = kv


def query_kernel(n1_ref, wq_ref, bq_ref, q_ref):
    q_ref[...] = (dot(n1_ref[...], wq_ref[...]) + vec(bq_ref)).astype(bf16)


def block_bias(kp, sp, st):
    bias = jnp.where((kp <= sp) & (kp >= st), 0.0, MASKED)
    return jnp.concatenate([bias] * (QB // 128), axis=1)


def visit(cls_ref, kb, step):
    def row_block(rb, _):
        kind = cls_ref[rb * KB + kb]

        @pl.when(kind == 2)
        def _():
            step(rb, False)

        @pl.when(kind == 1)
        def _():
            step(rb, True)

        return 0

    lax.fori_loop(0, RB, row_block, 0)


def forward_kernel(at_ref, cls_ref, q_ref, same_ref, other_ref, kpb_ref, spl_ref, stl_ref, n1_ref,
                   att_ref, keep_ref, send_ref, x_ref, o_ref, lse_ref, kv_ref, m_ref, l_ref, acc_ref, kt_ref):
    kv_ref[:CHIPS] = same_ref[...]
    kv_ref[CHIPS:] = other_ref[...]
    low = lanes_low((ROWS, 2 * HD))
    for h in range(H):
        pair = q_ref[:, (h // 2) * 128 : (h // 2) * 128 + 128].astype(f32) * 0.125
        if h % 2:
            pair = pltpu.roll(pair, HD, 1)
        head = jnp.where(low, pair, 0.0).astype(bf16)
        for rb in range(RB):
            x_ref[rb, h * RBR : (h + 1) * RBR, :] = head[rb * RBR : (rb + 1) * RBR, :]
    m_ref[...] = jnp.full((RB, 1, QB), MASKED, f32)
    l_ref[...] = jnp.zeros((RB, 1, QB), f32)
    acc_ref[...] = jnp.zeros((RB, 2 * HD, QB), f32)

    def key_block(kb, _):
        cols = pl.ds(pl.multiple_of(kb * KBR, KBR), KBR)
        kt_ref[...] = jnp.transpose(kv_ref[:, cols, :].reshape(KEYS, 2 * HD).astype(f32)).astype(bf16)

        def step(rb, masked):
            s = dot_nt(kv_ref[:, cols, :].reshape(KEYS, 2 * HD), x_ref[rb])
            if masked:
                s = s + block_bias(kpb_ref[kb], spl_ref[rb], stl_ref[rb])
            m_old = m_ref[rb]
            m_new = jnp.maximum(m_old, jnp.max(s, axis=0, keepdims=True))
            alpha = jnp.exp(m_old - m_new)
            p = jnp.exp(s - m_new)
            l_ref[rb] = l_ref[rb] * alpha + jnp.sum(p, axis=0, keepdims=True)
            acc_ref[rb] = acc_ref[rb] * alpha + dot(kt_ref[...], p.astype(bf16))
            m_ref[rb] = m_new

        visit(cls_ref, kb, step)
        return 0

    lax.fori_loop(0, KB, key_block, 0)
    keep = lanes_low((RBR, 2 * HD))
    first = at_ref[0] == 0
    for rb in range(RB):
        rows = slice(rb * RBR, (rb + 1) * RBR)
        l = l_ref[rb]
        lse_ref[rb] = m_ref[rb] + jnp.log(l)
        out = jnp.transpose(acc_ref[rb] / l)
        o_ref[rb] = out
        for h in range(0, H, 2):
            even = out[h * RBR : (h + 1) * RBR, :]
            odd = out[(h + 1) * RBR : (h + 2) * RBR, :]
            att_ref[rows, h * HD : (h + 2) * HD] = jnp.where(keep, pltpu.roll(even, HD, 1), odd).astype(bf16)
    n1, att = n1_ref[...], att_ref[...]
    keep_ref[...] = jnp.where(first, n1, att)
    send_ref[...] = jnp.where(first, att, n1)


def backward_kernel(at_ref, cls_ref, x_ref, do_ref, o_ref, lse_ref, kv_ref, kpb_ref, spl_ref, stl_ref, gb_ref,
                    dq_ref, keep_ref, send_ref, same_ref, other_ref, y_ref, drow_ref, dqt_ref, acc_ref, kt_ref):
    low = lanes_low((ROWS, 2 * HD))
    for h in range(H):
        pair = do_ref[:, (h // 2) * 128 : (h // 2) * 128 + 128].astype(f32)
        if h % 2 == 0:
            pair = pltpu.roll(pair, HD, 1)
        head = jnp.where(low, 0.0, pair).astype(bf16)
        for rb in range(RB):
            y_ref[rb, h * RBR : (h + 1) * RBR, :] = head[rb * RBR : (rb + 1) * RBR, :]
    for rb in range(RB):
        delta = jnp.sum(y_ref[rb].astype(f32) * o_ref[rb], axis=1, keepdims=True)
        drow_ref[rb] = jnp.transpose(jnp.broadcast_to(delta, (QB, 128)))[:8]
    dqt_ref[...] = jnp.zeros((RB, 128, QB), f32)

    def key_block(kb, _):
        cols = pl.ds(pl.multiple_of(kb * KBR, KBR), KBR)
        kvb = kv_ref[:, cols, :].reshape(KEYS, 2 * HD)
        kt_ref[...] = jnp.transpose(kvb.astype(f32)).astype(bf16)
        acc_ref[...] = jnp.zeros((KEYS, 2 * HD), f32)

        def step(rb, masked):
            kvb = kv_ref[:, cols, :].reshape(KEYS, 2 * HD)
            xb, yb = x_ref[rb], y_ref[rb]
            s = dot_nt(kvb, xb)
            if masked:
                s = s + block_bias(kpb_ref[kb], spl_ref[rb], stl_ref[rb])
            p = jnp.exp(s - lse_ref[rb])
            ds = (p * (dot_nt(kvb, yb) - drow_ref[rb, :1])).astype(bf16)
            acc_ref[...] += dot(ds, xb) + dot(p.astype(bf16), yb)
            dqt_ref[rb] += dot(kt_ref[...], ds)

        visit(cls_ref, kb, step)
        sums = acc_ref[...].reshape(WIDE, KBR, 2 * HD).astype(bf16)
        same_ref[:, cols, :] = sums[:CHIPS]
        other_ref[:, cols, :] = sums[CHIPS:]
        return 0

    lax.fori_loop(0, KB, key_block, 0)
    keep = lanes_low((RBR, 2 * HD))
    for rb in range(RB):
        dq = jnp.transpose(dqt_ref[rb]) * 0.125
        for h in range(0, H, 2):
            even = dq[h * RBR : (h + 1) * RBR, :]
            odd = dq[(h + 1) * RBR : (h + 2) * RBR, :]
            dq_ref[rb * RBR : (rb + 1) * RBR, h * HD : (h + 2) * HD] = jnp.where(
                keep, even, pltpu.roll(odd, HD, 1)
            ).astype(bf16)
    first = at_ref[0] == 0
    dq, gb = dq_ref[...], gb_ref[...]
    keep_ref[...] = jnp.where(first, dq, gb)
    send_ref[...] = jnp.where(first, gb, dq)


def put_rows(ref, at, row):
    for i in range(row.shape[1] // 128):
        ref[pl.ds(at + i, 1), :] = row[:, i * 128 : (i + 1) * 128]


def middle_kernel(at_ref, att_ref, x_ref, g_ref, wout_ref, bout_ref, gain_ref, bias_ref, wup_ref, bup_ref, wdown_ref, bdown_ref,
                  y_ref, bk_ref, bs_ref, sk_ref, ss_ref, gr_ref, gb_ref, ga_ref, vec_ref,
                  resid_ref, out_ref, gn2_ref, n2_ref):
    step = pl.program_id(0)
    first = at_ref[0] == 0

    @pl.when(step == 0)
    def _():
        resid = x_ref[...].astype(f32) + (dot(att_ref[...], wout_ref[...]) + vec(bout_ref))
        resid_ref[...] = resid
        n, _ = norm_parts(resid)
        n2 = (n * vec(gain_ref) + vec(bias_ref)).astype(bf16)
        n2_ref[...] = n2
        sk_ref[...] = jnp.where(first, g_ref[...], n2)
        ss_ref[...] = jnp.where(first, n2, g_ref[...])
        out_ref[...] = jnp.zeros_like(out_ref)
        gn2_ref[...] = jnp.zeros_like(gn2_ref)

    g = g_ref[...]
    pre = dot(n2_ref[...], wup_ref[...]) + vec(bup_ref)
    sq = pre * pre
    t = jnp.tanh(0.7978845608028654 * (pre + 0.044715 * sq * pre))
    half = 0.5 + 0.5 * t
    act = (pre * half).astype(bf16)
    slope = half + (0.5 * 0.7978845608028654) * pre * (1.0 - t * t) * (1.0 + (3 * 0.044715) * sq)
    gp = (slope * dot_nt(g, wdown_ref[...])).astype(bf16)
    bk_ref[...] = jnp.where(first, act, gp)
    bs_ref[...] = jnp.where(first, gp, act)
    put_rows(vec_ref, 24 + step * (FC // 128), jnp.sum(gp.astype(f32), axis=0, keepdims=True))
    out_ref[...] += dot(act, wdown_ref[...])
    gn2_ref[...] += dot_nt(gp, wup_ref[...])

    @pl.when(step == pl.num_programs(0) - 1)
    def _():
        resid = resid_ref[...]
        gf = g.astype(f32)
        y_ref[...] = (resid + (out_ref[...] + vec(bdown_ref))).astype(bf16)
        n, rstd = norm_parts(resid)
        e = gn2_ref[...]
        gr = gf + norm_back(e, n, rstd, vec(gain_ref))
        gr_ref[...] = gr
        gb = gr.astype(bf16)
        gb_ref[...] = gb
        ga_ref[...] = dot_nt(gb, wout_ref[...]).astype(bf16)
        put_rows(vec_ref, 0, jnp.sum(gf, axis=0, keepdims=True))
        put_rows(vec_ref, 6, jnp.sum(e * n, axis=0, keepdims=True))
        put_rows(vec_ref, 12, jnp.sum(e, axis=0, keepdims=True))
        put_rows(vec_ref, 18, jnp.sum(gb.astype(f32), axis=0, keepdims=True))


def leave_kernel(at_ref, x_ref, gain_ref, wq_ref, wkv_ref, gq_ref, gr_ref, mid_ref, parts_ref, gin_ref, keep_ref, send_ref, vec_ref):
    gkv = jnp.sum(parts_ref[...].astype(f32), axis=0).astype(bf16)
    gq = gq_ref[...]
    e = dot_nt(gq, wq_ref[...]) + dot_nt(gkv, wkv_ref[...])
    n, rstd = norm_parts(x_ref[...].astype(f32))
    gin = gr_ref[...] + norm_back(e, n, rstd, vec(gain_ref))
    for i in range(D // 128):
        gin_ref[pl.ds(i, ROWS, stride=D // 128), :] = gin[:, i * 128 : (i + 1) * 128]
    gkv = gkv.astype(f32)
    vec_ref[0:48, :] = mid_ref[...]
    vec_ref[48:128, :] = jnp.zeros((80, 128), f32)
    put_rows(vec_ref, 48, jnp.sum(e * n, axis=0, keepdims=True))
    put_rows(vec_ref, 54, jnp.sum(e, axis=0, keepdims=True))
    put_rows(vec_ref, 60, jnp.sum(gq.astype(f32), axis=0, keepdims=True))
    put_rows(vec_ref, 66, jnp.sum(gkv, axis=0, keepdims=True))
    first = at_ref[0] == 0
    vecs = vec_ref[...]
    keep_ref[...] = jnp.where(first, gkv, vecs)
    send_ref[...] = jnp.where(first, vecs, gkv)


def pack_kernel(bk_ref, sk_ref, bp_ref, sp_ref, out_ref):
    for i in range(4):
        cols = slice(i * D, (i + 1) * D)
        out_ref[i, 0:ROWS, 0:D] = bk_ref[:, cols]
        out_ref[i, ROWS:, 0:D] = bp_ref[:, cols]
        out_ref[i, 0:ROWS, D:] = sk_ref[...]
        out_ref[i, ROWS:, D:] = sp_ref[...]

def quarters(at, which, total_ref, outs):
    rows = total_ref.shape[0]//4
    for rel, out in zip((0,1,3,2), outs):
        out[...] = total_ref[pl.ds(pl.multiple_of(((at[which]+rel)&3)*rows, rows), rows), :].astype(out.dtype)

def weight_kernel(at_ref, slab_ref, own_ref, plus_ref, minus_ref, far_ref, total_ref):
    step = pl.program_id(0)

    @pl.when(step == 0)
    def _():
        total_ref[...] = jnp.zeros_like(total_ref)

    @pl.when(at_ref[0] == 0)
    def _():
        total_ref[...] += dot_tn(slab_ref[0, :, :D], slab_ref[0, :, D:])

    @pl.when(at_ref[0] == 1)
    def _():
        total_ref[...] += dot_tn(slab_ref[0, :, D:], slab_ref[0, :, :D])

    @pl.when(step == pl.num_programs(0) - 1)
    def _():
        quarters(at_ref, 2, total_ref, (own_ref, plus_ref, minus_ref, far_ref))


def join_kernel(at_ref,a_ref,b_ref,c_ref,d_ref,out_ref):
    rows=a_ref.shape[0]
    for rel, v in zip(FROM,(a_ref,b_ref,c_ref,d_ref)):
        out_ref[pl.ds(pl.multiple_of(((at_ref[2]+rel)&3)*rows,rows),rows),:] = v[...]

def place_kernel(at_ref, own_ref, other_ref, *rest):
    down_ref, up_ref = rest[-2:]
    first = at_ref[0]==0
    own, other = own_ref[...], other_ref[...]
    down_ref[...] = jnp.where(first, own, other).astype(f32)
    up_ref[...] = jnp.where(first, other, own).astype(f32)

def place(at, rel, own, other, kept, part=0):
    tile = D // 2
    piece = pl.BlockSpec((tile, D), lambda i, at: (i, 0))
    outs = (
        pl.BlockSpec((tile, D), lambda i, at: (((at[4] + rel) & 3) * 2 + part + i, 0)),
        pl.BlockSpec((tile, D), lambda i, at: (part + i, (at[5] + rel) & 3)),
    )
    return pl.pallas_call(
        place_kernel,
        grid_spec=pltpu.PrefetchScalarGridSpec(
            num_scalar_prefetch=1, grid=(own.shape[0] // tile,), in_specs=[piece, piece] + [ANY] * len(kept), out_specs=outs
        ),
        out_shape=shapes(((FF, D), f32), ((D, FF), f32)),
        input_output_aliases={3: 0, 4: 1} if kept else {},
        compiler_params=params(62),
        cost_estimate=cost(0, 0),
        name="place",
    )(at, own, other, *kept)


def share_kernel(same_ref, other_ref, out_ref):
    out_ref[...] = (same_ref[...].astype(f32) + other_ref[...].astype(f32)).astype(bf16)


def square_kernel(lk_ref, lo_ref, rk_ref, ro_ref, out_ref):
    out_ref[...] = (dot_tn(lk_ref[...], rk_ref[...]) + dot_tn(lo_ref[...], ro_ref[...])).astype(bf16)


def late_kernel(at_ref, lk_ref, lo_ref, tk_ref, to_ref, square_ref, out_ref, total_ref):
    first = at_ref[0] == 0

    @pl.when(first)
    def _():
        total_ref[...] = dot_tn(lk_ref[...], tk_ref[...].astype(bf16)) + dot_tn(lo_ref[...], to_ref[...].astype(bf16))

    @pl.when(jnp.logical_not(first))
    def _():
        total_ref[0:128, :] = tk_ref[...] + to_ref[...]
        total_ref[128:, :] = jnp.zeros((D - 128, 128), f32)

    for i in range(CHIPS):
        rows = slice(STRIP * i, STRIP * (i + 1))
        out_ref[i, :, :D] = square_ref[rows, :]
        out_ref[i, :, D:] = total_ref[rows, :].astype(bf16)


def strip_kernel(parts_ref, out_ref):
    out_ref[...] = jnp.sum(parts_ref[...].astype(f32), axis=0).astype(bf16)


def part_kernel(a_ref, b_ref, c_ref, d_ref, out_ref):
    out_ref[...] = pair_sums(a_ref[...], b_ref[...], c_ref[...], d_ref[...])


def copies_kernel(a_ref, b_ref, c_ref, d_ref, out_ref):
    total = pair_sums(a_ref[...], b_ref[...], c_ref[...], d_ref[...])
    for i in range(CHIPS):
        out_ref[i] = total


VECTORS = ((0, 6), (6, 6), (12, 6), (18, 6), (24, 24), (48, 6), (54, 6), (60, 6))


def late_place_kernel(at_ref, own_ref, other_ref, query_ref, out_ref, kv_ref, value_ref, *vec_refs):
    first = at_ref[0] == 0
    vecs = []
    for a in range(CHIPS):
        rows = slice(STRIP * a, STRIP * (a + 1))
        own, other = own_ref[a].astype(f32), other_ref[a].astype(f32)
        zero, one = jnp.where(first, own, other), jnp.where(first, other, own)
        query_ref[rows, :] = zero[:, :D]
        out_ref[rows, :] = one[:, :D]
        kv_ref[rows, :] = zero[:, D:]
        if a < 2:
            vecs.append(one[:, D:])
    row = lambda i: vecs[i // STRIP][i % STRIP]
    value_ref[...] = row(66)[HD:]
    for ref, (at, count) in zip(vec_refs, VECTORS):
        for i in range(count):
            ref[i * 128 : (i + 1) * 128] = row(at + i)


def call(kernel, args, outs, scratch=(), name=None, flops=0, nbytes=2e6, after=()):
    given, extra = len(args), len(after)
    run = lambda *refs: kernel(*refs[:given], *refs[given + extra :])
    return pl.pallas_call(
        run,
        out_shape=outs,
        in_specs=[SMEM if v.dtype == jnp.int32 and v.ndim == 1 else VMEM for v in args] + [ANY] * extra,
        out_specs=jax.tree.map(lambda _: VMEM, outs),
        scratch_shapes=list(scratch),
        compiler_params=params(),
        cost_estimate=cost(flops, nbytes),
        name=name,
    )(*args, *after)


def shapes(*pairs):
    return tuple(jax.ShapeDtypeStruct(s, t) for s, t in pairs)


def positions(lengths, splits, wide_index, core):
    ends = jnp.cumsum(lengths, dtype=jnp.int32)
    starts = ends - lengths
    first = lengths * jnp.minimum(splits[:, 0], splits[:, 1]) // 1024
    second = lengths * jnp.maximum(splits[:, 0], splits[:, 1]) // 1024

    def place(row):
        shape = (1,) * row.ndim + (-1,)
        s, e, a, b, n = (v.reshape(shape) for v in (starts, ends, first, second, lengths))
        row = row[..., None]
        inside = (row >= s) & (row < e)
        u = row - s
        moved = jnp.where(u < a, u, jnp.where(u >= b, a + u - b, a + n - b + u - a))
        return (
            jnp.sum(jnp.where(inside, s + moved, 0), axis=-1, dtype=jnp.int32),
            jnp.sum(jnp.where(inside, s, 0), axis=-1, dtype=jnp.int32),
        )

    k = jnp.arange(KB, dtype=jnp.int32)[:, None, None]
    j = jnp.arange(CHIPS, dtype=jnp.int32) * 2
    j = jnp.concatenate([j + core, j + 1 - core])[None, :, None]
    r = jnp.arange(KBR, dtype=jnp.int32)[None, None, :]
    keys, _ = place(((k * KBR + r) * WIDE + j).reshape(KB, KEYS))
    own, own_start = place(jnp.arange(ROWS, dtype=jnp.int32) * WIDE + wide_index)
    low, high = jnp.min(keys, axis=1), jnp.max(keys, axis=1)
    blocks, block_starts = own.reshape(RB, RBR), own_start.reshape(RB, RBR)
    top, start_low = jnp.max(blocks, axis=1), jnp.min(block_starts, axis=1)
    bottom, start_high = jnp.min(blocks, axis=1), jnp.max(block_starts, axis=1)
    some = (low[None] <= top[:, None]) & (high[None] >= start_low[:, None])
    every = (high[None] <= bottom[:, None]) & (low[None] >= start_high[:, None])
    kinds = jnp.where(every, 2, jnp.where(some, 1, 0)).astype(jnp.int32).reshape(-1)
    return keys, own, own_start, kinds


NARROW = ((ROWS, D), bf16)
KV_HALF = ((CHIPS, ROWS, 2 * HD), bf16)


def attend(*args):
    stat = pltpu.VMEM((RB, 1, QB), f32)
    return call(
        forward_kernel, args,
        shapes(NARROW, NARROW, NARROW, ((RB, QB, 128), bf16), ((RB, QB, 128), f32), ((RB, 1, QB), f32), ((WIDE, ROWS, 2 * HD), bf16)),
        [stat, stat, pltpu.VMEM((RB, 2 * HD, QB), f32), pltpu.VMEM((2 * HD, KEYS), bf16)],
        name="attend", flops=4 * ROWS * H * WINDOW * 64, nbytes=4e6,
    )


def attend_back(*args, after=()):
    return call(
        backward_kernel, args,
        shapes(NARROW, NARROW, NARROW, KV_HALF, KV_HALF),
        [
            pltpu.VMEM((RB, QB, 128), bf16), pltpu.VMEM((RB, 8, QB), f32),
            pltpu.VMEM((RB, 128, QB), f32), pltpu.VMEM((KEYS, 2 * HD), f32), pltpu.VMEM((2 * HD, KEYS), bf16),
        ],
        name="attend_back", flops=10 * ROWS * H * WINDOW * 64, nbytes=8e6, after=after,
    )


def coords():
    x, y, z, c = (lax.axis_index(a) for a in AXES)
    first = c == 0
    at = (c, jnp.where(first, z, y), jnp.where(first, y, x), jnp.where(first, x, z), z, y)
    return jnp.stack(at).astype(jnp.int32)


QUARTER = ((D // 4, D), bf16)
HALF = ((D // 2, D), bf16)


def pair_sums(a, b, c, d):
    a, b, c, d = (v.astype(f32) for v in (a, b, c, d))
    return ((a + d) + (b + c)).astype(bf16)


def tie_kernel(v_ref, *refs):
    pass


def tie(v, *after):
    return pl.pallas_call(
        tie_kernel,
        out_shape=jax.ShapeDtypeStruct(v.shape, v.dtype),
        in_specs=[ANY] * (1 + len(after)),
        out_specs=ANY,
        input_output_aliases={0: 0},
        cost_estimate=cost(0, 0),
        name="tie",
    )(v, *after)


def corner(v):
    return swap(v[:8, :128])


def halves_kernel(before_ref, after_ref, low_ref, high_ref):
    low_ref[...] = before_ref[D // 2 :, :]
    high_ref[...] = after_ref[: D // 2, :]


def feed_forward_rest(at, before, after, kept, mark):
    low, high = call(halves_kernel, (before, after), shapes(HALF, HALF), name="halves", after=(mark,))
    before, after = tie(before, low), tie(after, high)
    low, high = send(low, 0, 1), send(high, 0, 3)
    kept = place(at, 3, before, swap(before), kept)
    kept = place(at, 1, after, swap(after), kept)
    low, high = (tie(v, kept[0]) for v in (low, high))
    kept = place(at, 2, high, swap(high), kept)
    return *place(at, 2, low, swap(low), kept, part=1), low, high


def body(block_input, file_lengths, file_splits, ln1_gain, ln1_bias, w_query, b_query, w_kv, b_value, w_out, b_out,
         ln2_gain, ln2_bias, w_up, b_up, w_down, b_down, out_cotangent):
    x = block_input.reshape(ROWS, D)
    g = out_cotangent.reshape(ROWS, D)
    wide = ("y", "z", "c")
    at = coords()
    narrow = NARROW

    n1, copies = call(enter_kernel, (x, ln1_gain, ln1_bias, w_kv, b_value), shapes(narrow, ((CHIPS, ROWS, 2 * HD), bf16)),
                      name="enter", flops=2 * ROWS * D * 128)
    kv_same = lax.all_to_all(copies, ("y", "z"), 0, 0, tiled=True)
    keys, own, own_start, kinds = positions(file_lengths[0], file_splits[0], lax.axis_index(wide), at[0])
    key_cols = jnp.broadcast_to(keys[:, :, None], (KB, KEYS, 128))
    own_lanes = jnp.tile(own.reshape(RB, 1, RBR), (1, 1, 128 // RBR))
    start_lanes = jnp.tile(own_start.reshape(RB, 1, RBR), (1, 1, 128 // RBR))
    q = call(query_kernel, (n1, w_query, b_query), shapes(narrow)[0], name="query", flops=2 * ROWS * D * D,
             after=(key_cols, own_lanes, start_lanes, kinds))
    kv_same = tie(kv_same, q)
    kv_other = swap(kv_same)

    att, left, left_send, xq, o, lse, kv_all = attend(at, kinds, q, kv_same, kv_other, key_cols, own_lanes, start_lanes, n1)
    left_other = swap(left_send)

    steps = FF // FC
    whole = lambda *s: pl.BlockSpec(s, lambda i: (0,) * len(s))
    wide_cols = pl.BlockSpec((ROWS, FC), lambda i: (0, i))
    y, big, big_send, small, small_send, gr, gb, ga, vec_mid = pl.pallas_call(
        middle_kernel,
        grid=(steps,),
        out_shape=shapes(narrow, ((ROWS, FF), bf16), ((ROWS, FF), bf16), narrow, narrow, ((ROWS, D), f32), narrow, narrow, ((48, 128), f32)),
        in_specs=[
            SMEM, whole(ROWS, D), whole(ROWS, D), whole(ROWS, D), whole(D, D), whole(D), whole(D), whole(D),
            pl.BlockSpec((D, FC), lambda i: (0, i)), pl.BlockSpec((FC,), lambda i: (i,)),
            pl.BlockSpec((FC, D), lambda i: (i, 0)), whole(D),
        ],
        out_specs=(
            whole(ROWS, D), wide_cols, wide_cols, whole(ROWS, D), whole(ROWS, D), whole(ROWS, D), whole(ROWS, D),
            whole(ROWS, D), whole(48, 128),
        ),
        scratch_shapes=[pltpu.VMEM((ROWS, D), f32)] * 3 + [pltpu.VMEM((ROWS, D), bf16)],
        compiler_params=params(),
        cost_estimate=cost(8 * ROWS * D * FF, 2e7),
        name="middle",
    )(at, att, x, g, w_out, b_out, ln2_gain, ln2_bias, w_up, b_up, w_down, b_down)

    packed = call(pack_kernel, (big, small, swap(big_send), swap(small_send)), shapes(((4, 2 * ROWS, 2 * D), bf16))[0], name="pack")
    slabs = lax.all_to_all(packed, AXES, 0, 0, axis_index_groups=ring_groups(0), tiled=True)

    gq, right, right_send, kv_grads, kv_send = attend_back(at, kinds, xq, ga, o, lse, kv_all, key_cols, own_lanes, start_lanes, gb, after=(packed,))
    shares = call(share_kernel, (kv_grads, swap(kv_send)), shapes(KV_HALF)[0], name="share", after=(slabs[0, :8, :128],))
    parts = lax.all_to_all(shares, ("y", "z"), 0, 0, tiled=True)

    pieces = pl.pallas_call(
        weight_kernel,
        grid=(4,),
        out_shape=shapes(*[QUARTER] * 4),
        in_specs=[SMEM, pl.BlockSpec((1, 2 * ROWS, 2 * D), lambda i: (i, 0, 0))],
        out_specs=(VMEM,) * 4,
        scratch_shapes=[pltpu.VMEM((D, D), f32)],
        compiler_params=params(62),
        cost_estimate=cost(0, 0),
        name="weights",
    )(at, slabs)
    ff_parts = (pieces[0],) + spread(1, *pieces[1:])
    square = call(square_kernel, (left, left_other, right, swap(right_send)), shapes(((D, D), bf16))[0], name="square")
    gin, tail, tail_send, _ = call(
        leave_kernel, (at, x, ln1_gain, w_query, w_kv, gq, gr, vec_mid, parts),
        shapes(((ROWS * D // 128, 128), f32), ((128, 128), f32), ((128, 128), f32), ((128, 128), f32)),
        name="leave", after=(pieces[0], square),
    )

    shares = call(late_kernel, (at, left, left_other, tail, swap(tail_send), square), shapes(((CHIPS, STRIP, D + 128), bf16))[0],
                  [pltpu.VMEM((D, 128), f32)], name="late", after=ff_parts[1:])
    ff_part = call(part_kernel, ff_parts, shapes(QUARTER)[0], name="part", after=(shares,))
    ff_crossed = gather4(ff_part, 2)
    late_parts = in_plane(shares)
    ff_totals = gather4(pair_sums(*ff_crossed), 1)
    strip = call(strip_kernel, (late_parts,), shapes(((STRIP, D + 128), bf16))[0], name="strip", after=ff_crossed[1:])
    u = call(join_kernel, (at,) + ff_totals, shapes(((D, D), bf16))[0], name="join", after=(strip,))
    before, after = send(u, 0, 1), send(u, 0, 3)
    kept = place(at, 0, u, swap(u), ())
    mark = corner(kept[0])
    copies = call(copies_kernel, gather4(strip, 3), shapes(((CHIPS, STRIP, D + 128), bf16))[0], name="copies",
                  after=(before, after, mark))
    late = in_plane(copies)
    g_down, g_up, *rest = feed_forward_rest(at, before, after, kept, mark)
    late = tie(late, *rest)
    one = lambda n: ((n,), f32)
    outs = call(
        late_place_kernel, (at, late, swap(late)),
        shapes(((D, D), f32), ((D, D), f32), ((D, 128), f32), one(HD), *[one(128 * n) for _, n in VECTORS]), name="late_place",
    )
    g_query, g_out, g_kv, g_value, g_bdown, g_gain2, g_bias2, g_bout, g_bup, g_gain1, g_bias1, g_bq = outs
    shape = block_input.shape
    return (
        y.reshape(shape), gin.reshape(shape), g_gain1, g_bias1, g_query, g_bq, g_kv, g_value,
        g_out, g_bout, g_gain2, g_bias2, g_up, g_bup, g_down, g_bdown,
    )


def solution(mesh):
    split = P("x", None, ("y", "z", "c"), None)
    return jax.shard_map(
        body,
        mesh=Mesh(mesh.devices.reshape(4, 4, 4, 2), AXES),
        in_specs=(split, P("x", None), P("x", None, None)) + (P(),) * 14 + (split,),
        out_specs=(split, split) + (P(),) * 14,
        check_vma=False,
    )
```

```python
import itertools

import jax
import jax.numpy as jnp
from jax import lax
from jax.experimental import pallas as pl
from jax.experimental.pallas import tpu as pltpu
from jax.sharding import Mesh, PartitionSpec as P

EPS = 1e-05
MASKED = -1e30
ROWS = 128
WIDE = 32
CHIPS = 16
D = 768
H = 12
HD = 64
FF = 3072
WINDOW = ROWS * WIDE
RB = 2
RBR = ROWS // RB
QB = RBR * H
KB = 4
KBR = ROWS // KB
KEYS = WINDOW // KB
STRIP = D // CHIPS
FC = 1024
VMEM = pl.BlockSpec(memory_space=pltpu.VMEM)
SMEM = pl.BlockSpec(memory_space=pltpu.SMEM)
ANY = pl.BlockSpec(memory_space=pl.ANY)
f32 = jnp.float32
bf16 = jnp.bfloat16


def params(limit=56):
    return pltpu.CompilerParams(vmem_limit_bytes=limit * 1024 * 1024)


def cost(flops, nbytes):
    return pl.CostEstimate(flops=1, bytes_accessed=1, transcendentals=0)


def dot(a, b):
    return jnp.dot(a, b, preferred_element_type=f32)


def dot_nt(a, b):
    return lax.dot_general(a, b, (((1,), (1,)), ((), ())), preferred_element_type=f32)


def dot_tn(a, b):
    return lax.dot_general(a, b, (((0,), (0,)), ((), ())), preferred_element_type=f32)


def norm_parts(x):
    mean = jnp.mean(x, axis=-1, keepdims=True)
    centered = x - mean
    var = jnp.mean(centered * centered, axis=-1, keepdims=True)
    rstd = lax.rsqrt(var + EPS)
    return centered * rstd, rstd


def norm_back(e, n, rstd, gain):
    m = e * gain
    return rstd * (
        m - jnp.mean(m, axis=-1, keepdims=True) - n * jnp.mean(m * n, axis=-1, keepdims=True)
    )


AXES = ("x", "y", "z", "c")
ORDER = ((2, 1, 0, 0), (1, 0, 2, 2))
FROM = (0, 3, 1, 2)


def ring(place, shift):
    pairs = []
    for at in itertools.product(range(4), range(4), range(4), range(2)):
        to = list(at)
        axis = ORDER[at[3]][place]
        to[axis] = (to[axis] + shift) % 4
        index = lambda v: ((v[0] * 4 + v[1]) * 4 + v[2]) * 2 + v[3]
        pairs.append((index(at), index(to)))
    return pairs


def groups_by(key):
    groups = {}
    for at in itertools.product(range(4), range(4), range(4), range(2)):
        groups.setdefault(key(at), []).append(((at[0] * 4 + at[1]) * 4 + at[2]) * 2 + at[3])
    return list(groups.values())


def ring_groups(place):
    return groups_by(lambda at: tuple(-1 if i == ORDER[at[3]][place] else v for i, v in enumerate(at)))


def in_plane(v):
    planes = groups_by(lambda at: (at[ORDER[at[3]][3]], at[3]))
    return lax.all_to_all(v, AXES, 0, 0, axis_index_groups=planes, tiled=True)


def send(v, place, shift):
    return lax.ppermute(v, AXES, ring(place, shift))


def swap(v):
    return lax.ppermute(v, "c", [(0, 1), (1, 0)])


def spread(place, plus, minus, far):
    return send(plus, place, 1), send(minus, place, 3), send(far, place, 2)


def gather4(v, place):
    return (v,) + spread(place, v, v, v)


def lanes_low(shape):
    return lax.broadcasted_iota(jnp.int32, shape, len(shape) - 1) < HD


def vec(ref):
    return ref[...].astype(f32).reshape(1, -1)


def enter_kernel(x_ref, gain_ref, bias_ref, wkv_ref, bv_ref, n1_ref, kv_ref):
    n, _ = norm_parts(x_ref[...].astype(f32))
    n1 = (n * vec(gain_ref) + vec(bias_ref)).astype(bf16)
    n1_ref[...] = n1
    shift = jnp.concatenate([jnp.zeros((1, HD), f32), vec(bv_ref)], axis=1)
    kv = (dot(n1, wkv_ref[...]) + shift).astype(bf16)
    for i in range(CHIPS):
        kv_ref[i] = kv


def query_kernel(n1_ref, wq_ref, bq_ref, q_ref):
    q_ref[...] = (dot(n1_ref[...], wq_ref[...]) + vec(bq_ref)).astype(bf16)


def block_bias(kp, sp, st):
    bias = jnp.where((kp <= sp) & (kp >= st), 0.0, MASKED)
    return jnp.concatenate([bias] * (QB // 128), axis=1)


def visit(cls_ref, kb, step):
    def row_block(rb, _):
        kind = cls_ref[rb * KB + kb]

        @pl.when(kind == 2)
        def _():
            step(rb, False)

        @pl.when(kind == 1)
        def _():
            step(rb, True)

        return 0

    lax.fori_loop(0, RB, row_block, 0)


def forward_kernel(at_ref, cls_ref, q_ref, same_ref, other_ref, kpb_ref, spl_ref, stl_ref, n1_ref,
                   att_ref, keep_ref, send_ref, x_ref, o_ref, lse_ref, kv_ref, m_ref, l_ref, acc_ref, kt_ref):
    kv_ref[:CHIPS] = same_ref[...]
    kv_ref[CHIPS:] = other_ref[...]
    low = lanes_low((ROWS, 2 * HD))
    for h in range(H):
        pair = q_ref[:, (h // 2) * 128 : (h // 2) * 128 + 128].astype(f32) * 0.125
        if h % 2:
            pair = pltpu.roll(pair, HD, 1)
        head = jnp.where(low, pair, 0.0).astype(bf16)
        for rb in range(RB):
            x_ref[rb, h * RBR : (h + 1) * RBR, :] = head[rb * RBR : (rb + 1) * RBR, :]
    m_ref[...] = jnp.full((RB, 1, QB), MASKED, f32)
    l_ref[...] = jnp.zeros((RB, 1, QB), f32)
    acc_ref[...] = jnp.zeros((RB, 2 * HD, QB), f32)

    def key_block(kb, _):
        cols = pl.ds(pl.multiple_of(kb * KBR, KBR), KBR)
        kt_ref[...] = jnp.transpose(kv_ref[:, cols, :].reshape(KEYS, 2 * HD).astype(f32)).astype(bf16)

        def step(rb, masked):
            s = dot_nt(kv_ref[:, cols, :].reshape(KEYS, 2 * HD), x_ref[rb])
            if masked:
                s = s + block_bias(kpb_ref[kb], spl_ref[rb], stl_ref[rb])
            m_old = m_ref[rb]
            m_new = jnp.maximum(m_old, jnp.max(s, axis=0, keepdims=True))
            alpha = jnp.exp(m_old - m_new)
            p = jnp.exp(s - m_new)
            l_ref[rb] = l_ref[rb] * alpha + jnp.sum(p, axis=0, keepdims=True)
            acc_ref[rb] = acc_ref[rb] * alpha + dot(kt_ref[...], p.astype(bf16))
            m_ref[rb] = m_new

        visit(cls_ref, kb, step)
        return 0

    lax.fori_loop(0, KB, key_block, 0)
    keep = lanes_low((RBR, 2 * HD))
    first = at_ref[0] == 0
    for rb in range(RB):
        rows = slice(rb * RBR, (rb + 1) * RBR)
        l = l_ref[rb]
        lse_ref[rb] = m_ref[rb] + jnp.log(l)
        out = jnp.transpose(acc_ref[rb] / l)
        o_ref[rb] = out
        for h in range(0, H, 2):
            even = out[h * RBR : (h + 1) * RBR, :]
            odd = out[(h + 1) * RBR : (h + 2) * RBR, :]
            att_ref[rows, h * HD : (h + 2) * HD] = jnp.where(keep, pltpu.roll(even, HD, 1), odd).astype(bf16)
    n1, att = n1_ref[...], att_ref[...]
    keep_ref[...] = jnp.where(first, n1, att)
    send_ref[...] = jnp.where(first, att, n1)


def backward_kernel(at_ref, cls_ref, x_ref, do_ref, o_ref, lse_ref, kv_ref, kpb_ref, spl_ref, stl_ref, gb_ref,
                    dq_ref, keep_ref, send_ref, same_ref, other_ref, y_ref, drow_ref, dqt_ref, acc_ref, kt_ref):
    low = lanes_low((ROWS, 2 * HD))
    for h in range(H):
        pair = do_ref[:, (h // 2) * 128 : (h // 2) * 128 + 128].astype(f32)
        if h % 2 == 0:
            pair = pltpu.roll(pair, HD, 1)
        head = jnp.where(low, 0.0, pair).astype(bf16)
        for rb in range(RB):
            y_ref[rb, h * RBR : (h + 1) * RBR, :] = head[rb * RBR : (rb + 1) * RBR, :]
    for rb in range(RB):
        delta = jnp.sum(y_ref[rb].astype(f32) * o_ref[rb], axis=1, keepdims=True)
        drow_ref[rb] = jnp.transpose(jnp.broadcast_to(delta, (QB, 128)))[:8]
    dqt_ref[...] = jnp.zeros((RB, 128, QB), f32)

    def key_block(kb, _):
        cols = pl.ds(pl.multiple_of(kb * KBR, KBR), KBR)
        kvb = kv_ref[:, cols, :].reshape(KEYS, 2 * HD)
        kt_ref[...] = jnp.transpose(kvb.astype(f32)).astype(bf16)
        acc_ref[...] = jnp.zeros((KEYS, 2 * HD), f32)

        def step(rb, masked):
            kvb = kv_ref[:, cols, :].reshape(KEYS, 2 * HD)
            xb, yb = x_ref[rb], y_ref[rb]
            s = dot_nt(kvb, xb)
            if masked:
                s = s + block_bias(kpb_ref[kb], spl_ref[rb], stl_ref[rb])
            p = jnp.exp(s - lse_ref[rb])
            ds = (p * (dot_nt(kvb, yb) - drow_ref[rb, :1])).astype(bf16)
            acc_ref[...] += dot(ds, xb) + dot(p.astype(bf16), yb)
            dqt_ref[rb] += dot(kt_ref[...], ds)

        visit(cls_ref, kb, step)
        sums = acc_ref[...].reshape(WIDE, KBR, 2 * HD).astype(bf16)
        same_ref[:, cols, :] = sums[:CHIPS]
        other_ref[:, cols, :] = sums[CHIPS:]
        return 0

    lax.fori_loop(0, KB, key_block, 0)
    keep = lanes_low((RBR, 2 * HD))
    for rb in range(RB):
        dq = jnp.transpose(dqt_ref[rb]) * 0.125
        for h in range(0, H, 2):
            even = dq[h * RBR : (h + 1) * RBR, :]
            odd = dq[(h + 1) * RBR : (h + 2) * RBR, :]
            dq_ref[rb * RBR : (rb + 1) * RBR, h * HD : (h + 2) * HD] = jnp.where(
                keep, even, pltpu.roll(odd, HD, 1)
            ).astype(bf16)
    first = at_ref[0] == 0
    dq, gb = dq_ref[...], gb_ref[...]
    keep_ref[...] = jnp.where(first, dq, gb)
    send_ref[...] = jnp.where(first, gb, dq)


def put_rows(ref, at, row):
    for i in range(row.shape[1] // 128):
        ref[pl.ds(at + i, 1), :] = row[:, i * 128 : (i + 1) * 128]


def middle_kernel(at_ref, att_ref, x_ref, g_ref, wout_ref, bout_ref, gain_ref, bias_ref, wup_ref, bup_ref, wdown_ref, bdown_ref,
                  y_ref, bk_ref, bs_ref, sk_ref, ss_ref, gr_ref, gb_ref, ga_ref, vec_ref,
                  resid_ref, out_ref, gn2_ref, n2_ref):
    step = pl.program_id(0)
    first = at_ref[0] == 0

    @pl.when(step == 0)
    def _():
        resid = x_ref[...].astype(f32) + (dot(att_ref[...], wout_ref[...]) + vec(bout_ref))
        resid_ref[...] = resid
        n, _ = norm_parts(resid)
        n2 = (n * vec(gain_ref) + vec(bias_ref)).astype(bf16)
        n2_ref[...] = n2
        sk_ref[...] = jnp.where(first, g_ref[...], n2)
        ss_ref[...] = jnp.where(first, n2, g_ref[...])
        out_ref[...] = jnp.zeros_like(out_ref)
        gn2_ref[...] = jnp.zeros_like(gn2_ref)

    g = g_ref[...]
    pre = dot(n2_ref[...], wup_ref[...]) + vec(bup_ref)
    sq = pre * pre
    t = jnp.tanh(0.7978845608028654 * (pre + 0.044715 * sq * pre))
    half = 0.5 + 0.5 * t
    act = (pre * half).astype(bf16)
    slope = half + (0.5 * 0.7978845608028654) * pre * (1.0 - t * t) * (1.0 + (3 * 0.044715) * sq)
    gp = (slope * dot_nt(g, wdown_ref[...])).astype(bf16)
    bk_ref[...] = jnp.where(first, act, gp)
    bs_ref[...] = jnp.where(first, gp, act)
    put_rows(vec_ref, 24 + step * (FC // 128), jnp.sum(gp.astype(f32), axis=0, keepdims=True))
    out_ref[...] += dot(act, wdown_ref[...])
    gn2_ref[...] += dot_nt(gp, wup_ref[...])

    @pl.when(step == pl.num_programs(0) - 1)
    def _():
        resid = resid_ref[...]
        gf = g.astype(f32)
        y_ref[...] = (resid + (out_ref[...] + vec(bdown_ref))).astype(bf16)
        n, rstd = norm_parts(resid)
        e = gn2_ref[...]
        gr = gf + norm_back(e, n, rstd, vec(gain_ref))
        gr_ref[...] = gr
        gb = gr.astype(bf16)
        gb_ref[...] = gb
        ga_ref[...] = dot_nt(gb, wout_ref[...]).astype(bf16)
        put_rows(vec_ref, 0, jnp.sum(gf, axis=0, keepdims=True))
        put_rows(vec_ref, 6, jnp.sum(e * n, axis=0, keepdims=True))
        put_rows(vec_ref, 12, jnp.sum(e, axis=0, keepdims=True))
        put_rows(vec_ref, 18, jnp.sum(gb.astype(f32), axis=0, keepdims=True))


def leave_kernel(at_ref, x_ref, gain_ref, wq_ref, wkv_ref, gq_ref, gr_ref, mid_ref, parts_ref, gin_ref, keep_ref, send_ref, vec_ref):
    gkv = jnp.sum(parts_ref[...].astype(f32), axis=0).astype(bf16)
    gq = gq_ref[...]
    e = dot_nt(gq, wq_ref[...]) + dot_nt(gkv, wkv_ref[...])
    n, rstd = norm_parts(x_ref[...].astype(f32))
    gin = gr_ref[...] + norm_back(e, n, rstd, vec(gain_ref))
    for i in range(D // 128):
        gin_ref[pl.ds(i, ROWS, stride=D // 128), :] = gin[:, i * 128 : (i + 1) * 128]
    gkv = gkv.astype(f32)
    vec_ref[0:48, :] = mid_ref[...]
    vec_ref[48:128, :] = jnp.zeros((80, 128), f32)
    put_rows(vec_ref, 48, jnp.sum(e * n, axis=0, keepdims=True))
    put_rows(vec_ref, 54, jnp.sum(e, axis=0, keepdims=True))
    put_rows(vec_ref, 60, jnp.sum(gq.astype(f32), axis=0, keepdims=True))
    put_rows(vec_ref, 66, jnp.sum(gkv, axis=0, keepdims=True))
    first = at_ref[0] == 0
    vecs = vec_ref[...]
    keep_ref[...] = jnp.where(first, gkv, vecs)
    send_ref[...] = jnp.where(first, vecs, gkv)


def pack_kernel(bk_ref, sk_ref, bp_ref, sp_ref, out_ref):
    for i in range(4):
        cols = slice(i * D, (i + 1) * D)
        out_ref[i, 0:ROWS, 0:D] = bk_ref[:, cols]
        out_ref[i, ROWS:, 0:D] = bp_ref[:, cols]
        out_ref[i, 0:ROWS, D:] = sk_ref[...]
        out_ref[i, ROWS:, D:] = sp_ref[...]

def quarters(at, which, total_ref, outs):
    rows = total_ref.shape[0]//4
    for rel, out in zip((0,1,3,2), outs):
        out[...] = total_ref[pl.ds(pl.multiple_of(((at[which]+rel)&3)*rows, rows), rows), :].astype(out.dtype)

def weight_kernel(at_ref, slab_ref, own_ref, plus_ref, minus_ref, far_ref, total_ref):
    step = pl.program_id(0)

    @pl.when(step == 0)
    def _():
        total_ref[...] = jnp.zeros_like(total_ref)

    @pl.when(at_ref[0] == 0)
    def _():
        total_ref[...] += dot_tn(slab_ref[0, :, :D], slab_ref[0, :, D:])

    @pl.when(at_ref[0] == 1)
    def _():
        total_ref[...] += dot_tn(slab_ref[0, :, D:], slab_ref[0, :, :D])

    @pl.when(step == pl.num_programs(0) - 1)
    def _():
        quarters(at_ref, 2, total_ref, (own_ref, plus_ref, minus_ref, far_ref))


def join_kernel(at_ref,a_ref,b_ref,c_ref,d_ref,out_ref):
    rows=a_ref.shape[0]
    for rel, v in zip(FROM,(a_ref,b_ref,c_ref,d_ref)):
        out_ref[pl.ds(pl.multiple_of(((at_ref[2]+rel)&3)*rows,rows),rows),:] = v[...]

def place_kernel(at_ref, own_ref, other_ref, *rest):
    down_ref, up_ref = rest[-2:]
    first = at_ref[0]==0
    own, other = own_ref[...], other_ref[...]
    down_ref[...] = jnp.where(first, own, other).astype(f32)
    up_ref[...] = jnp.where(first, other, own).astype(f32)

def place(at, rel, own, other, kept):
    tile = D // 2
    piece = pl.BlockSpec((tile, D), lambda i, at: (i, 0))
    outs = (
        pl.BlockSpec((tile, D), lambda i, at: (((at[4] + rel) & 3) * 2 + i, 0)),
        pl.BlockSpec((tile, D), lambda i, at: (i, (at[5] + rel) & 3)),
    )
    return pl.pallas_call(
        place_kernel,
        grid_spec=pltpu.PrefetchScalarGridSpec(
            num_scalar_prefetch=1, grid=(2,), in_specs=[piece, piece] + [ANY] * len(kept), out_specs=outs
        ),
        out_shape=shapes(((FF, D), f32), ((D, FF), f32)),
        input_output_aliases={3: 0, 4: 1} if kept else {},
        compiler_params=params(62),
        cost_estimate=cost(0, 0),
        name="place",
    )(at, own, other, *kept)


def share_kernel(same_ref, other_ref, out_ref):
    out_ref[...] = (same_ref[...].astype(f32) + other_ref[...].astype(f32)).astype(bf16)


def square_kernel(lk_ref, lo_ref, rk_ref, ro_ref, out_ref):
    out_ref[...] = (dot_tn(lk_ref[...], rk_ref[...]) + dot_tn(lo_ref[...], ro_ref[...])).astype(bf16)


def late_kernel(at_ref, lk_ref, lo_ref, tk_ref, to_ref, square_ref, out_ref, total_ref):
    first = at_ref[0] == 0

    @pl.when(first)
    def _():
        total_ref[...] = dot_tn(lk_ref[...], tk_ref[...].astype(bf16)) + dot_tn(lo_ref[...], to_ref[...].astype(bf16))

    @pl.when(jnp.logical_not(first))
    def _():
        total_ref[0:128, :] = tk_ref[...] + to_ref[...]
        total_ref[128:, :] = jnp.zeros((D - 128, 128), f32)

    for i in range(CHIPS):
        rows = slice(STRIP * i, STRIP * (i + 1))
        out_ref[i, :, :D] = square_ref[rows, :]
        out_ref[i, :, D:] = total_ref[rows, :].astype(bf16)


def strip_kernel(parts_ref, out_ref):
    out_ref[...] = jnp.sum(parts_ref[...].astype(f32), axis=0).astype(bf16)


def part_kernel(a_ref, b_ref, c_ref, d_ref, out_ref):
    out_ref[...] = pair_sums(a_ref[...], b_ref[...], c_ref[...], d_ref[...])


def copies_kernel(a_ref, b_ref, c_ref, d_ref, out_ref):
    total = pair_sums(a_ref[...], b_ref[...], c_ref[...], d_ref[...])
    for i in range(CHIPS):
        out_ref[i] = total


VECTORS = ((0, 6), (6, 6), (12, 6), (18, 6), (24, 24), (48, 6), (54, 6), (60, 6))


def late_place_kernel(at_ref, own_ref, other_ref, query_ref, out_ref, kv_ref, value_ref, *vec_refs):
    first = at_ref[0] == 0
    vecs = []
    for a in range(CHIPS):
        rows = slice(STRIP * a, STRIP * (a + 1))
        own, other = own_ref[a].astype(f32), other_ref[a].astype(f32)
        zero, one = jnp.where(first, own, other), jnp.where(first, other, own)
        query_ref[rows, :] = zero[:, :D]
        out_ref[rows, :] = one[:, :D]
        kv_ref[rows, :] = zero[:, D:]
        if a < 2:
            vecs.append(one[:, D:])
    row = lambda i: vecs[i // STRIP][i % STRIP]
    value_ref[...] = row(66)[HD:]
    for ref, (at, count) in zip(vec_refs, VECTORS):
        for i in range(count):
            ref[i * 128 : (i + 1) * 128] = row(at + i)


def call(kernel, args, outs, scratch=(), name=None, flops=0, nbytes=2e6, after=()):
    given, extra = len(args), len(after)
    run = lambda *refs: kernel(*refs[:given], *refs[given + extra :])
    return pl.pallas_call(
        run,
        out_shape=outs,
        in_specs=[SMEM if v.dtype == jnp.int32 and v.ndim == 1 else VMEM for v in args] + [ANY] * extra,
        out_specs=jax.tree.map(lambda _: VMEM, outs),
        scratch_shapes=list(scratch),
        compiler_params=params(),
        cost_estimate=cost(flops, nbytes),
        name=name,
    )(*args, *after)


def shapes(*pairs):
    return tuple(jax.ShapeDtypeStruct(s, t) for s, t in pairs)


def positions(lengths, splits, wide_index, core):
    ends = jnp.cumsum(lengths, dtype=jnp.int32)
    starts = ends - lengths
    first = lengths * jnp.minimum(splits[:, 0], splits[:, 1]) // 1024
    second = lengths * jnp.maximum(splits[:, 0], splits[:, 1]) // 1024

    def place(row):
        shape = (1,) * row.ndim + (-1,)
        s, e, a, b, n = (v.reshape(shape) for v in (starts, ends, first, second, lengths))
        row = row[..., None]
        inside = (row >= s) & (row < e)
        u = row - s
        moved = jnp.where(u < a, u, jnp.where(u >= b, a + u - b, a + n - b + u - a))
        return (
            jnp.sum(jnp.where(inside, s + moved, 0), axis=-1, dtype=jnp.int32),
            jnp.sum(jnp.where(inside, s, 0), axis=-1, dtype=jnp.int32),
        )

    k = jnp.arange(KB, dtype=jnp.int32)[:, None, None]
    j = jnp.arange(CHIPS, dtype=jnp.int32) * 2
    j = jnp.concatenate([j + core, j + 1 - core])[None, :, None]
    r = jnp.arange(KBR, dtype=jnp.int32)[None, None, :]
    keys, _ = place(((k * KBR + r) * WIDE + j).reshape(KB, KEYS))
    own, own_start = place(jnp.arange(ROWS, dtype=jnp.int32) * WIDE + wide_index)
    low, high = jnp.min(keys, axis=1), jnp.max(keys, axis=1)
    blocks, block_starts = own.reshape(RB, RBR), own_start.reshape(RB, RBR)
    top, start_low = jnp.max(blocks, axis=1), jnp.min(block_starts, axis=1)
    bottom, start_high = jnp.min(blocks, axis=1), jnp.max(block_starts, axis=1)
    some = (low[None] <= top[:, None]) & (high[None] >= start_low[:, None])
    every = (high[None] <= bottom[:, None]) & (low[None] >= start_high[:, None])
    kinds = jnp.where(every, 2, jnp.where(some, 1, 0)).astype(jnp.int32).reshape(-1)
    return keys, own, own_start, kinds


NARROW = ((ROWS, D), bf16)
KV_HALF = ((CHIPS, ROWS, 2 * HD), bf16)


def attend(*args):
    stat = pltpu.VMEM((RB, 1, QB), f32)
    return call(
        forward_kernel, args,
        shapes(NARROW, NARROW, NARROW, ((RB, QB, 128), bf16), ((RB, QB, 128), f32), ((RB, 1, QB), f32), ((WIDE, ROWS, 2 * HD), bf16)),
        [stat, stat, pltpu.VMEM((RB, 2 * HD, QB), f32), pltpu.VMEM((2 * HD, KEYS), bf16)],
        name="attend", flops=4 * ROWS * H * WINDOW * 64, nbytes=4e6,
    )


def attend_back(*args, after=()):
    return call(
        backward_kernel, args,
        shapes(NARROW, NARROW, NARROW, KV_HALF, KV_HALF),
        [
            pltpu.VMEM((RB, QB, 128), bf16), pltpu.VMEM((RB, 8, QB), f32),
            pltpu.VMEM((RB, 128, QB), f32), pltpu.VMEM((KEYS, 2 * HD), f32), pltpu.VMEM((2 * HD, KEYS), bf16),
        ],
        name="attend_back", flops=10 * ROWS * H * WINDOW * 64, nbytes=8e6, after=after,
    )


def coords():
    x, y, z, c = (lax.axis_index(a) for a in AXES)
    first = c == 0
    at = (c, jnp.where(first, z, y), jnp.where(first, y, x), jnp.where(first, x, z), z, y)
    return jnp.stack(at).astype(jnp.int32)


QUARTER = ((D // 4, D), bf16)


def pair_sums(a, b, c, d):
    a, b, c, d = (v.astype(f32) for v in (a, b, c, d))
    return ((a + d) + (b + c)).astype(bf16)


def tie_kernel(v_ref, *refs):
    pass


def tie(v, *after):
    return pl.pallas_call(
        tie_kernel,
        out_shape=jax.ShapeDtypeStruct(v.shape, v.dtype),
        in_specs=[ANY] * (1 + len(after)),
        out_specs=ANY,
        input_output_aliases={0: 0},
        cost_estimate=cost(0, 0),
        name="tie",
    )(v, *after)


def corner(v):
    return swap(v[:8, :128])


def body(block_input, file_lengths, file_splits, ln1_gain, ln1_bias, w_query, b_query, w_kv, b_value, w_out, b_out,
         ln2_gain, ln2_bias, w_up, b_up, w_down, b_down, out_cotangent):
    x = block_input.reshape(ROWS, D)
    g = out_cotangent.reshape(ROWS, D)
    wide = ("y", "z", "c")
    at = coords()
    narrow = NARROW

    n1, copies = call(enter_kernel, (x, ln1_gain, ln1_bias, w_kv, b_value), shapes(narrow, ((CHIPS, ROWS, 2 * HD), bf16)),
                      name="enter", flops=2 * ROWS * D * 128)
    kv_same = lax.all_to_all(copies, ("y", "z"), 0, 0, tiled=True)
    keys, own, own_start, kinds = positions(file_lengths[0], file_splits[0], lax.axis_index(wide), at[0])
    key_cols = jnp.broadcast_to(keys[:, :, None], (KB, KEYS, 128))
    own_lanes = jnp.tile(own.reshape(RB, 1, RBR), (1, 1, 128 // RBR))
    start_lanes = jnp.tile(own_start.reshape(RB, 1, RBR), (1, 1, 128 // RBR))
    q = call(query_kernel, (n1, w_query, b_query), shapes(narrow)[0], name="query", flops=2 * ROWS * D * D,
             after=(key_cols, own_lanes, start_lanes, kinds))
    kv_same = tie(kv_same, q)
    kv_other = swap(kv_same)

    att, left, left_send, xq, o, lse, kv_all = attend(at, kinds, q, kv_same, kv_other, key_cols, own_lanes, start_lanes, n1)
    left_other = swap(left_send)

    steps = FF // FC
    whole = lambda *s: pl.BlockSpec(s, lambda i: (0,) * len(s))
    wide_cols = pl.BlockSpec((ROWS, FC), lambda i: (0, i))
    y, big, big_send, small, small_send, gr, gb, ga, vec_mid = pl.pallas_call(
        middle_kernel,
        grid=(steps,),
        out_shape=shapes(narrow, ((ROWS, FF), bf16), ((ROWS, FF), bf16), narrow, narrow, ((ROWS, D), f32), narrow, narrow, ((48, 128), f32)),
        in_specs=[
            SMEM, whole(ROWS, D), whole(ROWS, D), whole(ROWS, D), whole(D, D), whole(D), whole(D), whole(D),
            pl.BlockSpec((D, FC), lambda i: (0, i)), pl.BlockSpec((FC,), lambda i: (i,)),
            pl.BlockSpec((FC, D), lambda i: (i, 0)), whole(D),
        ],
        out_specs=(
            whole(ROWS, D), wide_cols, wide_cols, whole(ROWS, D), whole(ROWS, D), whole(ROWS, D), whole(ROWS, D),
            whole(ROWS, D), whole(48, 128),
        ),
        scratch_shapes=[pltpu.VMEM((ROWS, D), f32)] * 3 + [pltpu.VMEM((ROWS, D), bf16)],
        compiler_params=params(),
        cost_estimate=cost(8 * ROWS * D * FF, 2e7),
        name="middle",
    )(at, att, x, g, w_out, b_out, ln2_gain, ln2_bias, w_up, b_up, w_down, b_down)

    packed = call(pack_kernel, (big, small, swap(big_send), swap(small_send)), shapes(((4, 2 * ROWS, 2 * D), bf16))[0], name="pack")
    slabs = lax.all_to_all(packed, AXES, 0, 0, axis_index_groups=ring_groups(0), tiled=True)

    gq, right, right_send, kv_grads, kv_send = attend_back(at, kinds, xq, ga, o, lse, kv_all, key_cols, own_lanes, start_lanes, gb, after=(packed,))
    shares = call(share_kernel, (kv_grads, swap(kv_send)), shapes(KV_HALF)[0], name="share", after=(slabs[0, :8, :128],))
    parts = lax.all_to_all(shares, ("y", "z"), 0, 0, tiled=True)

    pieces = pl.pallas_call(
        weight_kernel,
        grid=(4,),
        out_shape=shapes(*[QUARTER] * 4),
        in_specs=[SMEM, pl.BlockSpec((1, 2 * ROWS, 2 * D), lambda i: (i, 0, 0))],
        out_specs=(VMEM,) * 4,
        scratch_shapes=[pltpu.VMEM((D, D), f32)],
        compiler_params=params(62),
        cost_estimate=cost(0, 0),
        name="weights",
    )(at, slabs)
    ff_parts = (pieces[0],) + spread(1, *pieces[1:])
    square = call(square_kernel, (left, left_other, right, swap(right_send)), shapes(((D, D), bf16))[0], name="square")
    gin, tail, tail_send, _ = call(
        leave_kernel, (at, x, ln1_gain, w_query, w_kv, gq, gr, vec_mid, parts),
        shapes(((ROWS * D // 128, 128), f32), ((128, 128), f32), ((128, 128), f32), ((128, 128), f32)),
        name="leave", after=(pieces[0], square),
    )

    shares = call(late_kernel, (at, left, left_other, tail, swap(tail_send), square), shapes(((CHIPS, STRIP, D + 128), bf16))[0],
                  [pltpu.VMEM((D, 128), f32)], name="late", after=ff_parts[1:])
    ff_part = call(part_kernel, ff_parts, shapes(QUARTER)[0], name="part", after=(shares,))
    ff_crossed = gather4(ff_part, 2)
    late_parts = in_plane(shares)
    ff_totals = gather4(pair_sums(*ff_crossed), 1)
    strip = call(strip_kernel, (late_parts,), shapes(((STRIP, D + 128), bf16))[0], name="strip", after=ff_crossed[1:])
    u = call(join_kernel, (at,) + ff_totals, shapes(((D, D), bf16))[0], name="join", after=(strip,))
    before, after, far = spread(0, u, u, u)
    kept = place(at, 0, u, swap(u), ())
    mark = corner(kept[0])
    copies = call(copies_kernel, gather4(strip, 3), shapes(((CHIPS, STRIP, D + 128), bf16))[0], name="copies",
                  after=(before, after, far, mark))
    late = in_plane(copies)
    before, after, far = (tie(v, copies) for v in (before, after, far))
    kept = place(at, 3, before, swap(before), kept)
    kept = place(at, 1, after, swap(after), kept)
    g_down, g_up = place(at, 2, far, swap(far), kept)
    late = tie(late, corner(g_down))
    one = lambda n: ((n,), f32)
    outs = call(
        late_place_kernel, (at, late, swap(late)),
        shapes(((D, D), f32), ((D, D), f32), ((D, 128), f32), one(HD), *[one(128 * n) for _, n in VECTORS]), name="late_place",
    )
    g_query, g_out, g_kv, g_value, g_bdown, g_gain2, g_bias2, g_bout, g_bup, g_gain1, g_bias1, g_bq = outs
    shape = block_input.shape
    return (
        y.reshape(shape), gin.reshape(shape), g_gain1, g_bias1, g_query, g_bq, g_kv, g_value,
        g_out, g_bout, g_gain2, g_bias2, g_up, g_bup, g_down, g_bdown,
    )


def solution(mesh):
    split = P("x", None, ("y", "z", "c"), None)
    return jax.shard_map(
        body,
        mesh=Mesh(mesh.devices.reshape(4, 4, 4, 2), AXES),
        in_specs=(split, P("x", None), P("x", None, None)) + (P(),) * 14 + (split,),
        out_specs=(split, split) + (P(),) * 14,
        check_vma=False,
    )
```

```python
import itertools

import jax
import jax.numpy as jnp
from jax import lax
from jax.experimental import pallas as pl
from jax.experimental.pallas import tpu as pltpu
from jax.sharding import Mesh, PartitionSpec as P

EPS = 1e-05
MASKED = -1e30
ROWS = 128
WIDE = 32
CHIPS = 16
D = 768
H = 12
HD = 64
FF = 3072
WINDOW = ROWS * WIDE
RB = 2
RBR = ROWS // RB
QB = RBR * H
KB = 4
KBR = ROWS // KB
KEYS = WINDOW // KB
STRIP = D // CHIPS
FC = 1024
VMEM = pl.BlockSpec(memory_space=pltpu.VMEM)
SMEM = pl.BlockSpec(memory_space=pltpu.SMEM)
ANY = pl.BlockSpec(memory_space=pl.ANY)
f32 = jnp.float32
bf16 = jnp.bfloat16


def params(limit=56):
    return pltpu.CompilerParams(vmem_limit_bytes=limit * 1024 * 1024)


def cost(flops, nbytes):
    return pl.CostEstimate(flops=1, bytes_accessed=1, transcendentals=0)


def dot(a, b):
    return jnp.dot(a, b, preferred_element_type=f32)


def dot_nt(a, b):
    return lax.dot_general(a, b, (((1,), (1,)), ((), ())), preferred_element_type=f32)


def dot_tn(a, b):
    return lax.dot_general(a, b, (((0,), (0,)), ((), ())), preferred_element_type=f32)


def norm_parts(x):
    mean = jnp.mean(x, axis=-1, keepdims=True)
    centered = x - mean
    var = jnp.mean(centered * centered, axis=-1, keepdims=True)
    rstd = lax.rsqrt(var + EPS)
    return centered * rstd, rstd


def norm_back(e, n, rstd, gain):
    m = e * gain
    return rstd * (
        m - jnp.mean(m, axis=-1, keepdims=True) - n * jnp.mean(m * n, axis=-1, keepdims=True)
    )


AXES = ("x", "y", "z", "c")
ORDER = ((2, 1, 0, 0), (1, 0, 2, 2))
FROM = (0, 3, 1, 2)


def ring(place, shift):
    pairs = []
    for at in itertools.product(range(4), range(4), range(4), range(2)):
        to = list(at)
        axis = ORDER[at[3]][place]
        to[axis] = (to[axis] + shift) % 4
        index = lambda v: ((v[0] * 4 + v[1]) * 4 + v[2]) * 2 + v[3]
        pairs.append((index(at), index(to)))
    return pairs


def groups_by(key):
    groups = {}
    for at in itertools.product(range(4), range(4), range(4), range(2)):
        groups.setdefault(key(at), []).append(((at[0] * 4 + at[1]) * 4 + at[2]) * 2 + at[3])
    return list(groups.values())


def ring_groups(place):
    return groups_by(lambda at: tuple(-1 if i == ORDER[at[3]][place] else v for i, v in enumerate(at)))


def in_plane(v):
    planes = groups_by(lambda at: (at[ORDER[at[3]][3]], at[3]))
    return lax.all_to_all(v, AXES, 0, 0, axis_index_groups=planes, tiled=True)


def send(v, place, shift):
    return lax.ppermute(v, AXES, ring(place, shift))


def swap(v):
    return lax.ppermute(v, "c", [(0, 1), (1, 0)])


def spread(place, plus, minus, far):
    return send(plus, place, 1), send(minus, place, 3), send(far, place, 2)


def gather4(v, place):
    return (v,) + spread(place, v, v, v)


def lanes_low(shape):
    return lax.broadcasted_iota(jnp.int32, shape, len(shape) - 1) < HD


def vec(ref):
    return ref[...].astype(f32).reshape(1, -1)


def enter_kernel(x_ref, gain_ref, bias_ref, wkv_ref, bv_ref, n1_ref, kv_ref):
    n, _ = norm_parts(x_ref[...].astype(f32))
    n1 = (n * vec(gain_ref) + vec(bias_ref)).astype(bf16)
    n1_ref[...] = n1
    shift = jnp.concatenate([jnp.zeros((1, HD), f32), vec(bv_ref)], axis=1)
    kv = (dot(n1, wkv_ref[...]) + shift).astype(bf16)
    for i in range(CHIPS):
        kv_ref[i] = kv


def query_kernel(n1_ref, wq_ref, bq_ref, q_ref):
    q_ref[...] = (dot(n1_ref[...], wq_ref[...]) + vec(bq_ref)).astype(bf16)


def block_bias(kp, sp, st):
    bias = jnp.where((kp <= sp) & (kp >= st), 0.0, MASKED)
    return jnp.concatenate([bias] * (QB // 128), axis=1)


def visit(cls_ref, kb, step):
    def row_block(rb, _):
        kind = cls_ref[rb * KB + kb]

        @pl.when(kind == 2)
        def _():
            step(rb, False)

        @pl.when(kind == 1)
        def _():
            step(rb, True)

        return 0

    lax.fori_loop(0, RB, row_block, 0)


def forward_kernel(at_ref, cls_ref, q_ref, same_ref, other_ref, kpb_ref, spl_ref, stl_ref, n1_ref,
                   att_ref, keep_ref, send_ref, x_ref, o_ref, lse_ref, kv_ref, m_ref, l_ref, acc_ref, kt_ref):
    kv_ref[:CHIPS] = same_ref[...]
    kv_ref[CHIPS:] = other_ref[...]
    low = lanes_low((ROWS, 2 * HD))
    for h in range(H):
        pair = q_ref[:, (h // 2) * 128 : (h // 2) * 128 + 128].astype(f32) * 0.125
        if h % 2:
            pair = pltpu.roll(pair, HD, 1)
        head = jnp.where(low, pair, 0.0).astype(bf16)
        for rb in range(RB):
            x_ref[rb, h * RBR : (h + 1) * RBR, :] = head[rb * RBR : (rb + 1) * RBR, :]
    m_ref[...] = jnp.full((RB, 1, QB), MASKED, f32)
    l_ref[...] = jnp.zeros((RB, 1, QB), f32)
    acc_ref[...] = jnp.zeros((RB, 2 * HD, QB), f32)

    def key_block(kb, _):
        cols = pl.ds(pl.multiple_of(kb * KBR, KBR), KBR)
        kt_ref[...] = jnp.transpose(kv_ref[:, cols, :].reshape(KEYS, 2 * HD).astype(f32)).astype(bf16)

        def step(rb, masked):
            s = dot_nt(kv_ref[:, cols, :].reshape(KEYS, 2 * HD), x_ref[rb])
            if masked:
                s = s + block_bias(kpb_ref[kb], spl_ref[rb], stl_ref[rb])
            m_old = m_ref[rb]
            m_new = jnp.maximum(m_old, jnp.max(s, axis=0, keepdims=True))
            alpha = jnp.exp(m_old - m_new)
            p = jnp.exp(s - m_new)
            l_ref[rb] = l_ref[rb] * alpha + jnp.sum(p, axis=0, keepdims=True)
            acc_ref[rb] = acc_ref[rb] * alpha + dot(kt_ref[...], p.astype(bf16))
            m_ref[rb] = m_new

        visit(cls_ref, kb, step)
        return 0

    lax.fori_loop(0, KB, key_block, 0)
    keep = lanes_low((RBR, 2 * HD))
    first = at_ref[0] == 0
    for rb in range(RB):
        rows = slice(rb * RBR, (rb + 1) * RBR)
        l = l_ref[rb]
        lse_ref[rb] = m_ref[rb] + jnp.log(l)
        out = jnp.transpose(acc_ref[rb] / l)
        o_ref[rb] = out
        for h in range(0, H, 2):
            even = out[h * RBR : (h + 1) * RBR, :]
            odd = out[(h + 1) * RBR : (h + 2) * RBR, :]
            att_ref[rows, h * HD : (h + 2) * HD] = jnp.where(keep, pltpu.roll(even, HD, 1), odd).astype(bf16)
    n1, att = n1_ref[...], att_ref[...]
    keep_ref[...] = jnp.where(first, n1, att)
    send_ref[...] = jnp.where(first, att, n1)


def backward_kernel(at_ref, cls_ref, x_ref, do_ref, o_ref, lse_ref, kv_ref, kpb_ref, spl_ref, stl_ref, gb_ref,
                    dq_ref, keep_ref, send_ref, same_ref, other_ref, y_ref, drow_ref, dqt_ref, acc_ref, kt_ref):
    low = lanes_low((ROWS, 2 * HD))
    for h in range(H):
        pair = do_ref[:, (h // 2) * 128 : (h // 2) * 128 + 128].astype(f32)
        if h % 2 == 0:
            pair = pltpu.roll(pair, HD, 1)
        head = jnp.where(low, 0.0, pair).astype(bf16)
        for rb in range(RB):
            y_ref[rb, h * RBR : (h + 1) * RBR, :] = head[rb * RBR : (rb + 1) * RBR, :]
    for rb in range(RB):
        delta = jnp.sum(y_ref[rb].astype(f32) * o_ref[rb], axis=1, keepdims=True)
        drow_ref[rb] = jnp.transpose(jnp.broadcast_to(delta, (QB, 128)))[:8]
    dqt_ref[...] = jnp.zeros((RB, 128, QB), f32)

    def key_block(kb, _):
        cols = pl.ds(pl.multiple_of(kb * KBR, KBR), KBR)
        kvb = kv_ref[:, cols, :].reshape(KEYS, 2 * HD)
        kt_ref[...] = jnp.transpose(kvb.astype(f32)).astype(bf16)
        acc_ref[...] = jnp.zeros((KEYS, 2 * HD), f32)

        def step(rb, masked):
            kvb = kv_ref[:, cols, :].reshape(KEYS, 2 * HD)
            xb, yb = x_ref[rb], y_ref[rb]
            s = dot_nt(kvb, xb)
            if masked:
                s = s + block_bias(kpb_ref[kb], spl_ref[rb], stl_ref[rb])
            p = jnp.exp(s - lse_ref[rb])
            ds = (p * (dot_nt(kvb, yb) - drow_ref[rb, :1])).astype(bf16)
            acc_ref[...] += dot(ds, xb) + dot(p.astype(bf16), yb)
            dqt_ref[rb] += dot(kt_ref[...], ds)

        visit(cls_ref, kb, step)
        sums = acc_ref[...].reshape(WIDE, KBR, 2 * HD).astype(bf16)
        same_ref[:, cols, :] = sums[:CHIPS]
        other_ref[:, cols, :] = sums[CHIPS:]
        return 0

    lax.fori_loop(0, KB, key_block, 0)
    keep = lanes_low((RBR, 2 * HD))
    for rb in range(RB):
        dq = jnp.transpose(dqt_ref[rb]) * 0.125
        for h in range(0, H, 2):
            even = dq[h * RBR : (h + 1) * RBR, :]
            odd = dq[(h + 1) * RBR : (h + 2) * RBR, :]
            dq_ref[rb * RBR : (rb + 1) * RBR, h * HD : (h + 2) * HD] = jnp.where(
                keep, even, pltpu.roll(odd, HD, 1)
            ).astype(bf16)
    first = at_ref[0] == 0
    dq, gb = dq_ref[...], gb_ref[...]
    keep_ref[...] = jnp.where(first, dq, gb)
    send_ref[...] = jnp.where(first, gb, dq)


def put_rows(ref, at, row):
    for i in range(row.shape[1] // 128):
        ref[pl.ds(at + i, 1), :] = row[:, i * 128 : (i + 1) * 128]


def middle_kernel(at_ref, att_ref, x_ref, g_ref, wout_ref, bout_ref, gain_ref, bias_ref, wup_ref, bup_ref, wdown_ref, bdown_ref,
                  y_ref, bk_ref, bs_ref, sk_ref, ss_ref, gr_ref, gb_ref, ga_ref, vec_ref,
                  resid_ref, out_ref, gn2_ref, n2_ref):
    step = pl.program_id(0)
    first = at_ref[0] == 0

    @pl.when(step == 0)
    def _():
        resid = x_ref[...].astype(f32) + (dot(att_ref[...], wout_ref[...]) + vec(bout_ref))
        resid_ref[...] = resid
        n, _ = norm_parts(resid)
        n2 = (n * vec(gain_ref) + vec(bias_ref)).astype(bf16)
        n2_ref[...] = n2
        sk_ref[...] = jnp.where(first, g_ref[...], n2)
        ss_ref[...] = jnp.where(first, n2, g_ref[...])
        out_ref[...] = jnp.zeros_like(out_ref)
        gn2_ref[...] = jnp.zeros_like(gn2_ref)

    g = g_ref[...]
    pre = dot(n2_ref[...], wup_ref[...]) + vec(bup_ref)
    sq = pre * pre
    t = jnp.tanh(0.7978845608028654 * (pre + 0.044715 * sq * pre))
    half = 0.5 + 0.5 * t
    act = (pre * half).astype(bf16)
    slope = half + (0.5 * 0.7978845608028654) * pre * (1.0 - t * t) * (1.0 + (3 * 0.044715) * sq)
    gp = (slope * dot_nt(g, wdown_ref[...])).astype(bf16)
    bk_ref[...] = jnp.where(first, act, gp)
    bs_ref[...] = jnp.where(first, gp, act)
    put_rows(vec_ref, 24 + step * (FC // 128), jnp.sum(gp.astype(f32), axis=0, keepdims=True))
    out_ref[...] += dot(act, wdown_ref[...])
    gn2_ref[...] += dot_nt(gp, wup_ref[...])

    @pl.when(step == pl.num_programs(0) - 1)
    def _():
        resid = resid_ref[...]
        gf = g.astype(f32)
        y_ref[...] = (resid + (out_ref[...] + vec(bdown_ref))).astype(bf16)
        n, rstd = norm_parts(resid)
        e = gn2_ref[...]
        gr = gf + norm_back(e, n, rstd, vec(gain_ref))
        gr_ref[...] = gr
        gb = gr.astype(bf16)
        gb_ref[...] = gb
        ga_ref[...] = dot_nt(gb, wout_ref[...]).astype(bf16)
        put_rows(vec_ref, 0, jnp.sum(gf, axis=0, keepdims=True))
        put_rows(vec_ref, 6, jnp.sum(e * n, axis=0, keepdims=True))
        put_rows(vec_ref, 12, jnp.sum(e, axis=0, keepdims=True))
        put_rows(vec_ref, 18, jnp.sum(gb.astype(f32), axis=0, keepdims=True))


def leave_kernel(at_ref, x_ref, gain_ref, wq_ref, wkv_ref, gq_ref, gr_ref, mid_ref, parts_ref, gin_ref, keep_ref, send_ref, vec_ref):
    gkv = jnp.sum(parts_ref[...].astype(f32), axis=0).astype(bf16)
    gq = gq_ref[...]
    e = dot_nt(gq, wq_ref[...]) + dot_nt(gkv, wkv_ref[...])
    n, rstd = norm_parts(x_ref[...].astype(f32))
    gin = gr_ref[...] + norm_back(e, n, rstd, vec(gain_ref))
    for i in range(D // 128):
        gin_ref[pl.ds(i, ROWS, stride=D // 128), :] = gin[:, i * 128 : (i + 1) * 128]
    gkv = gkv.astype(f32)
    vec_ref[0:48, :] = mid_ref[...]
    vec_ref[48:128, :] = jnp.zeros((80, 128), f32)
    put_rows(vec_ref, 48, jnp.sum(e * n, axis=0, keepdims=True))
    put_rows(vec_ref, 54, jnp.sum(e, axis=0, keepdims=True))
    put_rows(vec_ref, 60, jnp.sum(gq.astype(f32), axis=0, keepdims=True))
    put_rows(vec_ref, 66, jnp.sum(gkv, axis=0, keepdims=True))
    first = at_ref[0] == 0
    vecs = vec_ref[...]
    keep_ref[...] = jnp.where(first, gkv, vecs)
    send_ref[...] = jnp.where(first, vecs, gkv)


def pack_kernel(bk_ref, sk_ref, bp_ref, sp_ref, out_ref):
    for i in range(4):
        cols = slice(i * D, (i + 1) * D)
        out_ref[i, 0:ROWS, 0:D] = bk_ref[:, cols]
        out_ref[i, ROWS:, 0:D] = bp_ref[:, cols]
        out_ref[i, 0:ROWS, D:] = sk_ref[...]
        out_ref[i, ROWS:, D:] = sp_ref[...]

def quarters(at, which, total_ref, outs):
    rows = total_ref.shape[0]//4
    for rel, out in zip((0,1,3,2), outs):
        out[...] = total_ref[pl.ds(pl.multiple_of(((at[which]+rel)&3)*rows, rows), rows), :].astype(out.dtype)

def weight_kernel(at_ref, slab_ref, own_ref, plus_ref, minus_ref, far_ref, total_ref):
    step = pl.program_id(0)

    @pl.when(step == 0)
    def _():
        total_ref[...] = jnp.zeros_like(total_ref)

    @pl.when(at_ref[0] == 0)
    def _():
        total_ref[...] += dot_tn(slab_ref[0, :, :D], slab_ref[0, :, D:])

    @pl.when(at_ref[0] == 1)
    def _():
        total_ref[...] += dot_tn(slab_ref[0, :, D:], slab_ref[0, :, :D])

    @pl.when(step == pl.num_programs(0) - 1)
    def _():
        quarters(at_ref, 2, total_ref, (own_ref, plus_ref, minus_ref, far_ref))


def join_kernel(at_ref,a_ref,b_ref,c_ref,d_ref,out_ref):
    rows=a_ref.shape[0]
    for rel, v in zip(FROM,(a_ref,b_ref,c_ref,d_ref)):
        out_ref[pl.ds(pl.multiple_of(((at_ref[2]+rel)&3)*rows,rows),rows),:] = v[...]

def place_kernel(at_ref, own_ref, other_ref, *rest):
    down_ref, up_ref = rest[-2:]
    first = at_ref[0]==0
    own, other = own_ref[...], other_ref[...]
    down_ref[...] = jnp.where(first, own, other).astype(f32)
    up_ref[...] = jnp.where(first, other, own).astype(f32)

def place(at, rel, own, other, kept):
    tile = D // 2
    piece = pl.BlockSpec((tile, D), lambda i, at: (i, 0))
    outs = (
        pl.BlockSpec((tile, D), lambda i, at: (((at[4] + rel) & 3) * 2 + i, 0)),
        pl.BlockSpec((tile, D), lambda i, at: (i, (at[5] + rel) & 3)),
    )
    return pl.pallas_call(
        place_kernel,
        grid_spec=pltpu.PrefetchScalarGridSpec(
            num_scalar_prefetch=1, grid=(2,), in_specs=[piece, piece] + [ANY] * len(kept), out_specs=outs
        ),
        out_shape=shapes(((FF, D), f32), ((D, FF), f32)),
        input_output_aliases={3: 0, 4: 1} if kept else {},
        compiler_params=params(62),
        cost_estimate=cost(0, 0),
        name="place",
    )(at, own, other, *kept)


def share_kernel(same_ref, other_ref, out_ref):
    out_ref[...] = (same_ref[...].astype(f32) + other_ref[...].astype(f32)).astype(bf16)


def square_kernel(lk_ref, lo_ref, rk_ref, ro_ref, out_ref):
    out_ref[...] = (dot_tn(lk_ref[...], rk_ref[...]) + dot_tn(lo_ref[...], ro_ref[...])).astype(bf16)


def late_kernel(at_ref, lk_ref, lo_ref, tk_ref, to_ref, square_ref, out_ref, total_ref):
    first = at_ref[0] == 0

    @pl.when(first)
    def _():
        total_ref[...] = dot_tn(lk_ref[...], tk_ref[...].astype(bf16)) + dot_tn(lo_ref[...], to_ref[...].astype(bf16))

    @pl.when(jnp.logical_not(first))
    def _():
        total_ref[0:128, :] = tk_ref[...] + to_ref[...]
        total_ref[128:, :] = jnp.zeros((D - 128, 128), f32)

    for i in range(CHIPS):
        rows = slice(STRIP * i, STRIP * (i + 1))
        out_ref[i, :, :D] = square_ref[rows, :]
        out_ref[i, :, D:] = total_ref[rows, :].astype(bf16)


def strip_kernel(parts_ref, out_ref):
    out_ref[...] = jnp.sum(parts_ref[...].astype(f32), axis=0).astype(bf16)


def part_kernel(a_ref, b_ref, c_ref, d_ref, out_ref):
    out_ref[...] = pair_sums(a_ref[...], b_ref[...], c_ref[...], d_ref[...])


def copies_kernel(a_ref, b_ref, c_ref, d_ref, out_ref):
    total = pair_sums(a_ref[...], b_ref[...], c_ref[...], d_ref[...])
    for i in range(CHIPS):
        out_ref[i] = total


VECTORS = ((0, 6), (6, 6), (12, 6), (18, 6), (24, 24), (48, 6), (54, 6), (60, 6))


def late_place_kernel(at_ref, own_ref, other_ref, query_ref, out_ref, kv_ref, value_ref, *vec_refs):
    first = at_ref[0] == 0
    vecs = []
    for a in range(CHIPS):
        rows = slice(STRIP * a, STRIP * (a + 1))
        own, other = own_ref[a].astype(f32), other_ref[a].astype(f32)
        zero, one = jnp.where(first, own, other), jnp.where(first, other, own)
        query_ref[rows, :] = zero[:, :D]
        out_ref[rows, :] = one[:, :D]
        kv_ref[rows, :] = zero[:, D:]
        if a < 2:
            vecs.append(one[:, D:])
    row = lambda i: vecs[i // STRIP][i % STRIP]
    value_ref[...] = row(66)[HD:]
    for ref, (at, count) in zip(vec_refs, VECTORS):
        for i in range(count):
            ref[i * 128 : (i + 1) * 128] = row(at + i)


def call(kernel, args, outs, scratch=(), name=None, flops=0, nbytes=2e6, after=()):
    given, extra = len(args), len(after)
    run = lambda *refs: kernel(*refs[:given], *refs[given + extra :])
    return pl.pallas_call(
        run,
        out_shape=outs,
        in_specs=[SMEM if v.dtype == jnp.int32 and v.ndim == 1 else VMEM for v in args] + [ANY] * extra,
        out_specs=jax.tree.map(lambda _: VMEM, outs),
        scratch_shapes=list(scratch),
        compiler_params=params(),
        cost_estimate=cost(flops, nbytes),
        name=name,
    )(*args, *after)


def shapes(*pairs):
    return tuple(jax.ShapeDtypeStruct(s, t) for s, t in pairs)


def positions(lengths, splits, wide_index, core):
    ends = jnp.cumsum(lengths, dtype=jnp.int32)
    starts = ends - lengths
    first = lengths * jnp.minimum(splits[:, 0], splits[:, 1]) // 1024
    second = lengths * jnp.maximum(splits[:, 0], splits[:, 1]) // 1024

    def place(row):
        shape = (1,) * row.ndim + (-1,)
        s, e, a, b, n = (v.reshape(shape) for v in (starts, ends, first, second, lengths))
        row = row[..., None]
        inside = (row >= s) & (row < e)
        u = row - s
        moved = jnp.where(u < a, u, jnp.where(u >= b, a + u - b, a + n - b + u - a))
        return (
            jnp.sum(jnp.where(inside, s + moved, 0), axis=-1, dtype=jnp.int32),
            jnp.sum(jnp.where(inside, s, 0), axis=-1, dtype=jnp.int32),
        )

    k = jnp.arange(KB, dtype=jnp.int32)[:, None, None]
    j = jnp.arange(CHIPS, dtype=jnp.int32) * 2
    j = jnp.concatenate([j + core, j + 1 - core])[None, :, None]
    r = jnp.arange(KBR, dtype=jnp.int32)[None, None, :]
    keys, _ = place(((k * KBR + r) * WIDE + j).reshape(KB, KEYS))
    own, own_start = place(jnp.arange(ROWS, dtype=jnp.int32) * WIDE + wide_index)
    low, high = jnp.min(keys, axis=1), jnp.max(keys, axis=1)
    blocks, block_starts = own.reshape(RB, RBR), own_start.reshape(RB, RBR)
    top, start_low = jnp.max(blocks, axis=1), jnp.min(block_starts, axis=1)
    bottom, start_high = jnp.min(blocks, axis=1), jnp.max(block_starts, axis=1)
    some = (low[None] <= top[:, None]) & (high[None] >= start_low[:, None])
    every = (high[None] <= bottom[:, None]) & (low[None] >= start_high[:, None])
    kinds = jnp.where(every, 2, jnp.where(some, 1, 0)).astype(jnp.int32).reshape(-1)
    return keys, own, own_start, kinds


NARROW = ((ROWS, D), bf16)
KV_HALF = ((CHIPS, ROWS, 2 * HD), bf16)


def attend(*args):
    stat = pltpu.VMEM((RB, 1, QB), f32)
    return call(
        forward_kernel, args,
        shapes(NARROW, NARROW, NARROW, ((RB, QB, 128), bf16), ((RB, QB, 128), f32), ((RB, 1, QB), f32), ((WIDE, ROWS, 2 * HD), bf16)),
        [stat, stat, pltpu.VMEM((RB, 2 * HD, QB), f32), pltpu.VMEM((2 * HD, KEYS), bf16)],
        name="attend", flops=4 * ROWS * H * WINDOW * 64, nbytes=4e6,
    )


def attend_back(*args, after=()):
    return call(
        backward_kernel, args,
        shapes(NARROW, NARROW, NARROW, KV_HALF, KV_HALF),
        [
            pltpu.VMEM((RB, QB, 128), bf16), pltpu.VMEM((RB, 8, QB), f32),
            pltpu.VMEM((RB, 128, QB), f32), pltpu.VMEM((KEYS, 2 * HD), f32), pltpu.VMEM((2 * HD, KEYS), bf16),
        ],
        name="attend_back", flops=10 * ROWS * H * WINDOW * 64, nbytes=8e6, after=after,
    )


def coords():
    x, y, z, c = (lax.axis_index(a) for a in AXES)
    first = c == 0
    at = (c, jnp.where(first, z, y), jnp.where(first, y, x), jnp.where(first, x, z), z, y)
    return jnp.stack(at).astype(jnp.int32)


QUARTER = ((D // 4, D), bf16)


def pair_sums(a, b, c, d):
    a, b, c, d = (v.astype(f32) for v in (a, b, c, d))
    return ((a + d) + (b + c)).astype(bf16)


def tie_kernel(v_ref, *refs):
    pass


def tie(v, *after):
    return pl.pallas_call(
        tie_kernel,
        out_shape=jax.ShapeDtypeStruct(v.shape, v.dtype),
        in_specs=[ANY] * (1 + len(after)),
        out_specs=ANY,
        input_output_aliases={0: 0},
        cost_estimate=cost(0, 0),
        name="tie",
    )(v, *after)


def corner(v):
    return swap(v[:8, :128])


def body(block_input, file_lengths, file_splits, ln1_gain, ln1_bias, w_query, b_query, w_kv, b_value, w_out, b_out,
         ln2_gain, ln2_bias, w_up, b_up, w_down, b_down, out_cotangent):
    x = block_input.reshape(ROWS, D)
    g = out_cotangent.reshape(ROWS, D)
    wide = ("y", "z", "c")
    at = coords()
    narrow = NARROW

    n1, copies = call(enter_kernel, (x, ln1_gain, ln1_bias, w_kv, b_value), shapes(narrow, ((CHIPS, ROWS, 2 * HD), bf16)),
                      name="enter", flops=2 * ROWS * D * 128)
    kv_same = lax.all_to_all(copies, ("y", "z"), 0, 0, tiled=True)
    keys, own, own_start, kinds = positions(file_lengths[0], file_splits[0], lax.axis_index(wide), at[0])
    key_cols = jnp.broadcast_to(keys[:, :, None], (KB, KEYS, 128))
    own_lanes = jnp.tile(own.reshape(RB, 1, RBR), (1, 1, 128 // RBR))
    start_lanes = jnp.tile(own_start.reshape(RB, 1, RBR), (1, 1, 128 // RBR))
    q = call(query_kernel, (n1, w_query, b_query), shapes(narrow)[0], name="query", flops=2 * ROWS * D * D,
             after=(key_cols, own_lanes, start_lanes, kinds))
    kv_same = tie(kv_same, q)
    kv_other = swap(kv_same)

    att, left, left_send, xq, o, lse, kv_all = attend(at, kinds, q, kv_same, kv_other, key_cols, own_lanes, start_lanes, n1)
    left_other = swap(left_send)

    steps = FF // FC
    whole = lambda *s: pl.BlockSpec(s, lambda i: (0,) * len(s))
    wide_cols = pl.BlockSpec((ROWS, FC), lambda i: (0, i))
    y, big, big_send, small, small_send, gr, gb, ga, vec_mid = pl.pallas_call(
        middle_kernel,
        grid=(steps,),
        out_shape=shapes(narrow, ((ROWS, FF), bf16), ((ROWS, FF), bf16), narrow, narrow, ((ROWS, D), f32), narrow, narrow, ((48, 128), f32)),
        in_specs=[
            SMEM, whole(ROWS, D), whole(ROWS, D), whole(ROWS, D), whole(D, D), whole(D), whole(D), whole(D),
            pl.BlockSpec((D, FC), lambda i: (0, i)), pl.BlockSpec((FC,), lambda i: (i,)),
            pl.BlockSpec((FC, D), lambda i: (i, 0)), whole(D),
        ],
        out_specs=(
            whole(ROWS, D), wide_cols, wide_cols, whole(ROWS, D), whole(ROWS, D), whole(ROWS, D), whole(ROWS, D),
            whole(ROWS, D), whole(48, 128),
        ),
        scratch_shapes=[pltpu.VMEM((ROWS, D), f32)] * 3 + [pltpu.VMEM((ROWS, D), bf16)],
        compiler_params=params(),
        cost_estimate=cost(8 * ROWS * D * FF, 2e7),
        name="middle",
    )(at, att, x, g, w_out, b_out, ln2_gain, ln2_bias, w_up, b_up, w_down, b_down)

    packed = call(pack_kernel, (big, small, swap(big_send), swap(small_send)), shapes(((4, 2 * ROWS, 2 * D), bf16))[0], name="pack")
    slabs = lax.all_to_all(packed, AXES, 0, 0, axis_index_groups=ring_groups(0), tiled=True)

    gq, right, right_send, kv_grads, kv_send = attend_back(at, kinds, xq, ga, o, lse, kv_all, key_cols, own_lanes, start_lanes, gb, after=(packed,))
    shares = call(share_kernel, (kv_grads, swap(kv_send)), shapes(KV_HALF)[0], name="share", after=(slabs[0, :8, :128],))
    parts = lax.all_to_all(shares, ("y", "z"), 0, 0, tiled=True)

    pieces = pl.pallas_call(
        weight_kernel,
        grid=(4,),
        out_shape=shapes(*[QUARTER] * 4),
        in_specs=[SMEM, pl.BlockSpec((1, 2 * ROWS, 2 * D), lambda i: (i, 0, 0))],
        out_specs=(VMEM,) * 4,
        scratch_shapes=[pltpu.VMEM((D, D), f32)],
        compiler_params=params(62),
        cost_estimate=cost(0, 0),
        name="weights",
    )(at, slabs)
    ff_parts = (pieces[0],) + spread(1, *pieces[1:])
    square = call(square_kernel, (left, left_other, right, swap(right_send)), shapes(((D, D), bf16))[0], name="square")
    gin, tail, tail_send, _ = call(
        leave_kernel, (at, x, ln1_gain, w_query, w_kv, gq, gr, vec_mid, parts),
        shapes(((ROWS * D // 128, 128), f32), ((128, 128), f32), ((128, 128), f32), ((128, 128), f32)),
        name="leave", after=(pieces[0], square),
    )

    shares = call(late_kernel, (at, left, left_other, tail, swap(tail_send), square), shapes(((CHIPS, STRIP, D + 128), bf16))[0],
                  [pltpu.VMEM((D, 128), f32)], name="late", after=ff_parts[1:])
    ff_part = call(part_kernel, ff_parts, shapes(QUARTER)[0], name="part", after=(shares,))
    ff_crossed = gather4(ff_part, 2)
    late_parts = in_plane(shares)
    ff_totals = gather4(pair_sums(*ff_crossed), 1)
    strip = call(strip_kernel, (late_parts,), shapes(((STRIP, D + 128), bf16))[0], name="strip", after=ff_crossed[1:])
    u = call(join_kernel, (at,) + ff_totals, shapes(((D, D), bf16))[0], name="join", after=(strip,))
    before, after, far = spread(0, u, u, u)
    kept = place(at, 0, u, swap(u), ())
    mark = corner(kept[0])
    copies = call(copies_kernel, gather4(strip, 3), shapes(((CHIPS, STRIP, D + 128), bf16))[0], name="copies",
                  after=(mark,))
    late = in_plane(copies)
    far = tie(far, copies)
    before, after = tie(before, far), tie(after, far)
    kept = place(at, 3, before, swap(before), kept)
    kept = place(at, 1, after, swap(after), kept)
    g_down, g_up = place(at, 2, far, swap(far), kept)
    late = tie(late, corner(kept[0]))
    one = lambda n: ((n,), f32)
    outs = call(
        late_place_kernel, (at, late, swap(late)),
        shapes(((D, D), f32), ((D, D), f32), ((D, 128), f32), one(HD), *[one(128 * n) for _, n in VECTORS]), name="late_place",
    )
    g_query, g_out, g_kv, g_value, g_bdown, g_gain2, g_bias2, g_bout, g_bup, g_gain1, g_bias1, g_bq = outs
    shape = block_input.shape
    return (
        y.reshape(shape), gin.reshape(shape), g_gain1, g_bias1, g_query, g_bq, g_kv, g_value,
        g_out, g_bout, g_gain2, g_bias2, g_up, g_bup, g_down, g_bdown,
    )


def solution(mesh):
    split = P("x", None, ("y", "z", "c"), None)
    return jax.shard_map(
        body,
        mesh=Mesh(mesh.devices.reshape(4, 4, 4, 2), AXES),
        in_specs=(split, P("x", None), P("x", None, None)) + (P(),) * 14 + (split,),
        out_specs=(split, split) + (P(),) * 14,
        check_vma=False,
    )
```

```python
import itertools

import jax
import jax.numpy as jnp
from jax import lax
from jax.experimental import pallas as pl
from jax.experimental.pallas import tpu as pltpu
from jax.sharding import Mesh, PartitionSpec as P

EPS = 1e-05
MASKED = -1e30
ROWS = 128
WIDE = 32
CHIPS = 16
D = 768
H = 12
HD = 64
FF = 3072
WINDOW = ROWS * WIDE
RB = 2
RBR = ROWS // RB
QB = RBR * H
KB = 4
KBR = ROWS // KB
KEYS = WINDOW // KB
STRIP = D // CHIPS
FC = 1024
VMEM = pl.BlockSpec(memory_space=pltpu.VMEM)
SMEM = pl.BlockSpec(memory_space=pltpu.SMEM)
ANY = pl.BlockSpec(memory_space=pl.ANY)
f32 = jnp.float32
bf16 = jnp.bfloat16


def params(limit=56):
    return pltpu.CompilerParams(vmem_limit_bytes=limit * 1024 * 1024)


def cost(flops, nbytes):
    return pl.CostEstimate(flops=1, bytes_accessed=1, transcendentals=0)


def dot(a, b):
    return jnp.dot(a, b, preferred_element_type=f32)


def dot_nt(a, b):
    return lax.dot_general(a, b, (((1,), (1,)), ((), ())), preferred_element_type=f32)


def dot_tn(a, b):
    return lax.dot_general(a, b, (((0,), (0,)), ((), ())), preferred_element_type=f32)


def norm_parts(x):
    mean = jnp.mean(x, axis=-1, keepdims=True)
    centered = x - mean
    var = jnp.mean(centered * centered, axis=-1, keepdims=True)
    rstd = lax.rsqrt(var + EPS)
    return centered * rstd, rstd


def norm_back(e, n, rstd, gain):
    m = e * gain
    return rstd * (
        m - jnp.mean(m, axis=-1, keepdims=True) - n * jnp.mean(m * n, axis=-1, keepdims=True)
    )


AXES = ("x", "y", "z", "c")
ORDER = ((2, 1, 0, 0), (1, 0, 2, 2))
FROM = (0, 3, 1, 2)


def ring(place, shift):
    pairs = []
    for at in itertools.product(range(4), range(4), range(4), range(2)):
        to = list(at)
        axis = ORDER[at[3]][place]
        to[axis] = (to[axis] + shift) % 4
        index = lambda v: ((v[0] * 4 + v[1]) * 4 + v[2]) * 2 + v[3]
        pairs.append((index(at), index(to)))
    return pairs


def groups_by(key):
    groups = {}
    for at in itertools.product(range(4), range(4), range(4), range(2)):
        groups.setdefault(key(at), []).append(((at[0] * 4 + at[1]) * 4 + at[2]) * 2 + at[3])
    return list(groups.values())


def ring_groups(place):
    return groups_by(lambda at: tuple(-1 if i == ORDER[at[3]][place] else v for i, v in enumerate(at)))


def in_plane(v):
    planes = groups_by(lambda at: (at[ORDER[at[3]][3]], at[3]))
    return lax.all_to_all(v, AXES, 0, 0, axis_index_groups=planes, tiled=True)


def send(v, place, shift):
    return lax.ppermute(v, AXES, ring(place, shift))


def swap(v):
    return lax.ppermute(v, "c", [(0, 1), (1, 0)])


def spread(place, plus, minus, far):
    return send(plus, place, 1), send(minus, place, 3), send(far, place, 2)


def gather4(v, place):
    return (v,) + spread(place, v, v, v)


def lanes_low(shape):
    return lax.broadcasted_iota(jnp.int32, shape, len(shape) - 1) < HD


def vec(ref):
    return ref[...].astype(f32).reshape(1, -1)


def enter_kernel(x_ref, gain_ref, bias_ref, wkv_ref, bv_ref, n1_ref, kv_ref):
    n, _ = norm_parts(x_ref[...].astype(f32))
    n1 = (n * vec(gain_ref) + vec(bias_ref)).astype(bf16)
    n1_ref[...] = n1
    shift = jnp.concatenate([jnp.zeros((1, HD), f32), vec(bv_ref)], axis=1)
    kv = (dot(n1, wkv_ref[...]) + shift).astype(bf16)
    for i in range(CHIPS):
        kv_ref[i] = kv


def query_kernel(n1_ref, wq_ref, bq_ref, q_ref):
    q_ref[...] = (dot(n1_ref[...], wq_ref[...]) + vec(bq_ref)).astype(bf16)


def block_bias(kp, sp, st):
    bias = jnp.where((kp <= sp) & (kp >= st), 0.0, MASKED)
    return jnp.concatenate([bias] * (QB // 128), axis=1)


def visit(cls_ref, kb, step):
    def row_block(rb, _):
        kind = cls_ref[rb * KB + kb]

        @pl.when(kind == 2)
        def _():
            step(rb, False)

        @pl.when(kind == 1)
        def _():
            step(rb, True)

        return 0

    lax.fori_loop(0, RB, row_block, 0)


def forward_kernel(at_ref, cls_ref, q_ref, same_ref, other_ref, kpb_ref, spl_ref, stl_ref, n1_ref,
                   att_ref, keep_ref, send_ref, x_ref, o_ref, lse_ref, kv_ref, m_ref, l_ref, acc_ref, kt_ref):
    kv_ref[:CHIPS] = same_ref[...]
    kv_ref[CHIPS:] = other_ref[...]
    low = lanes_low((ROWS, 2 * HD))
    for h in range(H):
        pair = q_ref[:, (h // 2) * 128 : (h // 2) * 128 + 128].astype(f32) * 0.125
        if h % 2:
            pair = pltpu.roll(pair, HD, 1)
        head = jnp.where(low, pair, 0.0).astype(bf16)
        for rb in range(RB):
            x_ref[rb, h * RBR : (h + 1) * RBR, :] = head[rb * RBR : (rb + 1) * RBR, :]
    m_ref[...] = jnp.full((RB, 1, QB), MASKED, f32)
    l_ref[...] = jnp.zeros((RB, 1, QB), f32)
    acc_ref[...] = jnp.zeros((RB, 2 * HD, QB), f32)

    def key_block(kb, _):
        cols = pl.ds(pl.multiple_of(kb * KBR, KBR), KBR)
        kt_ref[...] = jnp.transpose(kv_ref[:, cols, :].reshape(KEYS, 2 * HD).astype(f32)).astype(bf16)

        def step(rb, masked):
            s = dot_nt(kv_ref[:, cols, :].reshape(KEYS, 2 * HD), x_ref[rb])
            if masked:
                s = s + block_bias(kpb_ref[kb], spl_ref[rb], stl_ref[rb])
            m_old = m_ref[rb]
            m_new = jnp.maximum(m_old, jnp.max(s, axis=0, keepdims=True))
            alpha = jnp.exp(m_old - m_new)
            p = jnp.exp(s - m_new)
            l_ref[rb] = l_ref[rb] * alpha + jnp.sum(p, axis=0, keepdims=True)
            acc_ref[rb] = acc_ref[rb] * alpha + dot(kt_ref[...], p.astype(bf16))
            m_ref[rb] = m_new

        visit(cls_ref, kb, step)
        return 0

    lax.fori_loop(0, KB, key_block, 0)
    keep = lanes_low((RBR, 2 * HD))
    first = at_ref[0] == 0
    for rb in range(RB):
        rows = slice(rb * RBR, (rb + 1) * RBR)
        l = l_ref[rb]
        lse_ref[rb] = m_ref[rb] + jnp.log(l)
        out = jnp.transpose(acc_ref[rb] / l)
        o_ref[rb] = out
        for h in range(0, H, 2):
            even = out[h * RBR : (h + 1) * RBR, :]
            odd = out[(h + 1) * RBR : (h + 2) * RBR, :]
            att_ref[rows, h * HD : (h + 2) * HD] = jnp.where(keep, pltpu.roll(even, HD, 1), odd).astype(bf16)
    n1, att = n1_ref[...], att_ref[...]
    keep_ref[...] = jnp.where(first, n1, att)
    send_ref[...] = jnp.where(first, att, n1)


def backward_kernel(at_ref, cls_ref, x_ref, do_ref, o_ref, lse_ref, kv_ref, kpb_ref, spl_ref, stl_ref, gb_ref,
                    dq_ref, keep_ref, send_ref, same_ref, other_ref, y_ref, drow_ref, dqt_ref, acc_ref, kt_ref):
    low = lanes_low((ROWS, 2 * HD))
    for h in range(H):
        pair = do_ref[:, (h // 2) * 128 : (h // 2) * 128 + 128].astype(f32)
        if h % 2 == 0:
            pair = pltpu.roll(pair, HD, 1)
        head = jnp.where(low, 0.0, pair).astype(bf16)
        for rb in range(RB):
            y_ref[rb, h * RBR : (h + 1) * RBR, :] = head[rb * RBR : (rb + 1) * RBR, :]
    for rb in range(RB):
        delta = jnp.sum(y_ref[rb].astype(f32) * o_ref[rb], axis=1, keepdims=True)
        drow_ref[rb] = jnp.transpose(jnp.broadcast_to(delta, (QB, 128)))[:8]
    dqt_ref[...] = jnp.zeros((RB, 128, QB), f32)

    def key_block(kb, _):
        cols = pl.ds(pl.multiple_of(kb * KBR, KBR), KBR)
        kvb = kv_ref[:, cols, :].reshape(KEYS, 2 * HD)
        kt_ref[...] = jnp.transpose(kvb.astype(f32)).astype(bf16)
        acc_ref[...] = jnp.zeros((KEYS, 2 * HD), f32)

        def step(rb, masked):
            kvb = kv_ref[:, cols, :].reshape(KEYS, 2 * HD)
            xb, yb = x_ref[rb], y_ref[rb]
            s = dot_nt(kvb, xb)
            if masked:
                s = s + block_bias(kpb_ref[kb], spl_ref[rb], stl_ref[rb])
            p = jnp.exp(s - lse_ref[rb])
            ds = (p * (dot_nt(kvb, yb) - drow_ref[rb, :1])).astype(bf16)
            acc_ref[...] += dot(ds, xb) + dot(p.astype(bf16), yb)
            dqt_ref[rb] += dot(kt_ref[...], ds)

        visit(cls_ref, kb, step)
        sums = acc_ref[...].reshape(WIDE, KBR, 2 * HD).astype(bf16)
        same_ref[:, cols, :] = sums[:CHIPS]
        other_ref[:, cols, :] = sums[CHIPS:]
        return 0

    lax.fori_loop(0, KB, key_block, 0)
    keep = lanes_low((RBR, 2 * HD))
    for rb in range(RB):
        dq = jnp.transpose(dqt_ref[rb]) * 0.125
        for h in range(0, H, 2):
            even = dq[h * RBR : (h + 1) * RBR, :]
            odd = dq[(h + 1) * RBR : (h + 2) * RBR, :]
            dq_ref[rb * RBR : (rb + 1) * RBR, h * HD : (h + 2) * HD] = jnp.where(
                keep, even, pltpu.roll(odd, HD, 1)
            ).astype(bf16)
    first = at_ref[0] == 0
    dq, gb = dq_ref[...], gb_ref[...]
    keep_ref[...] = jnp.where(first, dq, gb)
    send_ref[...] = jnp.where(first, gb, dq)


def put_rows(ref, at, row):
    for i in range(row.shape[1] // 128):
        ref[pl.ds(at + i, 1), :] = row[:, i * 128 : (i + 1) * 128]


def middle_kernel(at_ref, att_ref, x_ref, g_ref, wout_ref, bout_ref, gain_ref, bias_ref, wup_ref, bup_ref, wdown_ref, bdown_ref,
                  y_ref, bk_ref, bs_ref, sk_ref, ss_ref, gr_ref, gb_ref, ga_ref, vec_ref,
                  resid_ref, out_ref, gn2_ref, n2_ref):
    step = pl.program_id(0)
    first = at_ref[0] == 0

    @pl.when(step == 0)
    def _():
        resid = x_ref[...].astype(f32) + (dot(att_ref[...], wout_ref[...]) + vec(bout_ref))
        resid_ref[...] = resid
        n, _ = norm_parts(resid)
        n2 = (n * vec(gain_ref) + vec(bias_ref)).astype(bf16)
        n2_ref[...] = n2
        sk_ref[...] = jnp.where(first, g_ref[...], n2)
        ss_ref[...] = jnp.where(first, n2, g_ref[...])
        out_ref[...] = jnp.zeros_like(out_ref)
        gn2_ref[...] = jnp.zeros_like(gn2_ref)

    g = g_ref[...]
    pre = dot(n2_ref[...], wup_ref[...]) + vec(bup_ref)
    sq = pre * pre
    t = jnp.tanh(0.7978845608028654 * (pre + 0.044715 * sq * pre))
    half = 0.5 + 0.5 * t
    act = (pre * half).astype(bf16)
    slope = half + (0.5 * 0.7978845608028654) * pre * (1.0 - t * t) * (1.0 + (3 * 0.044715) * sq)
    gp = (slope * dot_nt(g, wdown_ref[...])).astype(bf16)
    bk_ref[...] = jnp.where(first, act, gp)
    bs_ref[...] = jnp.where(first, gp, act)
    put_rows(vec_ref, 24 + step * (FC // 128), jnp.sum(gp.astype(f32), axis=0, keepdims=True))
    out_ref[...] += dot(act, wdown_ref[...])
    gn2_ref[...] += dot_nt(gp, wup_ref[...])

    @pl.when(step == pl.num_programs(0) - 1)
    def _():
        resid = resid_ref[...]
        gf = g.astype(f32)
        y_ref[...] = (resid + (out_ref[...] + vec(bdown_ref))).astype(bf16)
        n, rstd = norm_parts(resid)
        e = gn2_ref[...]
        gr = gf + norm_back(e, n, rstd, vec(gain_ref))
        gr_ref[...] = gr
        gb = gr.astype(bf16)
        gb_ref[...] = gb
        ga_ref[...] = dot_nt(gb, wout_ref[...]).astype(bf16)
        put_rows(vec_ref, 0, jnp.sum(gf, axis=0, keepdims=True))
        put_rows(vec_ref, 6, jnp.sum(e * n, axis=0, keepdims=True))
        put_rows(vec_ref, 12, jnp.sum(e, axis=0, keepdims=True))
        put_rows(vec_ref, 18, jnp.sum(gb.astype(f32), axis=0, keepdims=True))


def leave_kernel(at_ref, x_ref, gain_ref, wq_ref, wkv_ref, gq_ref, gr_ref, mid_ref, parts_ref, gin_ref, keep_ref, send_ref, vec_ref):
    gkv = jnp.sum(parts_ref[...].astype(f32), axis=0).astype(bf16)
    gq = gq_ref[...]
    e = dot_nt(gq, wq_ref[...]) + dot_nt(gkv, wkv_ref[...])
    n, rstd = norm_parts(x_ref[...].astype(f32))
    gin = gr_ref[...] + norm_back(e, n, rstd, vec(gain_ref))
    for i in range(D // 128):
        gin_ref[pl.ds(i, ROWS, stride=D // 128), :] = gin[:, i * 128 : (i + 1) * 128]
    gkv = gkv.astype(f32)
    vec_ref[0:48, :] = mid_ref[...]
    vec_ref[48:128, :] = jnp.zeros((80, 128), f32)
    put_rows(vec_ref, 48, jnp.sum(e * n, axis=0, keepdims=True))
    put_rows(vec_ref, 54, jnp.sum(e, axis=0, keepdims=True))
    put_rows(vec_ref, 60, jnp.sum(gq.astype(f32), axis=0, keepdims=True))
    put_rows(vec_ref, 66, jnp.sum(gkv, axis=0, keepdims=True))
    first = at_ref[0] == 0
    vecs = vec_ref[...]
    keep_ref[...] = jnp.where(first, gkv, vecs)
    send_ref[...] = jnp.where(first, vecs, gkv)


def pack_kernel(bk_ref, sk_ref, bp_ref, sp_ref, out_ref):
    for i in range(4):
        cols = slice(i * D, (i + 1) * D)
        out_ref[i, 0:ROWS, 0:D] = bk_ref[:, cols]
        out_ref[i, ROWS:, 0:D] = bp_ref[:, cols]
        out_ref[i, 0:ROWS, D:] = sk_ref[...]
        out_ref[i, ROWS:, D:] = sp_ref[...]

def quarters(at, which, total_ref, outs):
    rows = total_ref.shape[0]//4
    for rel, out in zip((0,1,3,2), outs):
        out[...] = total_ref[pl.ds(pl.multiple_of(((at[which]+rel)&3)*rows, rows), rows), :].astype(out.dtype)

def weight_kernel(at_ref, slab_ref, own_ref, plus_ref, minus_ref, far_ref, total_ref):
    step = pl.program_id(0)

    @pl.when(step == 0)
    def _():
        total_ref[...] = jnp.zeros_like(total_ref)

    @pl.when(at_ref[0] == 0)
    def _():
        total_ref[...] += dot_tn(slab_ref[0, :, :D], slab_ref[0, :, D:])

    @pl.when(at_ref[0] == 1)
    def _():
        total_ref[...] += dot_tn(slab_ref[0, :, D:], slab_ref[0, :, :D])

    @pl.when(step == pl.num_programs(0) - 1)
    def _():
        quarters(at_ref, 2, total_ref, (own_ref, plus_ref, minus_ref, far_ref))


def join_kernel(at_ref,a_ref,b_ref,c_ref,d_ref,out_ref):
    rows=a_ref.shape[0]
    for rel, v in zip(FROM,(a_ref,b_ref,c_ref,d_ref)):
        out_ref[pl.ds(pl.multiple_of(((at_ref[2]+rel)&3)*rows,rows),rows),:] = v[...]

def place_kernel(at_ref, own_ref, other_ref, *rest):
    down_ref, up_ref = rest[-2:]
    first = at_ref[0]==0
    own, other = own_ref[...], other_ref[...]
    down_ref[...] = jnp.where(first, own, other).astype(f32)
    up_ref[...] = jnp.where(first, other, own).astype(f32)

def place(at, rel, own, other, kept):
    tile = D // 2
    piece = pl.BlockSpec((tile, D), lambda i, at: (i, 0))
    outs = (
        pl.BlockSpec((tile, D), lambda i, at: (((at[4] + rel) & 3) * 2 + i, 0)),
        pl.BlockSpec((tile, D), lambda i, at: (i, (at[5] + rel) & 3)),
    )
    return pl.pallas_call(
        place_kernel,
        grid_spec=pltpu.PrefetchScalarGridSpec(
            num_scalar_prefetch=1, grid=(2,), in_specs=[piece, piece] + [ANY] * len(kept), out_specs=outs
        ),
        out_shape=shapes(((FF, D), f32), ((D, FF), f32)),
        input_output_aliases={3: 0, 4: 1} if kept else {},
        compiler_params=params(62),
        cost_estimate=cost(0, 0),
        name="place",
    )(at, own, other, *kept)


def share_kernel(same_ref, other_ref, out_ref):
    out_ref[...] = (same_ref[...].astype(f32) + other_ref[...].astype(f32)).astype(bf16)


def square_kernel(lk_ref, lo_ref, rk_ref, ro_ref, out_ref):
    out_ref[...] = (dot_tn(lk_ref[...], rk_ref[...]) + dot_tn(lo_ref[...], ro_ref[...])).astype(bf16)


def late_kernel(at_ref, lk_ref, lo_ref, tk_ref, to_ref, square_ref, out_ref, total_ref):
    first = at_ref[0] == 0

    @pl.when(first)
    def _():
        total_ref[...] = dot_tn(lk_ref[...], tk_ref[...].astype(bf16)) + dot_tn(lo_ref[...], to_ref[...].astype(bf16))

    @pl.when(jnp.logical_not(first))
    def _():
        total_ref[0:128, :] = tk_ref[...] + to_ref[...]
        total_ref[128:, :] = jnp.zeros((D - 128, 128), f32)

    for i in range(CHIPS):
        rows = slice(STRIP * i, STRIP * (i + 1))
        out_ref[i, :, :D] = square_ref[rows, :]
        out_ref[i, :, D:] = total_ref[rows, :].astype(bf16)


def strip_kernel(parts_ref, out_ref):
    out_ref[...] = jnp.sum(parts_ref[...].astype(f32), axis=0).astype(bf16)


def part_kernel(a_ref, b_ref, c_ref, d_ref, out_ref):
    out_ref[...] = pair_sums(a_ref[...], b_ref[...], c_ref[...], d_ref[...])


def copies_kernel(a_ref, b_ref, c_ref, d_ref, out_ref):
    total = pair_sums(a_ref[...], b_ref[...], c_ref[...], d_ref[...])
    for i in range(CHIPS):
        out_ref[i] = total


VECTORS = ((0, 6), (6, 6), (12, 6), (18, 6), (24, 24), (48, 6), (54, 6), (60, 6))


def late_place_kernel(at_ref, own_ref, other_ref, query_ref, out_ref, kv_ref, value_ref, *vec_refs):
    first = at_ref[0] == 0
    vecs = []
    for a in range(CHIPS):
        rows = slice(STRIP * a, STRIP * (a + 1))
        own, other = own_ref[a].astype(f32), other_ref[a].astype(f32)
        zero, one = jnp.where(first, own, other), jnp.where(first, other, own)
        query_ref[rows, :] = zero[:, :D]
        out_ref[rows, :] = one[:, :D]
        kv_ref[rows, :] = zero[:, D:]
        if a < 2:
            vecs.append(one[:, D:])
    row = lambda i: vecs[i // STRIP][i % STRIP]
    value_ref[...] = row(66)[HD:]
    for ref, (at, count) in zip(vec_refs, VECTORS):
        for i in range(count):
            ref[i * 128 : (i + 1) * 128] = row(at + i)


def call(kernel, args, outs, scratch=(), name=None, flops=0, nbytes=2e6, after=()):
    given, extra = len(args), len(after)
    run = lambda *refs: kernel(*refs[:given], *refs[given + extra :])
    return pl.pallas_call(
        run,
        out_shape=outs,
        in_specs=[SMEM if v.dtype == jnp.int32 and v.ndim == 1 else VMEM for v in args] + [ANY] * extra,
        out_specs=jax.tree.map(lambda _: VMEM, outs),
        scratch_shapes=list(scratch),
        compiler_params=params(),
        cost_estimate=cost(flops, nbytes),
        name=name,
    )(*args, *after)


def shapes(*pairs):
    return tuple(jax.ShapeDtypeStruct(s, t) for s, t in pairs)


def positions(lengths, splits, wide_index, core):
    ends = jnp.cumsum(lengths, dtype=jnp.int32)
    starts = ends - lengths
    first = lengths * jnp.minimum(splits[:, 0], splits[:, 1]) // 1024
    second = lengths * jnp.maximum(splits[:, 0], splits[:, 1]) // 1024

    def place(row):
        shape = (1,) * row.ndim + (-1,)
        s, e, a, b, n = (v.reshape(shape) for v in (starts, ends, first, second, lengths))
        row = row[..., None]
        inside = (row >= s) & (row < e)
        u = row - s
        moved = jnp.where(u < a, u, jnp.where(u >= b, a + u - b, a + n - b + u - a))
        return (
            jnp.sum(jnp.where(inside, s + moved, 0), axis=-1, dtype=jnp.int32),
            jnp.sum(jnp.where(inside, s, 0), axis=-1, dtype=jnp.int32),
        )

    k = jnp.arange(KB, dtype=jnp.int32)[:, None, None]
    j = jnp.arange(CHIPS, dtype=jnp.int32) * 2
    j = jnp.concatenate([j + core, j + 1 - core])[None, :, None]
    r = jnp.arange(KBR, dtype=jnp.int32)[None, None, :]
    keys, _ = place(((k * KBR + r) * WIDE + j).reshape(KB, KEYS))
    own, own_start = place(jnp.arange(ROWS, dtype=jnp.int32) * WIDE + wide_index)
    low, high = jnp.min(keys, axis=1), jnp.max(keys, axis=1)
    blocks, block_starts = own.reshape(RB, RBR), own_start.reshape(RB, RBR)
    top, start_low = jnp.max(blocks, axis=1), jnp.min(block_starts, axis=1)
    bottom, start_high = jnp.min(blocks, axis=1), jnp.max(block_starts, axis=1)
    some = (low[None] <= top[:, None]) & (high[None] >= start_low[:, None])
    every = (high[None] <= bottom[:, None]) & (low[None] >= start_high[:, None])
    kinds = jnp.where(every, 2, jnp.where(some, 1, 0)).astype(jnp.int32).reshape(-1)
    return keys, own, own_start, kinds


NARROW = ((ROWS, D), bf16)
KV_HALF = ((CHIPS, ROWS, 2 * HD), bf16)


def attend(*args):
    stat = pltpu.VMEM((RB, 1, QB), f32)
    return call(
        forward_kernel, args,
        shapes(NARROW, NARROW, NARROW, ((RB, QB, 128), bf16), ((RB, QB, 128), f32), ((RB, 1, QB), f32), ((WIDE, ROWS, 2 * HD), bf16)),
        [stat, stat, pltpu.VMEM((RB, 2 * HD, QB), f32), pltpu.VMEM((2 * HD, KEYS), bf16)],
        name="attend", flops=4 * ROWS * H * WINDOW * 64, nbytes=4e6,
    )


def attend_back(*args, after=()):
    return call(
        backward_kernel, args,
        shapes(NARROW, NARROW, NARROW, KV_HALF, KV_HALF),
        [
            pltpu.VMEM((RB, QB, 128), bf16), pltpu.VMEM((RB, 8, QB), f32),
            pltpu.VMEM((RB, 128, QB), f32), pltpu.VMEM((KEYS, 2 * HD), f32), pltpu.VMEM((2 * HD, KEYS), bf16),
        ],
        name="attend_back", flops=10 * ROWS * H * WINDOW * 64, nbytes=8e6, after=after,
    )


def coords():
    x, y, z, c = (lax.axis_index(a) for a in AXES)
    first = c == 0
    at = (c, jnp.where(first, z, y), jnp.where(first, y, x), jnp.where(first, x, z), z, y)
    return jnp.stack(at).astype(jnp.int32)


QUARTER = ((D // 4, D), bf16)


def pair_sums(a, b, c, d):
    a, b, c, d = (v.astype(f32) for v in (a, b, c, d))
    return ((a + d) + (b + c)).astype(bf16)


def tie_kernel(v_ref, *refs):
    pass


def tie(v, *after):
    return pl.pallas_call(
        tie_kernel,
        out_shape=jax.ShapeDtypeStruct(v.shape, v.dtype),
        in_specs=[ANY] * (1 + len(after)),
        out_specs=ANY,
        input_output_aliases={0: 0},
        cost_estimate=cost(0, 0),
        name="tie",
    )(v, *after)


def corner(v):
    return swap(v[:8, :128])


def body(block_input, file_lengths, file_splits, ln1_gain, ln1_bias, w_query, b_query, w_kv, b_value, w_out, b_out,
         ln2_gain, ln2_bias, w_up, b_up, w_down, b_down, out_cotangent):
    x = block_input.reshape(ROWS, D)
    g = out_cotangent.reshape(ROWS, D)
    wide = ("y", "z", "c")
    at = coords()
    narrow = NARROW

    n1, copies = call(enter_kernel, (x, ln1_gain, ln1_bias, w_kv, b_value), shapes(narrow, ((CHIPS, ROWS, 2 * HD), bf16)),
                      name="enter", flops=2 * ROWS * D * 128)
    kv_same = lax.all_to_all(copies, ("y", "z"), 0, 0, tiled=True)
    keys, own, own_start, kinds = positions(file_lengths[0], file_splits[0], lax.axis_index(wide), at[0])
    key_cols = jnp.broadcast_to(keys[:, :, None], (KB, KEYS, 128))
    own_lanes = jnp.tile(own.reshape(RB, 1, RBR), (1, 1, 128 // RBR))
    start_lanes = jnp.tile(own_start.reshape(RB, 1, RBR), (1, 1, 128 // RBR))
    q = call(query_kernel, (n1, w_query, b_query), shapes(narrow)[0], name="query", flops=2 * ROWS * D * D,
             after=(key_cols, own_lanes, start_lanes, kinds))
    kv_same = tie(kv_same, q)
    kv_other = swap(kv_same)

    att, left, left_send, xq, o, lse, kv_all = attend(at, kinds, q, kv_same, kv_other, key_cols, own_lanes, start_lanes, n1)
    left_other = swap(left_send)

    steps = FF // FC
    whole = lambda *s: pl.BlockSpec(s, lambda i: (0,) * len(s))
    wide_cols = pl.BlockSpec((ROWS, FC), lambda i: (0, i))
    y, big, big_send, small, small_send, gr, gb, ga, vec_mid = pl.pallas_call(
        middle_kernel,
        grid=(steps,),
        out_shape=shapes(narrow, ((ROWS, FF), bf16), ((ROWS, FF), bf16), narrow, narrow, ((ROWS, D), f32), narrow, narrow, ((48, 128), f32)),
        in_specs=[
            SMEM, whole(ROWS, D), whole(ROWS, D), whole(ROWS, D), whole(D, D), whole(D), whole(D), whole(D),
            pl.BlockSpec((D, FC), lambda i: (0, i)), pl.BlockSpec((FC,), lambda i: (i,)),
            pl.BlockSpec((FC, D), lambda i: (i, 0)), whole(D),
        ],
        out_specs=(
            whole(ROWS, D), wide_cols, wide_cols, whole(ROWS, D), whole(ROWS, D), whole(ROWS, D), whole(ROWS, D),
            whole(ROWS, D), whole(48, 128),
        ),
        scratch_shapes=[pltpu.VMEM((ROWS, D), f32)] * 3 + [pltpu.VMEM((ROWS, D), bf16)],
        compiler_params=params(),
        cost_estimate=cost(8 * ROWS * D * FF, 2e7),
        name="middle",
    )(at, att, x, g, w_out, b_out, ln2_gain, ln2_bias, w_up, b_up, w_down, b_down)

    packed = call(pack_kernel, (big, small, swap(big_send), swap(small_send)), shapes(((4, 2 * ROWS, 2 * D), bf16))[0], name="pack")
    slabs = lax.all_to_all(packed, AXES, 0, 0, axis_index_groups=ring_groups(0), tiled=True)

    gq, right, right_send, kv_grads, kv_send = attend_back(at, kinds, xq, ga, o, lse, kv_all, key_cols, own_lanes, start_lanes, gb, after=(packed,))
    shares = call(share_kernel, (kv_grads, swap(kv_send)), shapes(KV_HALF)[0], name="share", after=(slabs[0, :8, :128],))
    parts = lax.all_to_all(shares, ("y", "z"), 0, 0, tiled=True)

    pieces = pl.pallas_call(
        weight_kernel,
        grid=(4,),
        out_shape=shapes(*[QUARTER] * 4),
        in_specs=[SMEM, pl.BlockSpec((1, 2 * ROWS, 2 * D), lambda i: (i, 0, 0))],
        out_specs=(VMEM,) * 4,
        scratch_shapes=[pltpu.VMEM((D, D), f32)],
        compiler_params=params(62),
        cost_estimate=cost(0, 0),
        name="weights",
    )(at, slabs)
    ff_parts = (pieces[0],) + spread(1, *pieces[1:])
    square = call(square_kernel, (left, left_other, right, swap(right_send)), shapes(((D, D), bf16))[0], name="square")
    gin, tail, tail_send, _ = call(
        leave_kernel, (at, x, ln1_gain, w_query, w_kv, gq, gr, vec_mid, parts),
        shapes(((ROWS * D // 128, 128), f32), ((128, 128), f32), ((128, 128), f32), ((128, 128), f32)),
        name="leave", after=(pieces[0], square),
    )

    shares = call(late_kernel, (at, left, left_other, tail, swap(tail_send), square), shapes(((CHIPS, STRIP, D + 128), bf16))[0],
                  [pltpu.VMEM((D, 128), f32)], name="late", after=ff_parts[1:])
    ff_part = call(part_kernel, ff_parts, shapes(QUARTER)[0], name="part", after=(shares,))
    ff_crossed = gather4(ff_part, 2)
    late_parts = in_plane(shares)
    ff_totals = gather4(pair_sums(*ff_crossed), 1)
    strip = call(strip_kernel, (late_parts,), shapes(((STRIP, D + 128), bf16))[0], name="strip", after=ff_crossed[1:])
    strips = gather4(strip, 3)
    u = call(join_kernel, (at,) + ff_totals, shapes(((D, D), bf16))[0], name="join", after=strips[1:])
    before, after, far = spread(0, u, u, u)
    kept = place(at, 0, u, swap(u), ())
    mark = corner(kept[0])
    copies = call(copies_kernel, strips, shapes(((CHIPS, STRIP, D + 128), bf16))[0], name="copies",
                  after=(mark,))
    late = in_plane(copies)
    before, after, far = (tie(v, copies) for v in (before, after, far))
    kept = place(at, 3, before, swap(before), kept)
    kept = place(at, 1, after, swap(after), kept)
    g_down, g_up = place(at, 2, far, swap(far), kept)
    late = tie(late, corner(kept[0]))
    one = lambda n: ((n,), f32)
    outs = call(
        late_place_kernel, (at, late, swap(late)),
        shapes(((D, D), f32), ((D, D), f32), ((D, 128), f32), one(HD), *[one(128 * n) for _, n in VECTORS]), name="late_place",
    )
    g_query, g_out, g_kv, g_value, g_bdown, g_gain2, g_bias2, g_bout, g_bup, g_gain1, g_bias1, g_bq = outs
    shape = block_input.shape
    return (
        y.reshape(shape), gin.reshape(shape), g_gain1, g_bias1, g_query, g_bq, g_kv, g_value,
        g_out, g_bout, g_gain2, g_bias2, g_up, g_bup, g_down, g_bdown,
    )


def solution(mesh):
    split = P("x", None, ("y", "z", "c"), None)
    return jax.shard_map(
        body,
        mesh=Mesh(mesh.devices.reshape(4, 4, 4, 2), AXES),
        in_specs=(split, P("x", None), P("x", None, None)) + (P(),) * 14 + (split,),
        out_specs=(split, split) + (P(),) * 14,
        check_vma=False,
    )
```
